128 devices in a mesh: pp: 2 (over core), fsdp: 16 (over y, x), tp: 4 (over z).
Axes of the slice: x: 4, y: 4, z: 4, core: 2. Of those that a mesh axis runs over, the one named last changes fastest.
Arguments:
- inputs: bfloat16 [2, 512, 8192], P(None, 'tp', 'fsdp'), may hold values from -12 to 12
- head_grad: bfloat16 [2, 512, 8192], P(None, 'tp', 'fsdp'), may hold values from -0.3 to 0.3
- noise_mask: int32 [2, 512], P(None, 'tp'), may hold values 0 or 1
- lengths: int32 [2, 16, 2], replicated, may hold values from 1 to 24, 32 in all within a row
- rewards: int32 [2, 16, 2], replicated, may hold values from 0 to 3
- groups: int32 [2, 16, 2], replicated, may hold values from 0 to 31, as said below
- query_weight: bfloat16 [2, 8192, 4096], P('pp', 'fsdp', 'tp'), may hold values from -0.0625 to 0.0625
- key_weight: bfloat16 [2, 8192, 1024], P('pp', 'fsdp', 'tp'), may hold values from -0.0625 to 0.0625
- value_weight: bfloat16 [2, 8192, 1024], P('pp', 'fsdp', 'tp'), may hold values from -1 to 1
- out_weight: bfloat16 [2, 4096, 8192], P('pp', 'tp', 'fsdp'), may hold values from -1 to 1
Outputs:
- query_weight_grad: float32 [2, 8192, 4096], P('pp', 'fsdp', 'tp')
- key_weight_grad: float32 [2, 8192, 1024], P('pp', 'fsdp', 'tp')
- value_weight_grad: float32 [2, 8192, 1024], P('pp', 'fsdp', 'tp')
- out_weight_grad: float32 [2, 4096, 8192], P('pp', 'tp', 'fsdp')
The draws below stay inside these ranges and needn't reach their ends.
Inputs may be any that keep to these rules, and one draw needn't show every extreme that they name: `groups`: every group value names exactly 2 completions.
All inputs are finite; a program needn't handle non-finite values. No bound on the sum of `noise_mask` on one device may be relied on, other than what follows from the above.
Results may differ from the reference program's by a relative error of at most 0.013.
Values may be sent and summed in bfloat16 or wider, within the bound.
A program may use at most 128 MiB of HBM per device.

```python
import math
import jax
import jax.numpy as jnp
import numpy as np
from jax import lax

MODEL_WIDTH = 8192
KEY_VALUE_HEADS = 8
HEAD_WIDTH = 128
QUERY_HEADS = 32
SLOT = 32
MICRO = 2
CPS = 2
REWARD_TOP = 4
MOST = 24
TOKENS_MB = 512
HQD = 4096
HKD = 1024
N_PP = 2
N_FSDP = 16


def draw_groups(key, part):
    completions = MICRO * N_FSDP * CPS
    shuffled = jax.random.permutation(jax.random.fold_in(key, 7), completions)
    return (shuffled % (2 * N_FSDP)).reshape(MICRO, N_FSDP, CPS).astype(jnp.int32)


def stream_parts(key):
    row_total = SLOT * N_FSDP
    mixing = 0.6
    common = jax.random.normal(jax.random.fold_in(key, 11), (MICRO, 1, MODEL_WIDTH), jnp.float32)
    own = jax.random.normal(jax.random.fold_in(key, 12), (MICRO, row_total, MODEL_WIDTH), jnp.float32)
    token_scale = jnp.exp(jax.random.uniform(jax.random.fold_in(key, 13), (MICRO, row_total, 1), jnp.float32, -1.0, 1.0))
    unit = mixing * common + jnp.sqrt(1.0 - mixing * mixing) * own
    return (unit, token_scale)


def draw_inputs(key, part):
    feature = jnp.arange(MODEL_WIDTH, dtype=jnp.float32) / (MODEL_WIDTH - 1)
    unit, token_scale = stream_parts(key)
    scale_feature = 0.2 * jnp.exp(feature * jnp.log(10.0))
    return jnp.clip(unit * scale_feature * token_scale, -12.0, 12.0).astype(jnp.bfloat16)


def draw_head_grad(key, part):
    unit, token_scale = stream_parts(key)
    aligned = 0.8
    noise = jax.random.normal(jax.random.fold_in(key, 14), unit.shape, jnp.float32)
    value_list = 0.05 * (aligned * unit + jnp.sqrt(1.0 - aligned * aligned) * noise)
    return jnp.clip(value_list, -0.3, 0.3).astype(jnp.bfloat16)


def value_parts(key):
    value_list = jax.random.normal(jax.random.fold_in(key, 21), (N_PP, MODEL_WIDTH, KEY_VALUE_HEADS * HEAD_WIDTH), jnp.float32)
    return jnp.clip(value_list, -5.0, 5.0) * MODEL_WIDTH ** (-0.5)


def draw_value_weight(key, part):
    return value_parts(key).astype(jnp.bfloat16)


def draw_out_weight(key, part):
    value_gathered = value_parts(key)
    flipped_order = jnp.transpose(value_gathered, (0, 2, 1)).reshape(N_PP, KEY_VALUE_HEADS, 1, HEAD_WIDTH, MODEL_WIDTH)
    copied_state = jnp.broadcast_to(flipped_order, (N_PP, KEY_VALUE_HEADS, QUERY_HEADS // KEY_VALUE_HEADS, HEAD_WIDTH, MODEL_WIDTH)).reshape(N_PP, QUERY_HEADS * HEAD_WIDTH, MODEL_WIDTH)
    noise = jnp.clip(jax.random.normal(jax.random.fold_in(key, 22), (N_PP, QUERY_HEADS * HEAD_WIDTH, MODEL_WIDTH), jnp.float32), -5.0, 5.0)
    value_list = 0.75 ** 0.5 * (MODEL_WIDTH / (QUERY_HEADS * HEAD_WIDTH)) ** 0.5 * copied_state + 0.5 * noise * (QUERY_HEADS * HEAD_WIDTH) ** (-0.5)
    return value_list.astype(jnp.bfloat16)


def plant(array, key, low, largest):
    dims = array.shape
    index_at = [jax.random.randint(jax.random.fold_in(key, axis), (), 0, dims[axis]) for axis in range(len(dims))]
    array = array.at[tuple(index_at)].set(low)
    longest = dims.index(max(dims))
    index_at[longest] = (index_at[longest] + 1) % dims[longest]
    return array.at[tuple(index_at)].set(largest)


def levels(rng, extent, pieces, least, top_value):
    def one(axis_at, parts):
        draws = jax.random.uniform(jax.random.fold_in(jax.random.fold_in(rng, 6), axis_at), (parts,), jnp.float32, least / len(pieces), top_value / len(pieces))
        return jnp.repeat(jnp.exp(draws), extent[axis_at] // parts).reshape((-1,) + (1,) * (len(extent) - axis_at - 1))

    gain = one(*pieces[0])
    for cut in pieces[1:]:
        gain = gain * one(*cut)
    return gain


def length_profile(amount, total, most, skew):
    portions = [(1 << 20) // math.isqrt(standing ** skew) + 1 for standing in range(2, amount + 1)]
    rest, given = total - most - (amount - 1), [1] * (amount - 1)
    while rest > 0:
        movable = [i for i in range(amount - 1) if given[i] < most]
        whole, left = sum([portions[i] for i in movable]), rest
        for i in movable:
            addition = min(most - given[i], max(1, left * portions[i] // whole), rest)
            given[i] = given[i] + addition
            rest = rest - addition
    return np.array([most] + given)


def uneven_parts(stream_key, count, total, bound, slope):
    if count == 2:
        one = jax.random.randint(stream_key, (), max(1, total - bound), min(bound, total - 1) + 1)
        return jnp.stack([one, total - one])
    sizes = jnp.asarray(length_profile(count, total, bound, slope), jnp.int32)
    twos = (count - 1) // 2
    donor, receiver = sizes[1:1 + 2 * twos:2], sizes[2:2 + 2 * twos:2]
    margin = jnp.minimum(donor - 1, bound - receiver)
    passed = jax.random.randint(jax.random.fold_in(stream_key, 1), (twos,), 0, 1 << 20) % (margin + 1)
    sizes = sizes.at[1:1 + 2 * twos:2].set(donor - passed).at[2:2 + 2 * twos:2].set(receiver + passed)
    return sizes[jax.random.permutation(jax.random.fold_in(stream_key, 2), count)]


def gaussian(own_key, dims, spread, limit, pieces=(), held_as=jnp.bfloat16):
    drawn = jax.random.normal(own_key, dims, jnp.float32) * spread
    if len(pieces) > 0:
        drawn = levels(own_key, dims, pieces, -0.22, 0.18) * drawn
    return jnp.clip(drawn, min=-limit, max=limit).astype(held_as)


def setup_inputs(seed: int = 0) -> dict:
    key_list = jax.random.split(jax.random.key(seed), 11)
    inputs = draw_inputs(jax.random.fold_in(key_list[10], 71), 0)
    head_grad = draw_head_grad(jax.random.fold_in(key_list[10], 71), 0)
    noise_mask = plant((jax.random.randint(key_list[2], (MICRO, TOKENS_MB), 0, 2) < 1).astype(jnp.int32), jax.random.fold_in(key_list[2], 1), 0, 1)
    lengths = jax.vmap(lambda own: uneven_parts(own, CPS, SLOT, MOST, 2))(jax.random.split(key_list[3], MICRO * N_FSDP)).reshape((MICRO, N_FSDP, CPS)).astype(jnp.int32)
    rewards = plant(jax.random.randint(key_list[4], (MICRO, N_FSDP, CPS), 0, REWARD_TOP), jax.random.fold_in(key_list[4], 1), 0, REWARD_TOP - 1).astype(jnp.int32)
    groups = draw_groups(jax.random.fold_in(key_list[10], 71), 0)
    query_weight = gaussian(key_list[6], (N_PP, MODEL_WIDTH, HQD), MODEL_WIDTH ** -0.5, 0.0625, ((0, 2), (1, 16), (2, 4)))
    key_weight = gaussian(key_list[7], (N_PP, MODEL_WIDTH, HKD), MODEL_WIDTH ** -0.5, 0.0625, ((0, 2), (1, 16), (2, 4)))
    value_weight = draw_value_weight(jax.random.fold_in(key_list[10], 71), 0)
    out_weight = draw_out_weight(jax.random.fold_in(key_list[10], 71), 0)
    return dict(inputs=inputs, head_grad=head_grad, noise_mask=noise_mask, lengths=lengths, rewards=rewards, groups=groups, query_weight=query_weight, key_weight=key_weight, value_weight=value_weight, out_weight=out_weight)


epsilon = 1e-06
masked_score = -1e+30

def segments(lengths):
    segment_ends = jnp.cumsum(lengths, -1)
    position = jnp.arange(SLOT, dtype=jnp.int32)
    return lax.optimization_barrier(jnp.sum((segment_ends[..., None, :] <= position[:, None]).astype(jnp.int32), -1)).astype(jnp.int32)

def token_weights(lengths, rewards, groups):
    group_total = 2 * lengths.shape[1]
    reward_flat = rewards.reshape(-1).astype(jnp.float32)
    member = (groups.reshape(-1)[:, None] == jnp.arange(group_total, dtype=jnp.int32)[None, :]).astype(jnp.float32)
    member_count = lax.optimization_barrier(jnp.sum(member, 0))
    group_mean = lax.optimization_barrier(jnp.sum(member * reward_flat[:, None], 0)) / member_count
    centered = reward_flat - lax.optimization_barrier(jnp.sum(member * group_mean[None, :], 1))
    variance = lax.optimization_barrier(jnp.sum(member * (centered * centered)[:, None], 0)) / member_count
    spread_own = lax.optimization_barrier(jnp.sum(member * jnp.sqrt(variance)[None, :], 1))
    advantage = (centered / jnp.maximum(spread_own, 1.0)).reshape(lengths.shape)
    segment = segments(lengths)
    choose = (segment[..., None] == jnp.arange(lengths.shape[2], dtype=jnp.int32)).astype(jnp.float32)
    token_adv = lax.optimization_barrier(jnp.sum(choose * advantage[:, :, None, :], -1))
    token_len = lax.optimization_barrier(jnp.sum(choose * lengths[:, :, None, :].astype(jnp.float32), -1))
    return (token_adv * SLOT / token_len).reshape(lengths.shape[0], -1)

def split_heads(query_rows, key_rows, value_rows):
    batch_count, slot_len = (query_rows.shape[0], query_rows.shape[1])
    kv_heads = key_rows.shape[-1] // HEAD_WIDTH
    group_heads = query_rows.shape[-1] // HEAD_WIDTH // kv_heads
    query_heads = query_rows.reshape(batch_count, slot_len, kv_heads, group_heads, HEAD_WIDTH).astype(jnp.float32)
    key_heads = key_rows.reshape(batch_count, slot_len, kv_heads, HEAD_WIDTH).astype(jnp.float32)
    value_heads = value_rows.reshape(batch_count, slot_len, kv_heads, HEAD_WIDTH).astype(jnp.float32)
    return (query_heads, key_heads, value_heads)

def attend(query_rows, key_rows, value_rows, segment):
    query_heads, key_heads, value_heads = split_heads(query_rows, key_rows, value_rows)
    score_scale = HEAD_WIDTH ** (-0.5)
    scores = jnp.einsum('bikgd,bjkd->bkgij', query_heads, key_heads) * score_scale
    same_doc = segment[:, None, None, :, None] == segment[:, None, None, None, :]
    scores = jnp.where(same_doc, scores, masked_score)
    attn_probs = jax.nn.softmax(scores, axis=-1)
    rounded = lax.optimization_barrier(attn_probs.astype(jnp.bfloat16)).astype(jnp.float32)
    mixture = jnp.einsum('bkgij,bjkd->bikgd', rounded, value_heads)
    return (mixture.reshape(query_rows.shape).astype(jnp.bfloat16), attn_probs)

def attend_back(query_rows, key_rows, value_rows, attn_probs, head_out_grad):
    query_heads, key_heads, value_heads = split_heads(query_rows, key_rows, value_rows)
    score_scale = HEAD_WIDTH ** (-0.5)
    grad_heads = head_out_grad.reshape(query_heads.shape).astype(jnp.float32)
    rounded = lax.optimization_barrier(attn_probs.astype(jnp.bfloat16)).astype(jnp.float32)
    prob_grad = jnp.einsum('bikgd,bjkd->bkgij', grad_heads, value_heads)
    value_grad = jnp.einsum('bkgij,bikgd->bjkd', rounded, grad_heads)
    score_grad = attn_probs * (prob_grad - lax.optimization_barrier(jnp.sum(prob_grad * attn_probs, -1, keepdims=True)))
    score_grad = lax.optimization_barrier(score_grad.astype(jnp.bfloat16)).astype(jnp.float32)
    query_grad = jnp.einsum('bkgij,bjkd->bikgd', score_grad, key_heads) * score_scale
    key_grad = jnp.einsum('bkgij,bikgd->bjkd', score_grad, query_heads) * score_scale
    return (query_grad.reshape(query_rows.shape).astype(jnp.bfloat16), key_grad.reshape(key_rows.shape).astype(jnp.bfloat16), value_grad.reshape(value_rows.shape).astype(jnp.bfloat16))

def layer_forward(stream, query_layer, key_layer, value_layer, out_layer, segment):
    slot_total = segment.shape[0]
    stream_float = stream.astype(jnp.float32)
    inv_rms = lax.rsqrt(lax.optimization_barrier(jnp.mean(stream_float * stream_float, -1)) + epsilon)
    normed = (stream_float * inv_rms[:, None]).astype(jnp.bfloat16)
    query_rows = jnp.dot(normed, query_layer, preferred_element_type=jnp.float32).astype(jnp.bfloat16)
    key_rows = jnp.dot(normed, key_layer, preferred_element_type=jnp.float32).astype(jnp.bfloat16)
    value_rows = jnp.dot(normed, value_layer, preferred_element_type=jnp.float32).astype(jnp.bfloat16)
    head_out, attn_probs = attend(query_rows.reshape(slot_total, SLOT, -1), key_rows.reshape(slot_total, SLOT, -1), value_rows.reshape(slot_total, SLOT, -1), segment)
    head_out = head_out.reshape(stream.shape[0], -1)
    summed = jnp.dot(head_out, out_layer, preferred_element_type=jnp.float32)
    return ((stream_float + summed).astype(jnp.bfloat16), (inv_rms, normed, query_rows, key_rows, value_rows, attn_probs, head_out))

def layer_backward(out_grad, stream, kept_state, query_layer, key_layer, value_layer, out_layer):
    inv_rms, normed, query_rows, key_rows, value_rows, attn_probs, head_out = kept_state
    slot_total = stream.shape[0] // SLOT
    out_weight_grad = jnp.dot(head_out.T, out_grad, preferred_element_type=jnp.float32)
    head_out_grad = jnp.dot(out_grad, out_layer.T, preferred_element_type=jnp.float32).astype(jnp.bfloat16)
    query_grad, key_grad, value_grad = attend_back(query_rows.reshape(slot_total, SLOT, -1), key_rows.reshape(slot_total, SLOT, -1), value_rows.reshape(slot_total, SLOT, -1), attn_probs, head_out_grad.reshape(slot_total, SLOT, -1))
    query_grad = query_grad.reshape(stream.shape[0], -1)
    key_grad = key_grad.reshape(stream.shape[0], -1)
    value_grad = value_grad.reshape(stream.shape[0], -1)
    query_weight_grad = jnp.dot(normed.T, query_grad, preferred_element_type=jnp.float32)
    key_weight_grad = jnp.dot(normed.T, key_grad, preferred_element_type=jnp.float32)
    value_weight_grad = jnp.dot(normed.T, value_grad, preferred_element_type=jnp.float32)
    normed_grad = jnp.dot(query_grad, query_layer.T, preferred_element_type=jnp.float32) + jnp.dot(key_grad, key_layer.T, preferred_element_type=jnp.float32) + jnp.dot(value_grad, value_layer.T, preferred_element_type=jnp.float32)
    stream_float = stream.astype(jnp.float32)
    grad_dot = lax.optimization_barrier(jnp.sum(normed_grad * stream_float, -1))
    input_grad = (out_grad.astype(jnp.float32) + inv_rms[:, None] * normed_grad - stream_float * (inv_rms ** 3 * grad_dot / MODEL_WIDTH)[:, None]).astype(jnp.bfloat16)
    return (input_grad, (query_weight_grad, key_weight_grad, value_weight_grad, out_weight_grad))

def reference(inputs, head_grad, noise_mask, lengths, rewards, groups, query_weight, key_weight, value_weight, out_weight):
    segment_all = segments(lengths)
    weight_all = token_weights(lengths, rewards, groups) * noise_mask.astype(jnp.float32)
    totals = [jnp.zeros(query_weight.shape, jnp.float32), jnp.zeros(key_weight.shape, jnp.float32), jnp.zeros(value_weight.shape, jnp.float32), jnp.zeros(out_weight.shape, jnp.float32)]
    for micro_index in range(MICRO):
        stream = inputs[micro_index]
        history = []
        for layer_index in range(N_PP):
            following, kept_state = layer_forward(stream, query_weight[layer_index], key_weight[layer_index], value_weight[layer_index], out_weight[layer_index], segment_all[micro_index])
            history.append((stream, kept_state))
            stream = following
        out_grad = (-weight_all[micro_index][:, None] * head_grad[micro_index].astype(jnp.float32)).astype(jnp.bfloat16)
        for layer_index in range(N_PP - 1, -1, -1):
            stream, kept_state = history[layer_index]
            out_grad, terms = layer_backward(out_grad, stream, kept_state, query_weight[layer_index], key_weight[layer_index], value_weight[layer_index], out_weight[layer_index])
            for which in range(4):
                totals[which] = totals[which].at[layer_index].add(terms[which])
    return (totals[0], totals[1], totals[2], totals[3])
```

```python
import jax
import jax.numpy as jnp
from jax import lax
from jax.sharding import PartitionSpec as P

MODEL_WIDTH = 8192
HEAD_WIDTH = 128
SLOT = 32

epsilon = 1e-06
masked_score = -1e30


def segments(lengths):
    ends = jnp.stack([jnp.sum(lengths[..., : c + 1], -1) for c in range(lengths.shape[-1])], -1)
    position = jnp.arange(SLOT, dtype=jnp.int32)
    return jnp.sum((ends[..., None, :] <= position[:, None]).astype(jnp.int32), -1)


def token_weights(lengths, rewards, groups):
    group_total = 2 * lengths.shape[1]
    reward_flat = rewards.reshape(-1).astype(jnp.float32)
    member = (
        groups.reshape(-1)[:, None] == jnp.arange(group_total, dtype=jnp.int32)[None, :]
    ).astype(jnp.float32)
    member_count = jnp.sum(member, 0)
    group_mean = jnp.sum(member * reward_flat[:, None], 0) / member_count
    centered = reward_flat - jnp.sum(member * group_mean[None, :], 1)
    variance = jnp.sum(member * (centered * centered)[:, None], 0) / member_count
    spread_own = jnp.sum(member * jnp.sqrt(variance)[None, :], 1)
    advantage = (centered / jnp.maximum(spread_own, 1.0)).reshape(lengths.shape)
    segment = segments(lengths)
    choose = (segment[..., None] == jnp.arange(lengths.shape[2], dtype=jnp.int32)).astype(
        jnp.float32
    )
    token_adv = jnp.sum(choose * advantage[:, :, None, :], -1)
    token_len = jnp.sum(choose * lengths[:, :, None, :].astype(jnp.float32), -1)
    return (token_adv * SLOT / token_len).reshape(lengths.shape[0], -1)


def heads_of(rows):
    return rows.reshape(rows.shape[0], -1, HEAD_WIDTH).astype(jnp.float32)


def attend(query_rows, key_rows, value_rows, same_doc):
    keys, values = heads_of(key_rows), heads_of(value_rows)
    count = keys.shape[1]
    queries = heads_of(query_rows).reshape(SLOT, count, -1, HEAD_WIDTH)
    scores = jnp.einsum("ikgd,jkd->kgij", queries, keys) * HEAD_WIDTH**-0.5
    probs = jax.nn.softmax(jnp.where(same_doc, scores, masked_score), axis=-1)
    mixture = jnp.einsum(
        "kgij,jkd->ikgd", probs.astype(jnp.bfloat16).astype(jnp.float32), values
    )
    return mixture.reshape(SLOT, -1).astype(jnp.bfloat16), probs


def attend_back(query_rows, key_rows, value_rows, probs, head_out_grad):
    keys, values = heads_of(key_rows), heads_of(value_rows)
    count = keys.shape[1]
    queries = heads_of(query_rows).reshape(SLOT, count, -1, HEAD_WIDTH)
    grads = heads_of(head_out_grad).reshape(queries.shape)
    rounded = probs.astype(jnp.bfloat16).astype(jnp.float32)
    prob_grad = jnp.einsum("ikgd,jkd->kgij", grads, values)
    value_grad = jnp.einsum("kgij,ikgd->jkd", rounded, grads)
    score_grad = probs * (prob_grad - jnp.sum(prob_grad * probs, -1, keepdims=True))
    score_grad = score_grad.astype(jnp.bfloat16).astype(jnp.float32)
    scale = HEAD_WIDTH**-0.5
    query_grad = jnp.einsum("kgij,jkd->ikgd", score_grad, keys) * scale
    key_grad = jnp.einsum("kgij,ikgd->jkd", score_grad, queries) * scale
    return jnp.concatenate(
        [v.reshape(SLOT, -1).astype(jnp.bfloat16) for v in (query_grad, key_grad, value_grad)], 1
    )


def dot(a, b, contract):
    return lax.dot_general(a, b, (contract, ((), ())), preferred_element_type=jnp.float32)


def scatter(value, axis):
    return lax.psum_scatter(value, axis, scatter_dimension=0, tiled=True)


def gather(value, axis):
    return lax.all_gather(value, axis, axis=0, tiled=True)


def local(
    inputs,
    head_grad,
    noise_mask,
    lengths,
    rewards,
    groups,
    query_weight,
    key_weight,
    value_weight,
    out_weight,
):
    core = lax.axis_index("pp")
    row_count = inputs.shape[1]
    query_cols, key_cols = query_weight.shape[2], key_weight.shape[2]
    cols = query_cols + 2 * key_cols
    own_qkv = jnp.concatenate([query_weight[0], key_weight[0], value_weight[0]], 1)
    own_out = out_weight[0]
    swap = [(0, 1), (1, 0)]
    far_qkv, far_out = lax.ppermute(own_qkv, "pp", swap), lax.ppermute(own_out, "pp", swap)
    qkv = [jnp.where(core == 0, own_qkv, far_qkv), jnp.where(core == 0, far_qkv, own_qkv)]
    out = [jnp.where(core == 0, own_out, far_out), jnp.where(core == 0, far_out, own_out)]

    segment = segments(lengths)[core, lax.axis_index("fsdp")]
    same_doc = segment[:, None] == segment[None, :]
    weight = lax.dynamic_slice_in_dim(
        token_weights(lengths, rewards, groups)[core], lax.axis_index("tp") * row_count, row_count, 0
    ) * noise_mask[core].astype(jnp.float32)
    top_grad = (-weight[:, None] * head_grad[core].astype(jnp.float32)).astype(jnp.bfloat16)

    def project(stream_all, layer):
        wide = stream_all.astype(jnp.float32)
        squares = jnp.sum(wide * wide, -1, keepdims=True)
        partial = jnp.concatenate(
            [
                dot(stream_all, qkv[layer], ((1,), (0,))),
                jnp.broadcast_to(squares, (squares.shape[0], 128)),
            ],
            1,
        )
        summed = scatter(partial, "fsdp")
        inv_rms = lax.rsqrt(summed[:, cols : cols + 1] / MODEL_WIDTH + epsilon)
        rows = (summed[:, :cols] * inv_rms).astype(jnp.bfloat16)
        return (
            inv_rms,
            rows[:, :query_cols],
            rows[:, query_cols : query_cols + key_cols],
            rows[:, query_cols + key_cols :],
        )

    def head_grads(grad_all, layer):
        return scatter(dot(grad_all, out[layer], ((1,), (1,))), "fsdp").astype(jnp.bfloat16)

    stream0 = inputs[core]
    stream0_all = gather(stream0, "tp")
    grad1_all = gather(top_grad, "tp")
    inv0, q0, k0, v0 = project(stream0_all, 0)
    head_grad1 = head_grads(grad1_all, 1)
    head0, probs0 = attend(q0, k0, v0, same_doc)
    heads0_all = gather(head0, "fsdp")
    stream1 = (
        stream0.astype(jnp.float32) + scatter(dot(heads0_all, out[0], ((1,), (0,))), "tp")
    ).astype(jnp.bfloat16)
    stream1_all = gather(stream1, "tp")
    inv1, q1, k1, v1 = project(stream1_all, 1)
    head1, probs1 = attend(q1, k1, v1, same_doc)
    heads1_all = gather(head1, "fsdp")
    grads1 = attend_back(q1, k1, v1, probs1, head_grad1).astype(jnp.float32)
    rows1 = jnp.concatenate([q1, k1, v1], 1).astype(jnp.float32)
    share = inv1 * jnp.sum(grads1 * rows1, -1, keepdims=True) * inv1 / MODEL_WIDTH
    scaled1 = (grads1 * inv1).astype(jnp.bfloat16)
    scaled1_all = gather(scaled1, "fsdp")
    share_all = gather(jnp.broadcast_to(share, (SLOT, 128)), "fsdp")[:, :1]
    part = dot(scaled1_all, qkv[1], ((1,), (1,))) - stream1_all.astype(jnp.float32) * share_all
    grad0 = (top_grad.astype(jnp.float32) + scatter(part, "tp")).astype(jnp.bfloat16)
    grad0_all = gather(grad0, "tp")
    head_grad0 = head_grads(grad0_all, 0)
    grads0 = attend_back(q0, k0, v0, probs0, head_grad0).astype(jnp.float32)
    scaled0_all = gather((grads0 * inv0).astype(jnp.bfloat16), "fsdp")

    def both(first, second):
        own = jnp.where(core == 0, first, second)
        other = lax.ppermute(jnp.where(core == 0, second, first), "pp", swap)
        return jnp.concatenate([own, other], 0)

    streams = both(stream0_all, stream1_all)
    heads = both(heads0_all, heads1_all)
    out_grads = both(grad0_all, grad1_all)
    scaled = both(scaled0_all, scaled1_all)
    qkv_grad = dot(streams, scaled, ((0,), (0,)))
    return (
        qkv_grad[None, :, :query_cols],
        qkv_grad[None, :, query_cols : query_cols + key_cols],
        qkv_grad[None, :, query_cols + key_cols :],
        dot(heads, out_grads, ((0,), (0,)))[None],
    )


def solution(mesh):
    return jax.shard_map(
        local,
        mesh=mesh,
        in_specs=(
            P(None, "tp", "fsdp"),
            P(None, "tp", "fsdp"),
            P(None, "tp"),
            P(),
            P(),
            P(),
            P("pp", "fsdp", "tp"),
            P("pp", "fsdp", "tp"),
            P("pp", "fsdp", "tp"),
            P("pp", "tp", "fsdp"),
        ),
        out_specs=(
            P("pp", "fsdp", "tp"),
            P("pp", "fsdp", "tp"),
            P("pp", "fsdp", "tp"),
            P("pp", "tp", "fsdp"),
        ),
        check_vma=False,
    )
```

```python
import jax
import jax.numpy as jnp
from jax import lax
from jax.experimental import pallas as pl
from jax.experimental.pallas import tpu as pltpu
from jax.sharding import PartitionSpec as P

MODEL_WIDTH = 8192
HEAD_WIDTH = 128
SLOT = 32
LANES = 128

epsilon = 1e-06
masked_score = -1e30
MESH = pl.DeviceIdType.MESH
NN = ((1,), (0,))
NT = ((1,), (1,))
TN = ((0,), (0,))


def segments(lengths):
    ends = jnp.stack([jnp.sum(lengths[..., : c + 1], -1) for c in range(lengths.shape[-1])], -1)
    position = jnp.arange(SLOT, dtype=jnp.int32)
    return jnp.sum((ends[..., None, :] <= position[:, None]).astype(jnp.int32), -1)


def token_weights(lengths, rewards, groups):
    group_total = 2 * lengths.shape[1]
    reward_flat = rewards.reshape(-1).astype(jnp.float32)
    member = (
        groups.reshape(-1)[:, None] == jnp.arange(group_total, dtype=jnp.int32)[None, :]
    ).astype(jnp.float32)
    member_count = jnp.sum(member, 0)
    group_mean = jnp.sum(member * reward_flat[:, None], 0) / member_count
    centered = reward_flat - jnp.sum(member * group_mean[None, :], 1)
    variance = jnp.sum(member * (centered * centered)[:, None], 0) / member_count
    spread_own = jnp.sum(member * jnp.sqrt(variance)[None, :], 1)
    advantage = (centered / jnp.maximum(spread_own, 1.0)).reshape(lengths.shape)
    segment = segments(lengths)
    choose = (segment[..., None] == jnp.arange(lengths.shape[2], dtype=jnp.int32)).astype(
        jnp.float32
    )
    token_adv = jnp.sum(choose * advantage[:, :, None, :], -1)
    token_len = jnp.sum(choose * lengths[:, :, None, :].astype(jnp.float32), -1)
    return (token_adv * SLOT / token_len).reshape(lengths.shape[0], -1)


def dot(a, b, contract):
    return lax.dot_general(a, b, (contract, ((), ())), preferred_element_type=jnp.float32)


def split_tile(column):
    high = column.astype(jnp.bfloat16).astype(jnp.float32)
    lane = lax.broadcasted_iota(jnp.int32, (column.shape[0], LANES), 1)
    tile = jnp.where(lane == 0, high, jnp.where(lane == 1, column - high, 0.0))
    return tile.astype(jnp.bfloat16)


RS_QKV0, AG_HEAD0, RS_HEAD1, RS_QKV1, AG_GRAD1, AG_HEAD1, RS_HEAD0, AG_GRAD0 = range(8)
AG_STREAM0, AG_TOP, RS_OUT0, AG_STREAM1, RS_IN1, AG_OUT0 = range(6)


def kernel(
    x_in, g_in, doc, wq, wk, wv, wo,
    xs_out, hs_out, gs_out, dq_out, dk_out, dv_out,
    X, H, G, Q, WQKV, WO, S0, R0, S1, R1, T1, V1, T0, V0, D, E, DH, EH, OWN, ROWS, INV, PROBS,
    fs, fr, zs, zr, ss, sr, ls, lo,
):
    core, f, t = lax.axis_index("pp"), lax.axis_index("fsdp"), lax.axis_index("tp")
    y = f // 4
    far = 1 - core
    slots, shares = R0.shape[0], E.shape[0]
    rows = X.shape[1] // shares
    query_cols, key_cols = wq.shape[2], wk.shape[2]
    cols = query_cols + 2 * key_cols
    cuts = ((wq, 0, query_cols), (wk, query_cols, key_cols), (wv, query_cols + key_cols, key_cols))
    per_block = rows // SLOT

    def block(b):
        return pl.ds(pl.multiple_of(b * rows, rows), rows)

    def slot(s):
        return pl.ds(pl.multiple_of(s * SLOT, SLOT), SLOT)

    def remote(src, dst, send, recv, **at):
        return pltpu.make_async_remote_copy(
            src_ref=src, dst_ref=dst, send_sem=send, recv_sem=recv,
            device_id=at, device_id_type=MESH,
        )

    mine, own = slot(f), block(t)

    loads = [
        pltpu.make_async_copy(x_in.at[core], X.at[0, own], ls.at[0]),
        pltpu.make_async_copy(g_in, G.at[1, own], ls.at[1]),
        pltpu.make_async_copy(wo.at[0], WO.at[core], ls.at[2]),
    ] + [
        pltpu.make_async_copy(w.at[0], WQKV.at[core, :, pl.ds(at, width)], ls.at[3 + i])
        for i, (w, at, width) in enumerate(cuts)
    ]
    for c in loads:
        c.start()

    barrier = pltpu.get_barrier_semaphore()

    def greet_slot(k, _):
        pl.semaphore_signal(
            barrier, inc=1, device_id={"fsdp": lax.rem(f + k, slots)}, device_id_type=MESH
        )
        return 0

    lax.fori_loop(1, slots, greet_slot, 0)
    for k in range(1, shares):
        pl.semaphore_signal(
            barrier, inc=1, device_id={"tp": lax.rem(t + k, shares)}, device_id_type=MESH
        )
    pl.semaphore_signal(barrier, inc=1, device_id={"pp": far}, device_id_type=MESH)
    pl.semaphore_wait(barrier, slots + shares - 1)

    def z_gather(phase, buf):
        for k in (2, 1, 3):
            remote(buf.at[own], buf.at[own], zs.at[phase], zr.at[phase, t], tp=lax.rem(t + k, shares)).start()

    def z_gather_wait(phase, buf, b):
        remote(buf.at[block(b)], buf.at[block(b)], zs.at[phase], zr.at[phase, b], tp=t).wait_recv()

    def z_send(phase, send, recv, b):
        remote(send.at[block(b)], recv.at[t], zs.at[phase], zr.at[phase, t], tp=b).start()

    def z_sum(phase, recv, total):
        for k in (1, 3, 2):
            s = lax.rem(t + k, shares)
            remote(recv.at[s], recv.at[s], zs.at[phase], zr.at[phase, s], tp=t).wait_recv()
            total = total + recv[s].astype(jnp.float32)
        return total

    def f_gather(phase, buf):
        def one(k, _):
            remote(
                buf.at[mine], buf.at[mine], fs.at[phase], fr.at[phase, f], fsdp=lax.rem(f + k, slots)
            ).start()
            return 0

        lax.fori_loop(1, slots, one, 0)

    def f_gather_wait(phase, buf, b):
        for j in range(per_block):
            s = b * per_block + j

            @pl.when(s != f)
            def _():
                remote(
                    buf.at[slot(s)], buf.at[slot(s)], fs.at[phase], fr.at[phase, s], fsdp=f
                ).wait_recv()

    def f_send(phase, send, recv, b):
        for j in range(per_block):
            s = b * per_block + j

            @pl.when(s != f)
            def _():
                remote(send.at[slot(s)], recv.at[f], fs.at[phase], fr.at[phase, f], fsdp=s).start()

    def f_sum(phase, send, recv):
        def one(k, total):
            s = lax.rem(f + k, slots)
            remote(recv.at[s], recv.at[s], fs.at[phase], fr.at[phase, s], fsdp=f).wait_recv()
            return total + recv[s].astype(jnp.float32)

        return lax.fori_loop(1, slots, one, send[mine].astype(jnp.float32))

    def project(layer, phase, gathered, send, recv):
        def one(k, _):
            b = lax.rem(y + k, shares)

            @pl.when(b != t)
            def _():
                z_gather_wait(gathered, X.at[layer], b)

            part = X[layer, block(b)]
            send[block(b), pl.ds(0, cols)] = dot(part, WQKV[layer], NN).astype(jnp.bfloat16)
            wide = part.astype(jnp.float32)
            send[block(b), pl.ds(cols, LANES)] = split_tile(
                jnp.sum(wide * wide, -1, keepdims=True)
            )
            f_send(phase, send, recv, b)
            return 0

        lax.fori_loop(0, shares, one, 0)

    def finish_rows(layer, phase, send, recv):
        summed = f_sum(phase, send, recv)
        squares = summed[:, cols : cols + 1] + summed[:, cols + 1 : cols + 2]
        inv_rms = lax.rsqrt(squares / MODEL_WIDTH + epsilon)
        ROWS[layer] = (summed[:, :cols] * inv_rms).astype(jnp.bfloat16)
        INV[layer] = jnp.broadcast_to(inv_rms, (SLOT, LANES))

    kv_heads = key_cols // HEAD_WIDTH
    group = query_cols // key_cols
    scale = HEAD_WIDTH**-0.5

    def stacked(ref, g):
        return jnp.concatenate(
            [ref[:, (g * group + h) * HEAD_WIDTH : (g * group + h + 1) * HEAD_WIDTH] for h in range(group)], 0
        )

    def key_value(layer, g):
        at = query_cols + g * HEAD_WIDTH
        return (
            ROWS[layer, :, at : at + HEAD_WIDTH],
            ROWS[layer, :, at + key_cols : at + key_cols + HEAD_WIDTH],
        )

    def attend(layer):
        for g in range(kv_heads):
            keys, values = key_value(layer, g)
            scores = dot(stacked(ROWS.at[layer], g), keys, NT) * scale
            scores = jnp.where(doc[...] > 0.5, scores, masked_score)
            raised = jnp.exp(scores - jnp.max(scores, -1, keepdims=True))
            probs = raised / jnp.sum(raised, -1, keepdims=True)
            PROBS[layer, g] = probs
            mixed = dot(probs.astype(jnp.bfloat16), values, NN).astype(jnp.bfloat16)
            for h in range(group):
                H[layer, mine, pl.ds((g * group + h) * HEAD_WIDTH, HEAD_WIDTH)] = mixed[
                    h * SLOT : (h + 1) * SLOT
                ]

    def attend_back(layer, phase, send, recv):
        head_grad = f_sum(phase, send, recv).astype(jnp.bfloat16)
        inv_rms = INV[layer]
        total = jnp.zeros((SLOT, LANES), jnp.float32)

        def put(at, grad, rows_at):
            rounded = grad.astype(jnp.bfloat16).astype(jnp.float32)
            Q[layer, mine, pl.ds(at, HEAD_WIDTH)] = (rounded * inv_rms).astype(jnp.bfloat16)
            return rounded * rows_at.astype(jnp.float32)

        for g in range(kv_heads):
            keys, values = key_value(layer, g)
            queries = stacked(ROWS.at[layer], g)
            grads = stacked(head_grad, g)
            probs = PROBS[layer, g]
            prob_grad = dot(grads, values, NT)
            value_grad = dot(probs.astype(jnp.bfloat16), grads, TN)
            score_grad = probs * (prob_grad - jnp.sum(prob_grad * probs, -1, keepdims=True))
            score_grad = score_grad.astype(jnp.bfloat16)
            query_grad = dot(score_grad, keys, NN) * scale
            key_grad = dot(score_grad, queries, TN) * scale
            for h in range(group):
                part = slice(h * SLOT, (h + 1) * SLOT)
                total = total + put((g * group + h) * HEAD_WIDTH, query_grad[part], queries[part])
            total = total + put(query_cols + g * HEAD_WIDTH, key_grad, keys)
            total = total + put(query_cols + key_cols + g * HEAD_WIDTH, value_grad, values)
        share = inv_rms[:, :1] * inv_rms[:, :1] * jnp.sum(total, -1, keepdims=True) / MODEL_WIDTH
        Q[layer, mine, pl.ds(cols, LANES)] = split_tile(share)

    def head_grads(layer, phase, gathered, send, recv):
        def one(k, _):
            b = lax.rem(y + k, shares)

            @pl.when(b != t)
            def _():
                z_gather_wait(gathered, G.at[layer], b)

            send[block(b)] = dot(G[layer, block(b)], WO[layer], NT).astype(jnp.bfloat16)
            f_send(phase, send, recv, b)
            return 0

        lax.fori_loop(0, shares, one, 0)

    def to_shares(phase, send, recv, term):
        def one(i, _):
            b = lax.rem(t + 1 + lax.rem(i + 1, 3), shares)
            send[block(b)] = term(b).astype(jnp.bfloat16)
            z_send(phase, send, recv, b)
            return 0

        lax.fori_loop(0, shares - 1, one, 0)
        OWN[...] = term(t)

    def out_term(b):
        f_gather_wait(AG_HEAD0, H.at[0], b)
        return dot(H[0, block(b)], WO[0], NN)

    def in_term(b):
        f_gather_wait(AG_GRAD1, Q.at[1], b)
        tile = Q[1, block(b), pl.ds(cols, LANES)].astype(jnp.float32)
        share = tile[:, :1] + tile[:, 1:2]
        back = dot(Q[1, block(b), pl.ds(0, cols)], WQKV[1], NT)
        return back - X[1, block(b)].astype(jnp.float32) * share

    loads[0].wait()
    z_gather(AG_STREAM0, X.at[0])
    swaps = [
        remote(w.at[0], WQKV.at[core, :, pl.ds(at, width)], ss.at[i], sr.at[i], pp=far)
        for i, (w, at, width) in enumerate(cuts)
    ] + [remote(wo.at[0], WO.at[core], ss.at[3], sr.at[3], pp=far)]
    for c in swaps:
        c.start()
    for c in loads[1:]:
        c.wait()
    for c in swaps[:3]:
        c.wait_recv()
    project(0, RS_QKV0, AG_STREAM0, S0, R0)
    z_gather(AG_TOP, G.at[1])
    finish_rows(0, RS_QKV0, S0, R0)
    attend(0)
    f_gather(AG_HEAD0, H.at[0])
    swaps[3].wait_recv()
    to_shares(RS_OUT0, D, E, out_term)
    head_grads(1, RS_HEAD1, AG_TOP, T1, V1)
    stream = X[0, own].astype(jnp.float32) + z_sum(RS_OUT0, E, OWN[...])
    X[1, own] = stream.astype(jnp.bfloat16)
    z_gather(AG_STREAM1, X.at[1])
    project(1, RS_QKV1, AG_STREAM1, S1, R1)

    def hand_over(i, buf, out):
        pair = (
            pltpu.make_async_copy(buf.at[core], out.at[0], lo.at[i]),
            remote(buf.at[far], out.at[1], ss.at[4 + i], sr.at[4 + i], pp=far),
        )
        for c in pair:
            c.start()
        return pair

    pairs = [hand_over(0, X, xs_out)]
    finish_rows(1, RS_QKV1, S1, R1)
    attend(1)
    attend_back(1, RS_HEAD1, T1, V1)
    f_gather(AG_GRAD1, Q.at[1])
    f_gather(AG_HEAD1, H.at[1])
    to_shares(RS_IN1, DH, EH, in_term)
    grad = G[1, own].astype(jnp.float32) + z_sum(RS_IN1, EH, OWN[...])
    G[0, own] = grad.astype(jnp.bfloat16)
    z_gather(AG_OUT0, G.at[0])
    head_grads(0, RS_HEAD0, AG_OUT0, T0, V0)
    pairs.append(hand_over(1, G, gs_out))
    for b in range(shares):
        f_gather_wait(AG_HEAD1, H.at[1], b)
    pairs.append(hand_over(2, H, hs_out))
    attend_back(0, RS_HEAD0, T0, V0)
    f_gather(AG_GRAD0, Q.at[0])
    for b in range(shares):
        f_gather_wait(AG_GRAD0, Q.at[0], b)
    for i, (at, width, out) in enumerate(
        ((0, query_cols, dq_out), (query_cols, key_cols, dk_out), (query_cols + key_cols, key_cols, dv_out))
    ):
        part = Q.at[:, :, pl.ds(at, width)]
        pairs.append(hand_over(3 + i, part, out))

    others = pl.ds(0, (slots - 1) * SLOT)
    for phase, buf in (
        (RS_QKV0, S0), (AG_HEAD0, H.at[0]), (RS_HEAD1, T1), (RS_QKV1, S1),
        (AG_GRAD1, Q.at[1]), (AG_HEAD1, H.at[1]), (RS_HEAD0, T0), (AG_GRAD0, Q.at[0]),
    ):
        remote(buf.at[others], buf.at[others], fs.at[phase], fr.at[phase, 0], fsdp=f).wait_send()
    others = pl.ds(0, (shares - 1) * rows)
    for phase, buf in (
        (AG_STREAM0, X.at[0]), (AG_TOP, G.at[1]), (RS_OUT0, D),
        (AG_STREAM1, X.at[1]), (RS_IN1, DH), (AG_OUT0, G.at[0]),
    ):
        remote(buf.at[others], buf.at[others], zs.at[phase], zr.at[phase, 0], tp=t).wait_send()
    for c in swaps:
        c.wait_send()
    for here, there in pairs:
        here.wait()
        there.wait()


def local(
    inputs,
    head_grad,
    noise_mask,
    lengths,
    rewards,
    groups,
    query_weight,
    key_weight,
    value_weight,
    out_weight,
):
    core = lax.axis_index("pp")
    row_count, width = inputs.shape[1:]
    slots, shares = lax.axis_size("fsdp"), lax.axis_size("tp")
    tokens = row_count * shares
    query_cols, key_cols = query_weight.shape[2], key_weight.shape[2]
    wide = query_cols + 2 * key_cols + LANES
    kv_heads, group = key_cols // HEAD_WIDTH, query_cols // key_cols

    segment = segments(lengths)[core, lax.axis_index("fsdp")]
    same_doc = jnp.tile((segment[:, None] == segment[None, :]).astype(jnp.float32), (group, 1))
    weight = lax.dynamic_slice_in_dim(
        token_weights(lengths, rewards, groups)[core], lax.axis_index("tp") * row_count, row_count, 0
    ) * noise_mask[core].astype(jnp.float32)
    top_grad = (-weight[:, None] * head_grad[core].astype(jnp.float32)).astype(jnp.bfloat16)

    bf16, f32 = jnp.bfloat16, jnp.float32
    any_space = pl.BlockSpec(memory_space=pl.ANY)
    streams, heads, out_grads, query_grads, key_grads, value_grads = pl.pallas_call(
        kernel,
        out_shape=[
            jax.ShapeDtypeStruct((2, tokens, n), bf16)
            for n in (width, query_cols, width, query_cols, key_cols, key_cols)
        ],
        in_specs=[any_space, any_space, pl.BlockSpec(memory_space=pltpu.VMEM)] + [any_space] * 4,
        out_specs=[any_space] * 6,
        scratch_shapes=[
            pltpu.VMEM((2, tokens, width), bf16),
            pltpu.VMEM((2, tokens, query_cols), bf16),
            pltpu.VMEM((2, tokens, width), bf16),
            pltpu.VMEM((2, tokens, wide), bf16),
            pltpu.VMEM((2, width, wide - LANES), bf16),
            pltpu.VMEM((2, query_cols, width), bf16),
            pltpu.VMEM((tokens, wide), bf16),
            pltpu.VMEM((slots, SLOT, wide), bf16),
            pltpu.VMEM((tokens, wide), bf16),
            pltpu.VMEM((slots, SLOT, wide), bf16),
            pltpu.VMEM((tokens, query_cols), bf16),
            pltpu.VMEM((slots, SLOT, query_cols), bf16),
            pltpu.VMEM((tokens, query_cols), bf16),
            pltpu.VMEM((slots, SLOT, query_cols), bf16),
            pltpu.VMEM((tokens, width), bf16),
            pltpu.VMEM((shares, row_count, width), bf16),
            pltpu.VMEM((tokens, width), bf16),
            pltpu.VMEM((shares, row_count, width), bf16),
            pltpu.VMEM((row_count, width), f32),
            pltpu.VMEM((2, SLOT, wide - LANES), bf16),
            pltpu.VMEM((2, SLOT, LANES), f32),
            pltpu.VMEM((2, kv_heads, group * SLOT, SLOT), f32),
            pltpu.SemaphoreType.DMA((8,)),
            pltpu.SemaphoreType.DMA((8, slots)),
            pltpu.SemaphoreType.DMA((6,)),
            pltpu.SemaphoreType.DMA((6, shares)),
            pltpu.SemaphoreType.DMA((10,)),
            pltpu.SemaphoreType.DMA((10,)),
            pltpu.SemaphoreType.DMA((6,)),
            pltpu.SemaphoreType.DMA((6,)),
        ],
        compiler_params=pltpu.CompilerParams(
            collective_id=0, has_side_effects=True, vmem_limit_bytes=56 * 1024 * 1024
        ),
    )(inputs, top_grad, same_doc, query_weight, key_weight, value_weight, out_weight)

    def weight_grad(a, b):
        return lax.dot_general(a, b, (((0, 1), (0, 1)), ((), ())), preferred_element_type=f32)[None]

    return (
        weight_grad(streams, query_grads),
        weight_grad(streams, key_grads),
        weight_grad(streams, value_grads),
        weight_grad(heads, out_grads),
    )


def solution(mesh):
    return jax.shard_map(
        local,
        mesh=mesh,
        in_specs=(
            P(None, "tp", "fsdp"),
            P(None, "tp", "fsdp"),
            P(None, "tp"),
            P(),
            P(),
            P(),
            P("pp", "fsdp", "tp"),
            P("pp", "fsdp", "tp"),
            P("pp", "fsdp", "tp"),
            P("pp", "tp", "fsdp"),
        ),
        out_specs=(
            P("pp", "fsdp", "tp"),
            P("pp", "fsdp", "tp"),
            P("pp", "fsdp", "tp"),
            P("pp", "tp", "fsdp"),
        ),
        check_vma=False,
    )
```

```python
import jax
import jax.numpy as jnp
from jax import lax
from jax.experimental import pallas as pl
from jax.experimental.pallas import tpu as pltpu
from jax.sharding import PartitionSpec as P

MODEL_WIDTH = 8192
HEAD_WIDTH = 128
SLOT = 32
LANES = 128

epsilon = 1e-06
masked_score = -1e30
MESH = pl.DeviceIdType.MESH
NN = ((1,), (0,))
NT = ((1,), (1,))
TN = ((0,), (0,))


def segments(lengths):
    ends = jnp.stack([jnp.sum(lengths[..., : c + 1], -1) for c in range(lengths.shape[-1])], -1)
    position = jnp.arange(SLOT, dtype=jnp.int32)
    return jnp.sum((ends[..., None, :] <= position[:, None]).astype(jnp.int32), -1)


def token_weights(lengths, rewards, groups):
    group_total = 2 * lengths.shape[1]
    reward_flat = rewards.reshape(-1).astype(jnp.float32)
    member = (
        groups.reshape(-1)[:, None] == jnp.arange(group_total, dtype=jnp.int32)[None, :]
    ).astype(jnp.float32)
    member_count = jnp.sum(member, 0)
    group_mean = jnp.sum(member * reward_flat[:, None], 0) / member_count
    centered = reward_flat - jnp.sum(member * group_mean[None, :], 1)
    variance = jnp.sum(member * (centered * centered)[:, None], 0) / member_count
    spread_own = jnp.sum(member * jnp.sqrt(variance)[None, :], 1)
    advantage = (centered / jnp.maximum(spread_own, 1.0)).reshape(lengths.shape)
    segment = segments(lengths)
    choose = (segment[..., None] == jnp.arange(lengths.shape[2], dtype=jnp.int32)).astype(
        jnp.float32
    )
    token_adv = jnp.sum(choose * advantage[:, :, None, :], -1)
    token_len = jnp.sum(choose * lengths[:, :, None, :].astype(jnp.float32), -1)
    return (token_adv * SLOT / token_len).reshape(lengths.shape[0], -1)


def dot(a, b, contract):
    return lax.dot_general(a, b, (contract, ((), ())), preferred_element_type=jnp.float32)


RS_QKV0, RS_QKV1, RS_HEAD1, RS_HEAD0, AG_HEAD0, AG_GRAD1, AG_HEAD1, AG_GRAD0 = range(8)
AG_STREAM0, AG_TOP, RS_OUT0, AG_STREAM1, RS_IN1, AG_OUT0 = range(6)
HALVES = (0, 1)
PEERS = (2, 1, 3)
SIDE = 4
SUB = 16


def split_tile(first, second):
    lane = lax.broadcasted_iota(jnp.int32, first.shape[:-1] + (LANES,), first.ndim - 1)
    tile = jnp.zeros(lane.shape, jnp.float32)
    for i, column in enumerate((first, second)):
        high = column.astype(jnp.bfloat16).astype(jnp.float32)
        tile = jnp.where(lane == 2 * i, high, jnp.where(lane == 2 * i + 1, column - high, tile))
    return tile.astype(jnp.bfloat16)


def join_tile(tile):
    tile = tile.astype(jnp.float32)
    return tile[..., 0:1] + tile[..., 1:2], tile[..., 2:3] + tile[..., 3:4]


def kernel(
    x_in, g_in, doc, wq, wk, wv, wo,
    xs_out, hs_out, gs_out, dq_out, dk_out, dv_out,
    X, H, G, Q, W, WO, D, E, DH, EH, ROWS, INV, PROBS, HG, *rest,
):
    scatter_bufs, (fs, fr, zs, zr, ss, sr, ls, lo) = rest[:28], rest[28:]
    rs_bufs = {
        phase: scatter_bufs[7 * i : 7 * i + 7]
        for i, phase in enumerate((RS_QKV0, RS_QKV1, RS_HEAD1, RS_HEAD0))
    }
    core, f, t = lax.axis_index("pp"), lax.axis_index("fsdp"), lax.axis_index("tp")
    far = 1 - core
    y, x = f // SIDE, f % SIDE
    j, g = x // 2, x % 2
    q_wide = wq.shape[2] // 2
    k_wide = wk.shape[2] // 2
    cols = q_wide + 2 * k_wide
    wide = cols + LANES
    group = q_wide // HEAD_WIDTH
    scale = HEAD_WIDTH**-0.5

    def span(which, stride, width, at=0):
        return pl.ds(pl.multiple_of(which * stride + at, LANES), width)

    def other(mine, k):
        return lax.rem(mine + k, SIDE)

    def remote(src, dst, send, recv, **at):
        return pltpu.make_async_remote_copy(
            src_ref=src, dst_ref=dst, send_sem=send, recv_sem=recv,
            device_id=at, device_id_type=MESH,
        )

    cuts = [
        (w, gg * width, gg, at, width)
        for gg in (0, 1)
        for w, at, width in ((wq, 0, q_wide), (wk, q_wide, k_wide), (wv, q_wide + k_wide, k_wide))
    ]
    loads = [pltpu.make_async_copy(x_in.at[core], X.at[0, :, t], ls.at[0])] + [
        pltpu.make_async_copy(
            w.at[0, :, pl.ds(at, width)], W.at[core, gg, :, pl.ds(to, width)], ls.at[1 + i]
        )
        for i, (w, at, gg, to, width) in enumerate(cuts)
    ]
    loads += [
        pltpu.make_async_copy(wo.at[0], WO.at[core], ls.at[7]),
        pltpu.make_async_copy(g_in, G.at[1, :, t], ls.at[8]),
    ]
    for c in loads:
        c.start()

    barrier = pltpu.get_barrier_semaphore()
    for k in (1, 2, 3):
        for at in (
            {"fsdp": y * SIDE + other(x, k)},
            {"fsdp": other(y, k) * SIDE + x},
            {"tp": other(t, k)},
        ):
            pl.semaphore_signal(barrier, inc=1, device_id=at, device_id_type=MESH)
    pl.semaphore_signal(barrier, inc=1, device_id={"pp": far}, device_id_type=MESH)
    pl.semaphore_wait(barrier, 10)

    def z_gather(phase, buf, h):
        for k in PEERS:
            remote(buf.at[h, t], buf.at[h, t], zs.at[phase, h], zr.at[phase, h], tp=other(t, k)).start()

    def z_scatter(phase, send, recv, h):
        for k in PEERS:
            b = other(t, k)
            remote(send.at[h, b], recv.at[h, t], zs.at[phase, h], zr.at[phase, h], tp=b).start()

    def z_all(phase, buf, h):
        three = buf.at[h, pl.ds(0, SIDE - 1)]
        return remote(three, three, zs.at[phase, h], zr.at[phase, h], tp=t)

    def z_sum(phase, send, recv, h, total):
        z_all(phase, recv, h).wait_recv()
        total = total + send[h, t].astype(jnp.float32)
        for k in PEERS:
            total = total + recv[h, other(t, k)].astype(jnp.float32)
        return total.astype(jnp.bfloat16)

    def push(phase, h, kind, src, dst, **at):
        remote(src, dst, fs.at[phase, h, kind], fr.at[phase, h, kind], **at).start()

    def f_all(phase, h, kind):
        S, RA, RB, UA, UB, VA, VB = rs_bufs[
            {AG_HEAD0: RS_HEAD0, AG_HEAD1: RS_HEAD0, AG_GRAD0: RS_QKV0, AG_GRAD1: RS_QKV0}.get(phase, phase)
        ]
        order = (RA, RB, VA, VB) if phase < AG_HEAD0 else (VA, VB, RA, RB)
        three = order[kind].at[h, pl.ds(0, SIDE - 1)]
        return remote(three, three, fs.at[phase, h, kind], fr.at[phase, h, kind], fsdp=f)

    def widths(buf_cols):
        return (wide, cols) if buf_cols == 2 * wide else (q_wide, q_wide)

    def rs_start(phase, h):
        S, RA, RB, UA, UB, VA, VB = rs_bufs[phase]
        ca, cb = widths(S.shape[-1])
        for k in PEERS:
            y2, x2 = other(y, k), other(x, k)
            push(phase, h, 0, S.at[h, y2, :, 0], RA.at[h, y], fsdp=y2 * SIDE + x)
            push(
                phase, h, 1, S.at[h, :, x2 // 2, 1, :, span(x2 % 2, ca, cb)], RB.at[h, x], fsdp=y * SIDE + x2
            )

    def rs_mid(phase, h):
        S, RA, RB, UA, UB, VA, VB = rs_bufs[phase]
        ca, cb = widths(S.shape[-1])
        f_all(phase, h, 0).wait_recv()
        total = S[h, y, :, 0].astype(jnp.float32)
        for k in PEERS:
            total = total + RA[h, other(y, k)].astype(jnp.float32)
        UA[h] = total.astype(jnp.bfloat16)
        for k in PEERS:
            x2 = other(x, k)
            push(
                phase, h, 2, UA.at[h, x2 // 2, :, span(x2 % 2, ca, ca)], VA.at[h, x], fsdp=y * SIDE + x2
            )
        f_all(phase, h, 1).wait_recv()
        total = S[h, :, j, 1, :, span(g, ca, cb)].astype(jnp.float32)
        for k in PEERS:
            total = total + RB[h, other(x, k)].astype(jnp.float32)
        UB[h] = total.astype(jnp.bfloat16)
        for k in PEERS:
            y2 = other(y, k)
            push(phase, h, 3, UB.at[h, y2], VB.at[h, y], fsdp=y2 * SIDE + x)

    def rs_end(phase, h):
        S, RA, RB, UA, UB, VA, VB = rs_bufs[phase]
        ca, cb = widths(S.shape[-1])
        f_all(phase, h, 2).wait_recv()
        first = UA[h, j, :, span(g, ca, ca)].astype(jnp.float32)
        for k in PEERS:
            first = first + VA[h, other(x, k)].astype(jnp.float32)
        f_all(phase, h, 3).wait_recv()
        second = UB[h, y].astype(jnp.float32)
        for k in PEERS:
            second = second + VB[h, other(y, k)].astype(jnp.float32)
        return first, second

    def ag_start(phase, buf, h):
        ca, cb = widths(buf.shape[-1])
        first = buf.at[h, y, j, 0, :, span(g, ca, ca)]
        second = buf.at[h, y, j, 1, :, span(g, ca, cb)]
        for k in PEERS:
            push(phase, h, 0, first, first, fsdp=y * SIDE + other(x, k))
            push(phase, h, 1, second, second, fsdp=other(y, k) * SIDE + x)

    def ag_mid(phase, buf, h):
        ca, cb = widths(buf.shape[-1])
        first = buf.at[h, y, :, 0]
        f_all(phase, h, 0).wait_recv()
        for k in PEERS:
            push(phase, h, 2, first, first, fsdp=other(y, k) * SIDE + x)
        second = buf.at[h, :, j, 1, :, span(g, ca, cb)]
        f_all(phase, h, 1).wait_recv()
        for k in PEERS:
            push(phase, h, 3, second, second, fsdp=y * SIDE + other(x, k))

    def ag_end(phase, h):
        f_all(phase, h, 2).wait_recv()
        f_all(phase, h, 3).wait_recv()

    def flat(value):
        return value.reshape(-1, value.shape[-1])

    def project(layer, gathered, phase, h):
        S = rs_bufs[phase][0]
        z_all(gathered, X.at[layer], h).wait_recv()
        rows = flat(X[layer, h])
        for gg in (0, 1):
            S[h, :, :, :, :, pl.ds(gg * wide, cols)] = (
                dot(rows, W[layer, gg], NN).astype(jnp.bfloat16).reshape(SIDE, 2, 2, SUB, cols)
            )
        squares = []
        for a in (0, 1):
            part = X[layer, h, :, :, a].astype(jnp.float32)
            squares.append(jnp.sum(part * part, -1, keepdims=True))
        tile = split_tile(*squares)
        for gg in (0, 1):
            S[h, :, :, 0, :, pl.ds(gg * wide + cols, LANES)] = tile
        rs_start(phase, h)

    def attend(layer, phase, h):
        first, second = rs_end(phase, h)
        squares = jnp.concatenate(join_tile(first[:, cols:]), 0)
        inv_rms = lax.rsqrt(squares / MODEL_WIDTH + epsilon)
        rows = (jnp.concatenate([first[:, :cols], second], 0) * inv_rms).astype(jnp.bfloat16)
        ROWS[layer, h] = rows
        INV[layer, h] = jnp.broadcast_to(inv_rms, (SLOT, LANES))
        queries = jnp.concatenate([rows[:, i * HEAD_WIDTH : (i + 1) * HEAD_WIDTH] for i in range(group)], 0)
        keys, values = rows[:, q_wide : q_wide + k_wide], rows[:, q_wide + k_wide :]
        scores = dot(queries, keys, NT) * scale
        scores = jnp.where(doc[h] > 0.5, scores, masked_score)
        raised = jnp.exp(scores - jnp.max(scores, -1, keepdims=True))
        probs = raised / jnp.sum(raised, -1, keepdims=True)
        PROBS[layer, h] = probs
        mixed = dot(probs.astype(jnp.bfloat16), values, NN).astype(jnp.bfloat16)
        for i in range(group):
            H[layer, h, y, j, :, :, span(g, q_wide, HEAD_WIDTH, i * HEAD_WIDTH)] = mixed[
                i * SLOT : (i + 1) * SLOT
            ].reshape(2, SUB, HEAD_WIDTH)

    def head_end(phase, h):
        first, second = rs_end(phase, h)
        HG[h] = jnp.concatenate([first, second], 0).astype(jnp.bfloat16)

    def attend_back(layer, h):
        rows, head_grad, inv_rms, probs = ROWS[layer, h], HG[h], INV[layer, h], PROBS[layer, h]

        def stacked(value):
            return jnp.concatenate(
                [value[:, i * HEAD_WIDTH : (i + 1) * HEAD_WIDTH] for i in range(group)], 0
            )

        queries, grads = stacked(rows), stacked(head_grad)
        keys, values = rows[:, q_wide : q_wide + k_wide], rows[:, q_wide + k_wide :]
        prob_grad = dot(grads, values, NT)
        value_grad = dot(probs.astype(jnp.bfloat16), grads, TN)
        score_grad = probs * (prob_grad - jnp.sum(prob_grad * probs, -1, keepdims=True))
        score_grad = score_grad.astype(jnp.bfloat16)
        query_grad = dot(score_grad, keys, NN) * scale
        key_grad = dot(score_grad, queries, TN) * scale
        total = jnp.zeros((SLOT, LANES), jnp.float32)
        parts = [query_grad[i * SLOT : (i + 1) * SLOT] for i in range(group)] + [key_grad, value_grad]
        for i, part in enumerate(parts):
            part = part.astype(jnp.bfloat16).astype(jnp.float32)
            total = total + part * rows[:, i * HEAD_WIDTH : (i + 1) * HEAD_WIDTH].astype(jnp.float32)
            Q[layer, h, y, j, :, :, span(g, wide, HEAD_WIDTH, i * HEAD_WIDTH)] = (
                (part * inv_rms).astype(jnp.bfloat16).reshape(2, SUB, HEAD_WIDTH)
            )
        share = inv_rms[:, :1] * inv_rms[:, :1] * jnp.sum(total, -1, keepdims=True) / MODEL_WIDTH
        Q[layer, h, y, j, 0, :, span(g, wide, LANES, cols)] = split_tile(share[:SUB], share[SUB:])

    def head_grads(layer, gathered, phase, h):
        S = rs_bufs[phase][0]
        z_all(gathered, G.at[layer], h).wait_recv()
        S[h] = dot(flat(G[layer, h]), WO[layer], NT).astype(jnp.bfloat16).reshape(S.shape[1:])
        rs_start(phase, h)

    def project_out(h):
        ag_end(AG_HEAD0, h)
        D[h] = dot(flat(H[0, h]), WO[0], NN).astype(jnp.bfloat16).reshape(D.shape[1:])
        z_scatter(RS_OUT0, D, E, h)

    def project_back(h):
        ag_end(AG_GRAD1, h)
        back = sum(
            dot(flat(Q[1, h, :, :, :, :, pl.ds(gg * wide, cols)]), W[1, gg], NT) for gg in (0, 1)
        ).reshape(DH.shape[1:])
        tiles = [
            Q[1, h, :, :, 0, :, pl.ds(gg * wide + cols, LANES)].astype(jnp.float32) for gg in (0, 1)
        ]
        shares = join_tile(tiles[0] + tiles[1])
        for a in (0, 1):
            term = back[:, :, a] - X[1, h, :, :, a].astype(jnp.float32) * shares[a]
            DH[h, :, :, a] = term.astype(jnp.bfloat16)
        z_scatter(RS_IN1, DH, EH, h)

    pairs = []

    def hand_over(src, dst):
        i = len(pairs)
        pair = (
            pltpu.make_async_copy(src(core), dst(0), lo.at[i]),
            remote(src(far), dst(1), ss.at[i], sr.at[i], pp=far),
        )
        for c in pair:
            c.start()
        pairs.append(pair)

    loads[0].wait()
    for h in HALVES:
        z_gather(AG_STREAM0, X.at[0], h)
    swaps = [
        remote(
            w.at[0, :, pl.ds(at, width)], W.at[core, gg, :, pl.ds(to, width)], ss.at[16 + i], sr.at[16 + i], pp=far
        )
        for i, (w, at, gg, to, width) in enumerate(cuts)
    ] + [remote(wo.at[0], WO.at[core], ss.at[22], sr.at[22], pp=far)]
    for c in swaps:
        c.start()
    for c in loads[1:]:
        c.wait()
    for c in swaps[:6]:
        c.wait_recv()
    for h in HALVES:
        project(0, AG_STREAM0, RS_QKV0, h)
    for h in HALVES:
        z_gather(AG_TOP, G.at[1], h)
    for h in HALVES:
        rs_mid(RS_QKV0, h)
    for h in HALVES:
        attend(0, RS_QKV0, h)
        ag_start(AG_HEAD0, H.at[0], h)
    for h in HALVES:
        ag_mid(AG_HEAD0, H.at[0], h)
    swaps[6].wait_recv()
    for h in HALVES:
        project_out(h)
    for h in HALVES:
        head_grads(1, AG_TOP, RS_HEAD1, h)
    for h in HALVES:
        X[1, h, t] = z_sum(RS_OUT0, D, E, h, X[0, h, t].astype(jnp.float32))
        z_gather(AG_STREAM1, X.at[1], h)
    for h in HALVES:
        rs_mid(RS_HEAD1, h)
    for h in HALVES:
        project(1, AG_STREAM1, RS_QKV1, h)
    hand_over(lambda m: X.at[m], lambda m: xs_out.at[m])
    for h in HALVES:
        head_end(RS_HEAD1, h)
    for h in HALVES:
        rs_mid(RS_QKV1, h)
    for h in HALVES:
        attend(1, RS_QKV1, h)
        attend_back(1, h)
        ag_start(AG_GRAD1, Q.at[1], h)
    for h in HALVES:
        ag_mid(AG_GRAD1, Q.at[1], h)
    for h in HALVES:
        project_back(h)
    for h in HALVES:
        ag_start(AG_HEAD1, H.at[1], h)
    for h in HALVES:
        G[0, h, t] = z_sum(RS_IN1, DH, EH, h, G[1, h, t].astype(jnp.float32))
        z_gather(AG_OUT0, G.at[0], h)
    for h in HALVES:
        ag_mid(AG_HEAD1, H.at[1], h)
    for h in HALVES:
        head_grads(0, AG_OUT0, RS_HEAD0, h)
    hand_over(lambda m: G.at[m], lambda m: gs_out.at[m])
    for h in HALVES:
        rs_mid(RS_HEAD0, h)
    for h in HALVES:
        ag_end(AG_HEAD1, h)
    hand_over(lambda m: H.at[m], lambda m: hs_out.at[m])
    for h in HALVES:
        head_end(RS_HEAD0, h)
        attend_back(0, h)
        ag_start(AG_GRAD0, Q.at[0], h)
    for h in HALVES:
        ag_mid(AG_GRAD0, Q.at[0], h)
    for h in HALVES:
        ag_end(AG_GRAD0, h)
        for at, width, out in ((0, q_wide, dq_out), (q_wide, k_wide, dk_out), (q_wide + k_wide, k_wide, dv_out)):
            for gg in (0, 1):
                hand_over(
                    lambda m: Q.at[m, h, :, :, :, :, pl.ds(gg * wide + at, width)],
                    lambda m: out.at[m, h, :, :, :, :, pl.ds(gg * width, width)],
                )

    for phase in range(8):
        for h in HALVES:
            for kind in range(4):
                f_all(phase, h, kind).wait_send()
    for phase, buf in (
        (AG_STREAM0, X.at[0]), (AG_TOP, G.at[1]), (RS_OUT0, E),
        (AG_STREAM1, X.at[1]), (RS_IN1, EH), (AG_OUT0, G.at[0]),
    ):
        for h in HALVES:
            z_all(phase, buf, h).wait_send()
    for c in swaps:
        c.wait_send()
    for here, there in pairs:
        here.wait()
        there.wait()


def local(
    inputs,
    head_grad,
    noise_mask,
    lengths,
    rewards,
    groups,
    query_weight,
    key_weight,
    value_weight,
    out_weight,
):
    core, f = lax.axis_index("pp"), lax.axis_index("fsdp")
    row_count, width = inputs.shape[1:]
    q_wide, k_wide = query_weight.shape[2] // 2, key_weight.shape[2] // 2
    cols = q_wide + 2 * k_wide
    wide = cols + LANES
    group = q_wide // k_wide
    y, x = f // SIDE, f % SIDE

    segment = lax.dynamic_slice_in_dim(segments(lengths)[core], y * SIDE, SIDE, 0)
    segment = segment.reshape(2, 2, SLOT)[:, x // 2]
    same_doc = (segment[:, :, None] == segment[:, None, :]).astype(jnp.float32)
    same_doc = jnp.tile(same_doc, (1, group, 1))
    weight = lax.dynamic_slice_in_dim(
        token_weights(lengths, rewards, groups)[core], lax.axis_index("tp") * row_count, row_count, 0
    ) * noise_mask[core].astype(jnp.float32)
    top_grad = (-weight[:, None] * head_grad[core].astype(jnp.float32)).astype(jnp.bfloat16)

    bf16, f32 = jnp.bfloat16, jnp.float32
    any_space = pl.BlockSpec(memory_space=pl.ANY)
    rows = (2, SIDE, 2, 2, SUB)

    def scatter_bufs(ca, cb):
        return [
            pltpu.VMEM(shape, bf16)
            for shape in (
                rows + (2 * ca,),
                (2, SIDE, 2, SUB, 2 * ca),
                (2, SIDE, SIDE, SUB, cb),
                (2, 2, SUB, 2 * ca),
                (2, SIDE, SUB, cb),
                (2, SIDE, SUB, ca),
                (2, SIDE, SUB, cb),
            )
        ]

    results = pl.pallas_call(
        kernel,
        out_shape=[
            jax.ShapeDtypeStruct((2,) + rows + (n,), bf16)
            for n in (width, 2 * q_wide, width, 2 * q_wide, 2 * k_wide, 2 * k_wide)
        ],
        in_specs=[any_space, any_space, pl.BlockSpec(memory_space=pltpu.VMEM)] + [any_space] * 4,
        out_specs=[any_space] * 6,
        scratch_shapes=[
            pltpu.VMEM((2,) + rows + (width,), bf16),
            pltpu.VMEM((2,) + rows + (2 * q_wide,), bf16),
            pltpu.VMEM((2,) + rows + (width,), bf16),
            pltpu.VMEM((2,) + rows + (2 * wide,), bf16),
            pltpu.VMEM((2, 2, width, cols), bf16),
            pltpu.VMEM((2, 2 * q_wide, width), bf16),
            pltpu.VMEM(rows + (width,), bf16),
            pltpu.VMEM(rows + (width,), bf16),
            pltpu.VMEM(rows + (width,), bf16),
            pltpu.VMEM(rows + (width,), bf16),
            pltpu.VMEM((2, 2, SLOT, cols), bf16),
            pltpu.VMEM((2, 2, SLOT, LANES), f32),
            pltpu.VMEM((2, 2, group * SLOT, SLOT), f32),
            pltpu.VMEM((2, SLOT, q_wide), bf16),
        ]
        + scatter_bufs(wide, cols) * 2
        + scatter_bufs(q_wide, q_wide) * 2
        + [
            pltpu.SemaphoreType.DMA((8, 2, 4)),
            pltpu.SemaphoreType.DMA((8, 2, 4)),
            pltpu.SemaphoreType.DMA((6, 2)),
            pltpu.SemaphoreType.DMA((6, 2)),
            pltpu.SemaphoreType.DMA((23,)),
            pltpu.SemaphoreType.DMA((23,)),
            pltpu.SemaphoreType.DMA((9,)),
            pltpu.SemaphoreType.DMA((15,)),
        ],
        compiler_params=pltpu.CompilerParams(
            collective_id=0, has_side_effects=True, vmem_limit_bytes=56 * 1024 * 1024
        ),
    )(
        inputs.reshape(2, 2, 2, 2, SUB, width),
        top_grad.reshape(2, 2, 2, SUB, width),
        same_doc,
        query_weight,
        key_weight,
        value_weight,
        out_weight,
    )
    streams, heads, out_grads, query_grads, key_grads, value_grads = (
        r.reshape(-1, r.shape[-1]) for r in results
    )

    def weight_grad(a, b):
        return dot(a, b, TN)[None]

    return (
        weight_grad(streams, query_grads),
        weight_grad(streams, key_grads),
        weight_grad(streams, value_grads),
        weight_grad(heads, out_grads),
    )


def solution(mesh):
    return jax.shard_map(
        local,
        mesh=mesh,
        in_specs=(
            P(None, "tp", "fsdp"),
            P(None, "tp", "fsdp"),
            P(None, "tp"),
            P(),
            P(),
            P(),
            P("pp", "fsdp", "tp"),
            P("pp", "fsdp", "tp"),
            P("pp", "fsdp", "tp"),
            P("pp", "tp", "fsdp"),
        ),
        out_specs=(
            P("pp", "fsdp", "tp"),
            P("pp", "fsdp", "tp"),
            P("pp", "fsdp", "tp"),
            P("pp", "tp", "fsdp"),
        ),
        check_vma=False,
    )
```

```python
import jax
import jax.numpy as jnp
from jax import lax
from jax.experimental import pallas as pl
from jax.experimental.pallas import tpu as pltpu
from jax.sharding import PartitionSpec as P

MODEL_WIDTH = 8192
HEAD_WIDTH = 128
SLOT = 32
LANES = 128

epsilon = 1e-06
masked_score = -1e30
MESH = pl.DeviceIdType.MESH
NN = ((1,), (0,))
NT = ((1,), (1,))
TN = ((0,), (0,))


def dot(a, b, contract):
    return lax.dot_general(a, b, (contract, ((), ())), preferred_element_type=jnp.float32)


RS_QKV0, RS_QKV1, RS_HEAD1, RS_HEAD0, AG_HEAD0, AG_GRAD1, AG_HEAD1, AG_GRAD0, AG_FAR0 = range(9)
AG_STREAM0, AG_TOP, RS_OUT0, AG_STREAM1, RS_IN1, AG_OUT0 = range(6)
HALVES = (0, 1)
PEERS = (2, 1, 3)
SIDE = 4
SUB = 16


def split_tile(first, second):
    lane = lax.broadcasted_iota(jnp.int32, first.shape[:-1] + (LANES,), first.ndim - 1)
    tile = jnp.zeros(lane.shape, jnp.float32)
    for i, column in enumerate((first, second)):
        high = column.astype(jnp.bfloat16).astype(jnp.float32)
        tile = jnp.where(lane == 2 * i, high, jnp.where(lane == 2 * i + 1, column - high, tile))
    return tile.astype(jnp.bfloat16)


def join_tile(tile):
    tile = tile.astype(jnp.float32)
    return tile[..., 0:1] + tile[..., 1:2], tile[..., 2:3] + tile[..., 3:4]


def token_weights(lengths, rewards, groups, noise, core, t):
    square = (LANES, LANES)
    micros, packed, slots = lengths.shape
    lane = lax.broadcasted_iota(jnp.int32, (1, LANES), 1)

    def row(ref):
        value = jnp.full((1, LANES), -1, jnp.int32)
        for m in range(micros):
            for s in range(slots):
                for c in range(packed):
                    value = jnp.where(lane == (m * slots + s) * packed + c, ref[m, c, s], value)
        return jnp.broadcast_to(value.astype(jnp.float32), square)

    group_row, reward_row, length_row = row(groups), row(rewards), row(lengths)
    member = (group_row == group_row.T).astype(jnp.float32)
    reward_column = reward_row.T
    count = jnp.sum(member, 0, keepdims=True)
    mean = jnp.sum(member * reward_column, 0, keepdims=True) / count
    centered = reward_column - mean
    variance = jnp.sum(member * centered * centered, 0, keepdims=True) / count
    advantage = (reward_row - mean) / jnp.maximum(jnp.sqrt(variance), 1.0)
    token = lax.broadcasted_iota(jnp.int32, square, 0)
    lanes = lax.broadcasted_iota(jnp.int32, square, 1)
    first = core * slots * packed + (t * (LANES // SLOT) + (token >> 5)) * packed
    length = jnp.sum(jnp.where(lanes == first, length_row, 0.0), -1, keepdims=True)
    position = (token & (SLOT - 1)).astype(jnp.float32)
    chosen = lanes == first + (position >= length).astype(jnp.int32)
    advantage = jnp.sum(jnp.where(chosen, advantage, 0.0), -1, keepdims=True)
    length = jnp.sum(jnp.where(chosen, length_row, 0.0), -1, keepdims=True)
    noise = jnp.broadcast_to(noise[pl.ds(core, 1), :].astype(jnp.float32), square).T
    return advantage * SLOT / length * noise[:, :1]


def kernel(
    x_in, g_in, noise, lengths, rewards, groups, wq, wk, wv, wo,
    dq_out, dk_out, dv_out, do_out,
    X, H, G, Q, FX, FH, FG, FQ, W, WO, DW, DWO, D, E, DH, EH, ROWS, INV, PROBS, HG, GIN, *rest,
):
    scatter_bufs, (fs, fr, zs, zr, ss, sr, ls, lo) = rest[:28], rest[28:]
    rs_bufs = {
        phase: scatter_bufs[7 * i : 7 * i + 7]
        for i, phase in enumerate((RS_QKV0, RS_QKV1, RS_HEAD1, RS_HEAD0))
    }
    core, f, t = lax.axis_index("pp"), lax.axis_index("fsdp"), lax.axis_index("tp")
    far = 1 - core
    y, x = f // SIDE, f % SIDE
    j, g = x // 2, x % 2
    q_wide = wq.shape[2] // 2
    k_wide = wk.shape[2] // 2
    cols = q_wide + 2 * k_wide
    wide = cols + LANES
    group = q_wide // HEAD_WIDTH
    scale = HEAD_WIDTH**-0.5

    def span(which, stride, width, at=0):
        return pl.ds(pl.multiple_of(which * stride + at, LANES), width)

    def other(mine, k):
        return lax.rem(mine + k, SIDE)

    def remote(src, dst, send, recv, **at):
        return pltpu.make_async_remote_copy(
            src_ref=src, dst_ref=dst, send_sem=send, recv_sem=recv,
            device_id=at, device_id_type=MESH,
        )

    cuts = [
        (w, gg * width, gg, at, width)
        for gg in (0, 1)
        for w, at, width in ((wq, 0, q_wide), (wk, q_wide, k_wide), (wv, q_wide + k_wide, k_wide))
    ]
    loads = [pltpu.make_async_copy(x_in.at[core], X.at[0, :, t], ls.at[0])] + [
        pltpu.make_async_copy(
            w.at[0, :, pl.ds(at, width)], W.at[core, gg, :, pl.ds(to, width)], ls.at[1 + i]
        )
        for i, (w, at, gg, to, width) in enumerate(cuts)
    ]
    loads += [
        pltpu.make_async_copy(wo.at[0], WO.at[core], ls.at[7]),
        pltpu.make_async_copy(g_in.at[core], GIN, ls.at[8]),
    ]
    for c in loads:
        c.start()

    barrier = pltpu.get_barrier_semaphore()
    for k in (1, 2, 3):
        for at in (
            {"fsdp": y * SIDE + other(x, k)},
            {"fsdp": other(y, k) * SIDE + x},
            {"pp": far, "fsdp": y * SIDE + other(x, k)},
            {"pp": far, "fsdp": other(y, k) * SIDE + x},
            {"tp": other(t, k)},
        ):
            pl.semaphore_signal(barrier, inc=1, device_id=at, device_id_type=MESH)
    pl.semaphore_signal(barrier, inc=1, device_id={"pp": far}, device_id_type=MESH)
    pl.semaphore_wait(barrier, 16)

    def z_gather(phase, buf, h):
        for k in PEERS:
            remote(buf.at[h, t], buf.at[h, t], zs.at[phase, h], zr.at[phase, h], tp=other(t, k)).start()

    def z_scatter(phase, send, recv, h):
        for k in PEERS:
            b = other(t, k)
            remote(send.at[h, b], recv.at[h, t], zs.at[phase, h], zr.at[phase, h], tp=b).start()

    def z_all(phase, buf, h):
        three = buf.at[h, pl.ds(0, SIDE - 1)]
        return remote(three, three, zs.at[phase, h], zr.at[phase, h], tp=t)

    def z_sum(phase, send, recv, h, total):
        z_all(phase, recv, h).wait_recv()
        total = total + send[h, t].astype(jnp.float32)
        for k in PEERS:
            total = total + recv[h, other(t, k)].astype(jnp.float32)
        return total.astype(jnp.bfloat16)

    def push(phase, h, kind, src, dst, **at):
        remote(src, dst, fs.at[phase, h, kind], fr.at[phase, h, kind], **at).start()

    def f_all(phase, h, kind):
        S, RA, RB, UA, UB, VA, VB = rs_bufs[
            {AG_HEAD0: RS_HEAD0, AG_HEAD1: RS_HEAD0, AG_GRAD0: RS_QKV0, AG_GRAD1: RS_QKV0}.get(phase, phase)
        ]
        order = (RA, RB, VA, VB) if phase < AG_HEAD0 else (VA, VB, RA, RB)
        three = order[kind].at[h, pl.ds(0, SIDE - 1)]
        return remote(three, three, fs.at[phase, h, kind], fr.at[phase, h, kind], fsdp=f)

    def widths(buf_cols):
        return (wide, cols) if buf_cols == 2 * wide else (q_wide, q_wide)

    def rs_start(phase, h):
        S, RA, RB, UA, UB, VA, VB = rs_bufs[phase]
        ca, cb = widths(S.shape[-1])
        for k in PEERS:
            y2, x2 = other(y, k), other(x, k)
            push(phase, h, 0, S.at[h, y2, :, 0], RA.at[h, y], fsdp=y2 * SIDE + x)
            push(
                phase, h, 1, S.at[h, :, x2 // 2, 1, :, span(x2 % 2, ca, cb)], RB.at[h, x], fsdp=y * SIDE + x2
            )

    def rs_mid(phase, h):
        S, RA, RB, UA, UB, VA, VB = rs_bufs[phase]
        ca, cb = widths(S.shape[-1])
        f_all(phase, h, 0).wait_recv()
        total = S[h, y, :, 0].astype(jnp.float32)
        for k in PEERS:
            total = total + RA[h, other(y, k)].astype(jnp.float32)
        UA[h] = total.astype(jnp.bfloat16)
        for k in PEERS:
            x2 = other(x, k)
            push(
                phase, h, 2, UA.at[h, x2 // 2, :, span(x2 % 2, ca, ca)], VA.at[h, x], fsdp=y * SIDE + x2
            )
        f_all(phase, h, 1).wait_recv()
        total = S[h, :, j, 1, :, span(g, ca, cb)].astype(jnp.float32)
        for k in PEERS:
            total = total + RB[h, other(x, k)].astype(jnp.float32)
        UB[h] = total.astype(jnp.bfloat16)
        for k in PEERS:
            y2 = other(y, k)
            push(phase, h, 3, UB.at[h, y2], VB.at[h, y], fsdp=y2 * SIDE + x)

    def rs_end(phase, h):
        S, RA, RB, UA, UB, VA, VB = rs_bufs[phase]
        ca, cb = widths(S.shape[-1])
        f_all(phase, h, 2).wait_recv()
        first = UA[h, j, :, span(g, ca, ca)].astype(jnp.float32)
        for k in PEERS:
            first = first + VA[h, other(x, k)].astype(jnp.float32)
        f_all(phase, h, 3).wait_recv()
        second = UB[h, y].astype(jnp.float32)
        for k in PEERS:
            second = second + VB[h, other(y, k)].astype(jnp.float32)
        return first, second

    def ag_start(phase, buf, h):
        ca, cb = widths(buf.shape[-1])
        first = buf.at[h, y, j, 0, :, span(g, ca, ca)]
        second = buf.at[h, y, j, 1, :, span(g, ca, cb)]
        for k in PEERS:
            push(phase, h, 0, first, first, fsdp=y * SIDE + other(x, k))
            push(phase, h, 1, second, second, fsdp=other(y, k) * SIDE + x)

    def ag_mid(phase, buf, h):
        ca, cb = widths(buf.shape[-1])
        first = buf.at[h, y, :, 0]
        f_all(phase, h, 0).wait_recv()
        for k in PEERS:
            push(phase, h, 2, first, first, fsdp=other(y, k) * SIDE + x)
        second = buf.at[h, :, j, 1, :, span(g, ca, cb)]
        f_all(phase, h, 1).wait_recv()
        for k in PEERS:
            push(phase, h, 3, second, second, fsdp=y * SIDE + other(x, k))

    def last_mid(h):
        first, second = Q.at[0, h, y, :, 0], Q.at[0, h, :, j, 1, :, span(g, wide, cols)]
        first_far, second_far = FQ.at[h, y, :, 0], FQ.at[h, :, j, 1, :, span(g, wide, cols)]
        f_all(AG_GRAD0, h, 0).wait_recv()

        @pl.when(core == 0)
        def _():
            for k in PEERS:
                push(AG_GRAD0, h, 2, first, first, fsdp=other(y, k) * SIDE + x)

        @pl.when(core == 1)
        def _():
            for k in PEERS + (0,):
                push(AG_FAR0, h, 2, first, first_far, pp=far, fsdp=other(y, k) * SIDE + x)

        f_all(AG_GRAD0, h, 1).wait_recv()

        @pl.when(core == 0)
        def _():
            for k in PEERS:
                push(AG_GRAD0, h, 3, second, second, fsdp=y * SIDE + other(x, k))

        @pl.when(core == 1)
        def _():
            for k in PEERS + (0,):
                push(AG_FAR0, h, 3, second, second_far, pp=far, fsdp=y * SIDE + other(x, k))

    def far_all(h, kind):
        four = rs_bufs[RS_QKV0][1 + (kind - 2)].at[h]
        return remote(four, four, fs.at[AG_FAR0, h, kind], fr.at[AG_FAR0, h, kind], fsdp=f)

    def ag_end(phase, h):
        f_all(phase, h, 2).wait_recv()
        f_all(phase, h, 3).wait_recv()

    def flat(value):
        return value.reshape(-1, value.shape[-1])

    def project(layer, gathered, phase, h):
        S = rs_bufs[phase][0]
        z_all(gathered, X.at[layer], h).wait_recv()
        rows = flat(X[layer, h])
        for gg in (0, 1):
            S[h, :, :, :, :, pl.ds(gg * wide, cols)] = (
                dot(rows, W[layer, gg], NN).astype(jnp.bfloat16).reshape(SIDE, 2, 2, SUB, cols)
            )
        squares = []
        for a in (0, 1):
            part = X[layer, h, :, :, a].astype(jnp.float32)
            squares.append(jnp.sum(part * part, -1, keepdims=True))
        tile = split_tile(*squares)
        for gg in (0, 1):
            S[h, :, :, 0, :, pl.ds(gg * wide + cols, LANES)] = tile
        rs_start(phase, h)

    def attend(layer, phase, h):
        first, second = rs_end(phase, h)
        squares = jnp.concatenate(join_tile(first[:, cols:]), 0)
        inv_rms = lax.rsqrt(squares / MODEL_WIDTH + epsilon)
        rows = (jnp.concatenate([first[:, :cols], second], 0) * inv_rms).astype(jnp.bfloat16)
        ROWS[layer, h] = rows
        INV[layer, h] = jnp.broadcast_to(inv_rms, (SLOT, LANES))
        queries = jnp.concatenate([rows[:, i * HEAD_WIDTH : (i + 1) * HEAD_WIDTH] for i in range(group)], 0)
        keys, values = rows[:, q_wide : q_wide + k_wide], rows[:, q_wide + k_wide :]
        scores = dot(queries, keys, NT) * scale
        cut = lengths[core, 0, y * SIDE + 2 * h + j]
        later = [
            ((lax.broadcasted_iota(jnp.int32, scores.shape, d) & (SLOT - 1)) >= cut).astype(jnp.int32)
            for d in (0, 1)
        ]
        scores = jnp.where(later[0] == later[1], scores, masked_score)
        raised = jnp.exp(scores - jnp.max(scores, -1, keepdims=True))
        probs = raised / jnp.sum(raised, -1, keepdims=True)
        PROBS[layer, h] = probs
        mixed = dot(probs.astype(jnp.bfloat16), values, NN).astype(jnp.bfloat16)
        for i in range(group):
            H[layer, h, y, j, :, :, span(g, q_wide, HEAD_WIDTH, i * HEAD_WIDTH)] = mixed[
                i * SLOT : (i + 1) * SLOT
            ].reshape(2, SUB, HEAD_WIDTH)

    def head_end(phase, h):
        first, second = rs_end(phase, h)
        HG[h] = jnp.concatenate([first, second], 0).astype(jnp.bfloat16)

    def attend_back(layer, h):
        rows, head_grad, inv_rms, probs = ROWS[layer, h], HG[h], INV[layer, h], PROBS[layer, h]

        def stacked(value):
            return jnp.concatenate(
                [value[:, i * HEAD_WIDTH : (i + 1) * HEAD_WIDTH] for i in range(group)], 0
            )

        queries, grads = stacked(rows), stacked(head_grad)
        keys, values = rows[:, q_wide : q_wide + k_wide], rows[:, q_wide + k_wide :]
        prob_grad = dot(grads, values, NT)
        value_grad = dot(probs.astype(jnp.bfloat16), grads, TN)
        score_grad = probs * (prob_grad - jnp.sum(prob_grad * probs, -1, keepdims=True))
        score_grad = score_grad.astype(jnp.bfloat16)
        query_grad = dot(score_grad, keys, NN) * scale
        key_grad = dot(score_grad, queries, TN) * scale
        total = jnp.zeros((SLOT, LANES), jnp.float32)
        parts = [query_grad[i * SLOT : (i + 1) * SLOT] for i in range(group)] + [key_grad, value_grad]
        for i, part in enumerate(parts):
            part = part.astype(jnp.bfloat16).astype(jnp.float32)
            total = total + part * rows[:, i * HEAD_WIDTH : (i + 1) * HEAD_WIDTH].astype(jnp.float32)
            Q[layer, h, y, j, :, :, span(g, wide, HEAD_WIDTH, i * HEAD_WIDTH)] = (
                (part * inv_rms).astype(jnp.bfloat16).reshape(2, SUB, HEAD_WIDTH)
            )
        share = inv_rms[:, :1] * inv_rms[:, :1] * jnp.sum(total, -1, keepdims=True) / MODEL_WIDTH
        Q[layer, h, y, j, 0, :, span(g, wide, LANES, cols)] = split_tile(share[:SUB], share[SUB:])

    def head_grads(layer, gathered, phase, h):
        S = rs_bufs[phase][0]
        z_all(gathered, G.at[layer], h).wait_recv()
        S[h] = dot(flat(G[layer, h]), WO[layer], NT).astype(jnp.bfloat16).reshape(S.shape[1:])
        rs_start(phase, h)

    def project_out(h):
        ag_end(AG_HEAD0, h)
        D[h] = dot(flat(H[0, h]), WO[0], NN).astype(jnp.bfloat16).reshape(D.shape[1:])
        z_scatter(RS_OUT0, D, E, h)

    def project_back(h):
        ag_end(AG_GRAD1, h)
        back = sum(
            dot(flat(Q[1, h, :, :, :, :, pl.ds(gg * wide, cols)]), W[1, gg], NT) for gg in (0, 1)
        ).reshape(DH.shape[1:])
        tiles = [
            Q[1, h, :, :, 0, :, pl.ds(gg * wide + cols, LANES)].astype(jnp.float32) for gg in (0, 1)
        ]
        shares = join_tile(tiles[0] + tiles[1])
        for a in (0, 1):
            term = back[:, :, a] - X[1, h, :, :, a].astype(jnp.float32) * shares[a]
            DH[h, :, :, a] = term.astype(jnp.bfloat16)
        z_scatter(RS_IN1, DH, EH, h)

    def hand_over(i, src, dst):
        return remote(src, dst, ss.at[i], sr.at[i], pp=far)

    x_far, h_far, g_far = hand_over(7, X.at[far], FX), hand_over(8, H.at[far], FH), hand_over(9, G.at[far], FG)
    q_far = hand_over(10, Q.at[1], FQ)
    stores = []

    def store(src, dst):
        c = pltpu.make_async_copy(src, dst, lo.at[len(stores)])
        c.start()
        stores.append(c)

    def weight_grads(h):
        rows, far_rows = flat(X[core, h]), flat(FX[h])
        for gg in (0, 1):
            at = pl.ds(gg * wide, cols)
            term = dot(rows, flat(Q[core, h, :, :, :, :, at]), TN) + dot(
                far_rows, flat(FQ[h, :, :, :, :, at]), TN
            )
            DW[gg] = term if h == 0 else DW[gg] + term
            if h == 1:
                for to, width, out in ((0, q_wide, dq_out), (q_wide, k_wide, dk_out), (q_wide + k_wide, k_wide, dv_out)):
                    store(DW.at[gg, :, pl.ds(to, width)], out.at[0, :, pl.ds(gg * width, width)])

    loads[0].wait()
    for h in HALVES:
        z_gather(AG_STREAM0, X.at[0], h)
    swaps = [
        remote(
            w.at[0, :, pl.ds(at, width)], W.at[core, gg, :, pl.ds(to, width)], ss.at[i], sr.at[i], pp=far
        )
        for i, (w, at, gg, to, width) in enumerate(cuts)
    ] + [remote(wo.at[0], WO.at[core], ss.at[6], sr.at[6], pp=far)]
    for c in swaps:
        c.start()
    loads[8].wait()
    top = token_weights(lengths, rewards, groups, noise, core, t)
    top = (-top * flat(GIN[...]).astype(jnp.float32)).astype(jnp.bfloat16)
    G[1, :, t] = top.reshape(GIN.shape)
    for c in loads[1:8]:
        c.wait()
    for c in swaps[:6]:
        c.wait_recv()
    for h in HALVES:
        project(0, AG_STREAM0, RS_QKV0, h)
    for h in HALVES:
        z_gather(AG_TOP, G.at[1], h)
    for h in HALVES:
        rs_mid(RS_QKV0, h)
    for h in HALVES:
        attend(0, RS_QKV0, h)
        ag_start(AG_HEAD0, H.at[0], h)
    for h in HALVES:
        ag_mid(AG_HEAD0, H.at[0], h)
    swaps[6].wait_recv()
    for h in HALVES:
        project_out(h)
    for h in HALVES:
        head_grads(1, AG_TOP, RS_HEAD1, h)
    for h in HALVES:
        X[1, h, t] = z_sum(RS_OUT0, D, E, h, X[0, h, t].astype(jnp.float32))
        z_gather(AG_STREAM1, X.at[1], h)
    for h in HALVES:
        rs_mid(RS_HEAD1, h)
    for h in HALVES:
        project(1, AG_STREAM1, RS_QKV1, h)
    x_far.start()
    for h in HALVES:
        head_end(RS_HEAD1, h)
    for h in HALVES:
        rs_mid(RS_QKV1, h)
    for h in HALVES:
        attend(1, RS_QKV1, h)
        attend_back(1, h)
        ag_start(AG_GRAD1, Q.at[1], h)
    for h in HALVES:
        ag_mid(AG_GRAD1, Q.at[1], h)
    for h in HALVES:
        project_back(h)

    @pl.when(core == 0)
    def _():
        q_far.start()

    for h in HALVES:
        ag_start(AG_HEAD1, H.at[1], h)
    for h in HALVES:
        G[0, h, t] = z_sum(RS_IN1, DH, EH, h, G[1, h, t].astype(jnp.float32))
        z_gather(AG_OUT0, G.at[0], h)
    for h in HALVES:
        ag_mid(AG_HEAD1, H.at[1], h)
    for h in HALVES:
        head_grads(0, AG_OUT0, RS_HEAD0, h)
    g_far.start()
    for h in HALVES:
        ag_end(AG_HEAD1, h)
    h_far.start()
    DWO[...] = dot(flat(H[core]), flat(G[core]), TN)
    for h in HALVES:
        rs_mid(RS_HEAD0, h)
    for h in HALVES:
        head_end(RS_HEAD0, h)
        attend_back(0, h)
        ag_start(AG_GRAD0, Q.at[0], h)
    for h in HALVES:
        last_mid(h)
    for c in (x_far, h_far, g_far):
        c.wait_recv()
    DWO[...] += dot(flat(FH[...]), flat(FG[...]), TN)
    store(DWO, do_out.at[0])
    for h in HALVES:

        @pl.when(core == 0)
        def _():
            ag_end(AG_GRAD0, h)
            far_all(h, 2).wait_recv()
            far_all(h, 3).wait_recv()

        if h == 0:

            @pl.when(core == 1)
            def _():
                q_far.wait_recv()

        weight_grads(h)

    for phase in range(AG_GRAD0):
        for h in HALVES:
            for kind in range(4):
                f_all(phase, h, kind).wait_send()
    for h in HALVES:
        for kind in (0, 1):
            f_all(AG_GRAD0, h, kind).wait_send()

        @pl.when(core == 0)
        def _():
            for kind in (2, 3):
                f_all(AG_GRAD0, h, kind).wait_send()

        @pl.when(core == 1)
        def _():
            for kind in (2, 3):
                far_all(h, kind).wait_send()

    for phase, buf in (
        (AG_STREAM0, X.at[0]), (AG_TOP, G.at[1]), (RS_OUT0, E),
        (AG_STREAM1, X.at[1]), (RS_IN1, EH), (AG_OUT0, G.at[0]),
    ):
        for h in HALVES:
            z_all(phase, buf, h).wait_send()
    for c in swaps + [x_far, h_far, g_far]:
        c.wait_send()

    @pl.when(core == 0)
    def _():
        q_far.wait_send()

    for c in stores:
        c.wait()


def local(
    inputs,
    head_grad,
    noise_mask,
    lengths,
    rewards,
    groups,
    query_weight,
    key_weight,
    value_weight,
    out_weight,
):
    row_count, width = inputs.shape[1:]
    q_wide, k_wide = query_weight.shape[2] // 2, key_weight.shape[2] // 2
    cols = q_wide + 2 * k_wide
    wide = cols + LANES
    group = q_wide // k_wide

    bf16, f32 = jnp.bfloat16, jnp.float32
    any_space = pl.BlockSpec(memory_space=pl.ANY)
    rows = (2, SIDE, 2, 2, SUB)

    def scatter_bufs(ca, cb):
        return [
            pltpu.VMEM(shape, bf16)
            for shape in (
                rows + (2 * ca,),
                (2, SIDE, 2, SUB, 2 * ca),
                (2, SIDE, SIDE, SUB, cb),
                (2, 2, SUB, 2 * ca),
                (2, SIDE, SUB, cb),
                (2, SIDE, SUB, ca),
                (2, SIDE, SUB, cb),
            )
        ]

    return pl.pallas_call(
        kernel,
        out_shape=[
            jax.ShapeDtypeStruct(w.shape, f32)
            for w in (query_weight, key_weight, value_weight, out_weight)
        ],
        in_specs=[any_space, any_space, pl.BlockSpec(memory_space=pltpu.VMEM)]
        + [pl.BlockSpec(memory_space=pltpu.SMEM)] * 3
        + [any_space] * 4,
        out_specs=[any_space] * 4,
        scratch_shapes=[
            pltpu.VMEM((2,) + rows + (width,), bf16),
            pltpu.VMEM((2,) + rows + (2 * q_wide,), bf16),
            pltpu.VMEM((2,) + rows + (width,), bf16),
            pltpu.VMEM((2,) + rows + (2 * wide,), bf16),
            pltpu.VMEM(rows + (width,), bf16),
            pltpu.VMEM(rows + (2 * q_wide,), bf16),
            pltpu.VMEM(rows + (width,), bf16),
            pltpu.VMEM(rows + (2 * wide,), bf16),
            pltpu.VMEM((2, 2, width, cols), bf16),
            pltpu.VMEM((2, 2 * q_wide, width), bf16),
            pltpu.VMEM((2, width, cols), f32),
            pltpu.VMEM((2 * q_wide, width), f32),
            pltpu.VMEM(rows + (width,), bf16),
            pltpu.VMEM(rows + (width,), bf16),
            pltpu.VMEM(rows + (width,), bf16),
            pltpu.VMEM(rows + (width,), bf16),
            pltpu.VMEM((2, 2, SLOT, cols), bf16),
            pltpu.VMEM((2, 2, SLOT, LANES), f32),
            pltpu.VMEM((2, 2, group * SLOT, SLOT), f32),
            pltpu.VMEM((2, SLOT, q_wide), bf16),
            pltpu.VMEM((2, 2, 2, SUB, width), bf16),
        ]
        + scatter_bufs(wide, cols) * 2
        + scatter_bufs(q_wide, q_wide) * 2
        + [
            pltpu.SemaphoreType.DMA((9, 2, 4)),
            pltpu.SemaphoreType.DMA((9, 2, 4)),
            pltpu.SemaphoreType.DMA((6, 2)),
            pltpu.SemaphoreType.DMA((6, 2)),
            pltpu.SemaphoreType.DMA((11,)),
            pltpu.SemaphoreType.DMA((11,)),
            pltpu.SemaphoreType.DMA((9,)),
            pltpu.SemaphoreType.DMA((7,)),
        ],
        compiler_params=pltpu.CompilerParams(
            collective_id=0, has_side_effects=True, vmem_limit_bytes=56 * 1024 * 1024
        ),
    )(
        inputs.reshape(2, 2, 2, 2, SUB, width),
        head_grad.reshape(2, 2, 2, 2, SUB, width),
        noise_mask,
        *(jnp.swapaxes(v, 1, 2) for v in (lengths, rewards, groups)),
        query_weight,
        key_weight,
        value_weight,
        out_weight,
    )


def solution(mesh):
    return jax.shard_map(
        local,
        mesh=mesh,
        in_specs=(
            P(None, "tp", "fsdp"),
            P(None, "tp", "fsdp"),
            P(None, "tp"),
            P(),
            P(),
            P(),
            P("pp", "fsdp", "tp"),
            P("pp", "fsdp", "tp"),
            P("pp", "fsdp", "tp"),
            P("pp", "tp", "fsdp"),
        ),
        out_specs=(
            P("pp", "fsdp", "tp"),
            P("pp", "fsdp", "tp"),
            P("pp", "fsdp", "tp"),
            P("pp", "tp", "fsdp"),
        ),
        check_vma=False,
    )
```

```python
import jax
import jax.numpy as jnp
from jax import lax
from jax.experimental import pallas as pl
from jax.experimental.pallas import tpu as pltpu
from jax.sharding import PartitionSpec as P

MODEL_WIDTH = 8192
HEAD_WIDTH = 128
SLOT = 32
LANES = 128

epsilon = 1e-06
masked_score = -1e30
MESH = pl.DeviceIdType.MESH
NN = ((1,), (0,))
NT = ((1,), (1,))
TN = ((0,), (0,))


def dot(a, b, contract):
    return lax.dot_general(a, b, (contract, ((), ())), preferred_element_type=jnp.float32)


RS_QKV0, RS_QKV1, RS_HEAD1, RS_HEAD0, AG_HEAD0, AG_GRAD1, AG_HEAD1, AG_GRAD0, AG_FAR0 = range(9)
AG_STREAM0, AG_TOP, RS_OUT0, AG_STREAM1, RS_IN1, AG_OUT0 = range(6)
HALVES = (0, 1)
PEERS = (2, 1, 3)
SIDE = 4
SUB = 16


def split_tile(first, second):
    lane = lax.broadcasted_iota(jnp.int32, first.shape[:-1] + (LANES,), first.ndim - 1)
    tile = jnp.zeros(lane.shape, jnp.float32)
    for i, column in enumerate((first, second)):
        high = column.astype(jnp.bfloat16).astype(jnp.float32)
        tile = jnp.where(lane == 2 * i, high, jnp.where(lane == 2 * i + 1, column - high, tile))
    return tile.astype(jnp.bfloat16)


def join_tile(tile):
    tile = tile.astype(jnp.float32)
    return tile[..., 0:1] + tile[..., 1:2], tile[..., 2:3] + tile[..., 3:4]


def token_weights(lengths, rewards, groups, noise, core, t):
    square = (LANES, LANES)
    micros, packed, slots = lengths.shape
    lane = lax.broadcasted_iota(jnp.int32, (1, LANES), 1)

    def row(ref):
        value = jnp.full((1, LANES), -1, jnp.int32)
        for m in range(micros):
            for s in range(slots):
                for c in range(packed):
                    value = jnp.where(lane == (m * slots + s) * packed + c, ref[m, c, s], value)
        return jnp.broadcast_to(value.astype(jnp.float32), square)

    group_row, reward_row, length_row = row(groups), row(rewards), row(lengths)
    member = (group_row == group_row.T).astype(jnp.float32)
    reward_column = reward_row.T
    count = jnp.sum(member, 0, keepdims=True)
    mean = jnp.sum(member * reward_column, 0, keepdims=True) / count
    centered = reward_column - mean
    variance = jnp.sum(member * centered * centered, 0, keepdims=True) / count
    advantage = (reward_row - mean) / jnp.maximum(jnp.sqrt(variance), 1.0)
    token = lax.broadcasted_iota(jnp.int32, square, 0)
    lanes = lax.broadcasted_iota(jnp.int32, square, 1)
    first = core * slots * packed + (t * (LANES // SLOT) + (token >> 5)) * packed
    length = jnp.sum(jnp.where(lanes == first, length_row, 0.0), -1, keepdims=True)
    position = (token & (SLOT - 1)).astype(jnp.float32)
    chosen = lanes == first + (position >= length).astype(jnp.int32)
    advantage = jnp.sum(jnp.where(chosen, advantage, 0.0), -1, keepdims=True)
    length = jnp.sum(jnp.where(chosen, length_row, 0.0), -1, keepdims=True)
    noise = jnp.broadcast_to(noise[pl.ds(core, 1), :].astype(jnp.float32), square).T
    return advantage * SLOT / length * noise[:, :1]


def kernel(
    x_in, g_in, noise, lengths, rewards, groups, wq, wk, wv, wo,
    dq_out, dk_out, dv_out, do_out,
    X, H, G, Q, FX, FH, FG, FQ, W, WO, D, E, DH, EH, ROWS, INV, PROBS, HG, GIN, *rest,
):
    scatter_bufs, (fs, fr, zs, zr, ss, sr, ls) = rest[:28], rest[28:]
    rs_bufs = {
        phase: scatter_bufs[7 * i : 7 * i + 7]
        for i, phase in enumerate((RS_QKV0, RS_QKV1, RS_HEAD1, RS_HEAD0))
    }
    core, f, t = lax.axis_index("pp"), lax.axis_index("fsdp"), lax.axis_index("tp")
    far = 1 - core
    y, x = f >> 2, f & 3
    j, g = x >> 1, x & 1
    q_wide = wq.shape[2] // 2
    k_wide = wk.shape[2] // 2
    cols = q_wide + 2 * k_wide
    wide = cols + LANES
    group = q_wide // HEAD_WIDTH
    scale = HEAD_WIDTH**-0.5

    def span(which, stride, width, at=0):
        return pl.ds(pl.multiple_of(which * stride + at, LANES), width)

    def other(mine, k):
        return (mine + k) & (SIDE - 1)

    def remote(src, dst, send, recv, **at):
        return pltpu.make_async_remote_copy(
            src_ref=src, dst_ref=dst, send_sem=send, recv_sem=recv,
            device_id=at, device_id_type=MESH,
        )

    cuts = [
        (w, gg * width, gg, at, width)
        for gg in (0, 1)
        for w, at, width in ((wq, 0, q_wide), (wk, q_wide, k_wide), (wv, q_wide + k_wide, k_wide))
    ]
    loads = [pltpu.make_async_copy(x_in.at[core], X.at[0, :, t], ls.at[0])] + [
        pltpu.make_async_copy(
            w.at[0, :, pl.ds(at, width)], W.at[core, gg, :, pl.ds(to, width)], ls.at[1 + i]
        )
        for i, (w, at, gg, to, width) in enumerate(cuts)
    ]
    loads += [
        pltpu.make_async_copy(wo.at[0], WO.at[core], ls.at[7]),
        pltpu.make_async_copy(g_in.at[core], GIN, ls.at[8]),
    ]
    for c in loads:
        c.start()

    barrier = pltpu.get_barrier_semaphore()
    for k in (1, 2, 3):
        for at in (
            {"fsdp": y * SIDE + other(x, k)},
            {"fsdp": other(y, k) * SIDE + x},
            {"pp": far, "fsdp": y * SIDE + other(x, k)},
            {"pp": far, "fsdp": other(y, k) * SIDE + x},
            {"tp": other(t, k)},
        ):
            pl.semaphore_signal(barrier, inc=1, device_id=at, device_id_type=MESH)
    pl.semaphore_signal(barrier, inc=1, device_id={"pp": far}, device_id_type=MESH)
    pl.semaphore_wait(barrier, 16)

    def z_gather(phase, buf, h):
        for k in PEERS:
            remote(buf.at[h, t], buf.at[h, t], zs.at[phase, h], zr.at[phase, h], tp=other(t, k)).start()

    def z_scatter(phase, send, recv, h):
        for k in PEERS:
            b = other(t, k)
            remote(send.at[h, b], recv.at[h, t], zs.at[phase, h], zr.at[phase, h], tp=b).start()

    def z_all(phase, buf, h):
        three = buf.at[h, pl.ds(0, SIDE - 1)]
        return remote(three, three, zs.at[phase, h], zr.at[phase, h], tp=t)

    def z_sum(phase, send, recv, h, total):
        z_all(phase, recv, h).wait_recv()
        total = total + send[h, t].astype(jnp.float32)
        for k in PEERS:
            total = total + recv[h, other(t, k)].astype(jnp.float32)
        return total.astype(jnp.bfloat16)

    def push(phase, h, kind, src, dst, **at):
        remote(src, dst, fs.at[phase, h, kind], fr.at[phase, h, kind], **at).start()

    def f_all(phase, h, kind):
        S, RA, RB, UA, UB, VA, VB = rs_bufs[
            {AG_HEAD0: RS_HEAD0, AG_HEAD1: RS_HEAD0, AG_GRAD0: RS_QKV0, AG_GRAD1: RS_QKV0}.get(phase, phase)
        ]
        order = (RA, RB, VA, VB) if phase < AG_HEAD0 else (VA, VB, RA, RB)
        three = order[kind].at[h, pl.ds(0, SIDE - 1)]
        return remote(three, three, fs.at[phase, h, kind], fr.at[phase, h, kind], fsdp=f)

    def widths(buf_cols):
        return (wide, cols) if buf_cols == 2 * wide else (q_wide, q_wide)

    def rs_start(phase, h):
        S, RA, RB, UA, UB, VA, VB = rs_bufs[phase]
        ca, cb = widths(S.shape[-1])
        for k in PEERS:
            y2, x2 = other(y, k), other(x, k)
            push(phase, h, 0, S.at[h, y2, :, 0], RA.at[h, y], fsdp=y2 * SIDE + x)
            push(
                phase, h, 1, S.at[h, :, x2 >> 1, 1, :, span(x2 & 1, ca, cb)], RB.at[h, x], fsdp=y * SIDE + x2
            )

    def rs_mid(phase, h):
        S, RA, RB, UA, UB, VA, VB = rs_bufs[phase]
        ca, cb = widths(S.shape[-1])
        f_all(phase, h, 0).wait_recv()
        total = S[h, y, :, 0].astype(jnp.float32)
        for k in PEERS:
            total = total + RA[h, other(y, k)].astype(jnp.float32)
        UA[h] = total.astype(jnp.bfloat16)
        for k in PEERS:
            x2 = other(x, k)
            push(
                phase, h, 2, UA.at[h, x2 >> 1, :, span(x2 & 1, ca, ca)], VA.at[h, x], fsdp=y * SIDE + x2
            )
        f_all(phase, h, 1).wait_recv()
        total = S[h, :, j, 1, :, span(g, ca, cb)].astype(jnp.float32)
        for k in PEERS:
            total = total + RB[h, other(x, k)].astype(jnp.float32)
        UB[h] = total.astype(jnp.bfloat16)
        for k in PEERS:
            y2 = other(y, k)
            push(phase, h, 3, UB.at[h, y2], VB.at[h, y], fsdp=y2 * SIDE + x)

    def rs_end(phase, h):
        S, RA, RB, UA, UB, VA, VB = rs_bufs[phase]
        ca, cb = widths(S.shape[-1])
        f_all(phase, h, 2).wait_recv()
        first = UA[h, j, :, span(g, ca, ca)].astype(jnp.float32)
        for k in PEERS:
            first = first + VA[h, other(x, k)].astype(jnp.float32)
        f_all(phase, h, 3).wait_recv()
        second = UB[h, y].astype(jnp.float32)
        for k in PEERS:
            second = second + VB[h, other(y, k)].astype(jnp.float32)
        return first, second

    def ag_start(phase, buf, h):
        ca, cb = widths(buf.shape[-1])
        first = buf.at[h, y, j, 0, :, span(g, ca, ca)]
        second = buf.at[h, y, j, 1, :, span(g, ca, cb)]
        for k in PEERS:
            push(phase, h, 0, first, first, fsdp=y * SIDE + other(x, k))
            push(phase, h, 1, second, second, fsdp=other(y, k) * SIDE + x)

    def ag_mid(phase, buf, h):
        ca, cb = widths(buf.shape[-1])
        first = buf.at[h, y, :, 0]
        f_all(phase, h, 0).wait_recv()
        for k in PEERS:
            push(phase, h, 2, first, first, fsdp=other(y, k) * SIDE + x)
        second = buf.at[h, :, j, 1, :, span(g, ca, cb)]
        f_all(phase, h, 1).wait_recv()
        for k in PEERS:
            push(phase, h, 3, second, second, fsdp=y * SIDE + other(x, k))

    def last_mid(h):
        first, second = Q.at[0, h, y, :, 0], Q.at[0, h, :, j, 1, :, span(g, wide, cols)]
        first_far, second_far = FQ.at[h, y, :, 0], FQ.at[h, :, j, 1, :, span(g, wide, cols)]
        f_all(AG_GRAD0, h, 0).wait_recv()

        @pl.when(core == 0)
        def _():
            for k in PEERS:
                push(AG_GRAD0, h, 2, first, first, fsdp=other(y, k) * SIDE + x)

        @pl.when(core == 1)
        def _():
            for k in PEERS + (0,):
                push(AG_FAR0, h, 2, first, first_far, pp=far, fsdp=other(y, k) * SIDE + x)

        f_all(AG_GRAD0, h, 1).wait_recv()

        @pl.when(core == 0)
        def _():
            for k in PEERS:
                push(AG_GRAD0, h, 3, second, second, fsdp=y * SIDE + other(x, k))

        @pl.when(core == 1)
        def _():
            for k in PEERS + (0,):
                push(AG_FAR0, h, 3, second, second_far, pp=far, fsdp=y * SIDE + other(x, k))

    def far_all(h, kind):
        four = rs_bufs[RS_QKV0][1 + (kind - 2)].at[h]
        return remote(four, four, fs.at[AG_FAR0, h, kind], fr.at[AG_FAR0, h, kind], fsdp=f)

    def ag_end(phase, h):
        f_all(phase, h, 2).wait_recv()
        f_all(phase, h, 3).wait_recv()

    def flat(value):
        return value.reshape(-1, value.shape[-1])

    def project(layer, gathered, phase, h):
        S = rs_bufs[phase][0]
        z_all(gathered, X.at[layer], h).wait_recv()
        rows = flat(X[layer, h])
        for gg in (0, 1):
            S[h, :, :, :, :, pl.ds(gg * wide, cols)] = (
                dot(rows, W[layer, gg], NN).astype(jnp.bfloat16).reshape(SIDE, 2, 2, SUB, cols)
            )
        squares = []
        for a in (0, 1):
            part = X[layer, h, :, :, a].astype(jnp.float32)
            squares.append(jnp.sum(part * part, -1, keepdims=True))
        tile = split_tile(*squares)
        for gg in (0, 1):
            S[h, :, :, 0, :, pl.ds(gg * wide + cols, LANES)] = tile
        rs_start(phase, h)

    def attend(layer, phase, h):
        first, second = rs_end(phase, h)
        squares = jnp.concatenate(join_tile(first[:, cols:]), 0)
        inv_rms = lax.rsqrt(squares / MODEL_WIDTH + epsilon)
        rows = (jnp.concatenate([first[:, :cols], second], 0) * inv_rms).astype(jnp.bfloat16)
        ROWS[layer, h] = rows
        INV[layer, h] = jnp.broadcast_to(inv_rms, (SLOT, LANES))
        queries = jnp.concatenate([rows[:, i * HEAD_WIDTH : (i + 1) * HEAD_WIDTH] for i in range(group)], 0)
        keys, values = rows[:, q_wide : q_wide + k_wide], rows[:, q_wide + k_wide :]
        scores = dot(queries, keys, NT) * scale
        cut = lengths[core, 0, y * SIDE + 2 * h + j]
        later = [
            ((lax.broadcasted_iota(jnp.int32, scores.shape, d) & (SLOT - 1)) >= cut).astype(jnp.int32)
            for d in (0, 1)
        ]
        scores = jnp.where(later[0] == later[1], scores, masked_score)
        raised = jnp.exp(scores - jnp.max(scores, -1, keepdims=True))
        probs = raised / jnp.sum(raised, -1, keepdims=True)
        PROBS[layer, h] = probs
        mixed = dot(probs.astype(jnp.bfloat16), values, NN).astype(jnp.bfloat16)
        for i in range(group):
            H[layer, h, y, j, :, :, span(g, q_wide, HEAD_WIDTH, i * HEAD_WIDTH)] = mixed[
                i * SLOT : (i + 1) * SLOT
            ].reshape(2, SUB, HEAD_WIDTH)

    def head_end(phase, h):
        first, second = rs_end(phase, h)
        HG[h] = jnp.concatenate([first, second], 0).astype(jnp.bfloat16)

    def attend_back(layer, h):
        rows, head_grad, inv_rms, probs = ROWS[layer, h], HG[h], INV[layer, h], PROBS[layer, h]

        def stacked(value):
            return jnp.concatenate(
                [value[:, i * HEAD_WIDTH : (i + 1) * HEAD_WIDTH] for i in range(group)], 0
            )

        queries, grads = stacked(rows), stacked(head_grad)
        keys, values = rows[:, q_wide : q_wide + k_wide], rows[:, q_wide + k_wide :]
        prob_grad = dot(grads, values, NT)
        value_grad = dot(probs.astype(jnp.bfloat16), grads, TN)
        score_grad = probs * (prob_grad - jnp.sum(prob_grad * probs, -1, keepdims=True))
        score_grad = score_grad.astype(jnp.bfloat16)
        query_grad = dot(score_grad, keys, NN) * scale
        key_grad = dot(score_grad, queries, TN) * scale
        total = jnp.zeros((SLOT, LANES), jnp.float32)
        parts = [query_grad[i * SLOT : (i + 1) * SLOT] for i in range(group)] + [key_grad, value_grad]
        for i, part in enumerate(parts):
            part = part.astype(jnp.bfloat16).astype(jnp.float32)
            total = total + part * rows[:, i * HEAD_WIDTH : (i + 1) * HEAD_WIDTH].astype(jnp.float32)
            Q[layer, h, y, j, :, :, span(g, wide, HEAD_WIDTH, i * HEAD_WIDTH)] = (
                (part * inv_rms).astype(jnp.bfloat16).reshape(2, SUB, HEAD_WIDTH)
            )
        share = inv_rms[:, :1] * inv_rms[:, :1] * jnp.sum(total, -1, keepdims=True) / MODEL_WIDTH
        Q[layer, h, y, j, 0, :, span(g, wide, LANES, cols)] = split_tile(share[:SUB], share[SUB:])

    def head_grads(layer, gathered, phase, h):
        S = rs_bufs[phase][0]
        z_all(gathered, G.at[layer], h).wait_recv()
        S[h] = dot(flat(G[layer, h]), WO[layer], NT).astype(jnp.bfloat16).reshape(S.shape[1:])
        rs_start(phase, h)

    def project_out(h):
        ag_end(AG_HEAD0, h)
        D[h] = dot(flat(H[0, h]), WO[0], NN).astype(jnp.bfloat16).reshape(D.shape[1:])
        z_scatter(RS_OUT0, D, E, h)

    def project_back(h):
        ag_end(AG_GRAD1, h)
        back = sum(
            dot(flat(Q[1, h, :, :, :, :, pl.ds(gg * wide, cols)]), W[1, gg], NT) for gg in (0, 1)
        ).reshape(DH.shape[1:])
        tiles = [
            Q[1, h, :, :, 0, :, pl.ds(gg * wide + cols, LANES)].astype(jnp.float32) for gg in (0, 1)
        ]
        shares = join_tile(tiles[0] + tiles[1])
        for a in (0, 1):
            term = back[:, :, a] - X[1, h, :, :, a].astype(jnp.float32) * shares[a]
            DH[h, :, :, a] = term.astype(jnp.bfloat16)
        z_scatter(RS_IN1, DH, EH, h)

    def hand_over(i, src, dst):
        return remote(src, dst, ss.at[i], sr.at[i], pp=far)

    x_far, h_far, g_far = hand_over(7, X.at[far], FX), hand_over(8, H.at[far], FH), hand_over(9, G.at[far], FG)
    q_far = hand_over(10, Q.at[1], FQ)
    def weight_grads(h):
        rows, far_rows = flat(X[core, h]), flat(FX[h])
        for gg in (0, 1):
            at = pl.ds(gg * wide, cols)
            term = dot(rows, flat(Q[core, h, :, :, :, :, at]), TN) + dot(
                far_rows, flat(FQ[h, :, :, :, :, at]), TN
            )
            for to, width, out in (
                (0, q_wide, dq_out), (q_wide, k_wide, dk_out), (q_wide + k_wide, k_wide, dv_out)
            ):
                to_at = pl.ds(gg * width, width)
                part = term[:, to : to + width]
                out[0, :, to_at] = part if h == 0 else out[0, :, to_at] + part

    loads[0].wait()
    for h in HALVES:
        z_gather(AG_STREAM0, X.at[0], h)
    swaps = [
        remote(
            w.at[0, :, pl.ds(at, width)], W.at[core, gg, :, pl.ds(to, width)], ss.at[i], sr.at[i], pp=far
        )
        for i, (w, at, gg, to, width) in enumerate(cuts)
    ] + [remote(wo.at[0], WO.at[core], ss.at[6], sr.at[6], pp=far)]
    for c in swaps[:6]:
        c.start()
    for c in loads[1:8]:
        c.wait()
    for c in swaps[:6]:
        c.wait_recv()
    for h in HALVES:
        project(0, AG_STREAM0, RS_QKV0, h)
    swaps[6].start()
    loads[8].wait()
    top = token_weights(lengths, rewards, groups, noise, core, t)
    top = (-top * flat(GIN[...]).astype(jnp.float32)).astype(jnp.bfloat16)
    G[1, :, t] = top.reshape(GIN.shape)
    for h in HALVES:
        z_gather(AG_TOP, G.at[1], h)
    for h in HALVES:
        rs_mid(RS_QKV0, h)
    for h in HALVES:
        attend(0, RS_QKV0, h)
        ag_start(AG_HEAD0, H.at[0], h)
    for h in HALVES:
        ag_mid(AG_HEAD0, H.at[0], h)
    swaps[6].wait_recv()
    for h in HALVES:
        project_out(h)
    for h in HALVES:
        head_grads(1, AG_TOP, RS_HEAD1, h)
    for h in HALVES:
        X[1, h, t] = z_sum(RS_OUT0, D, E, h, X[0, h, t].astype(jnp.float32))
        z_gather(AG_STREAM1, X.at[1], h)
    for h in HALVES:
        rs_mid(RS_HEAD1, h)
    for h in HALVES:
        project(1, AG_STREAM1, RS_QKV1, h)
    x_far.start()
    for h in HALVES:
        head_end(RS_HEAD1, h)
    for h in HALVES:
        rs_mid(RS_QKV1, h)
    for h in HALVES:
        attend(1, RS_QKV1, h)
        attend_back(1, h)
        ag_start(AG_GRAD1, Q.at[1], h)
    for h in HALVES:
        ag_mid(AG_GRAD1, Q.at[1], h)
    for h in HALVES:
        project_back(h)

    @pl.when(core == 0)
    def _():
        q_far.start()

    for h in HALVES:
        ag_start(AG_HEAD1, H.at[1], h)
    for h in HALVES:
        G[0, h, t] = z_sum(RS_IN1, DH, EH, h, G[1, h, t].astype(jnp.float32))
        z_gather(AG_OUT0, G.at[0], h)
    for h in HALVES:
        ag_mid(AG_HEAD1, H.at[1], h)
    for h in HALVES:
        head_grads(0, AG_OUT0, RS_HEAD0, h)
    g_far.start()
    for h in HALVES:
        ag_end(AG_HEAD1, h)
    h_far.start()
    do_out[0] = dot(flat(H[core]), flat(G[core]), TN)
    for h in HALVES:
        rs_mid(RS_HEAD0, h)
    for h in HALVES:
        head_end(RS_HEAD0, h)
        attend_back(0, h)
        ag_start(AG_GRAD0, Q.at[0], h)
    for h in HALVES:
        last_mid(h)
    for c in (x_far, h_far, g_far):
        c.wait_recv()
    do_out[0] += dot(flat(FH[...]), flat(FG[...]), TN)
    for h in HALVES:

        @pl.when(core == 0)
        def _():
            ag_end(AG_GRAD0, h)
            far_all(h, 2).wait_recv()
            far_all(h, 3).wait_recv()

        if h == 0:

            @pl.when(core == 1)
            def _():
                q_far.wait_recv()

        weight_grads(h)

    for phase in range(AG_GRAD0):
        for h in HALVES:
            for kind in range(4):
                f_all(phase, h, kind).wait_send()
    for h in HALVES:
        for kind in (0, 1):
            f_all(AG_GRAD0, h, kind).wait_send()

        @pl.when(core == 0)
        def _():
            for kind in (2, 3):
                f_all(AG_GRAD0, h, kind).wait_send()

        @pl.when(core == 1)
        def _():
            for kind in (2, 3):
                far_all(h, kind).wait_send()

    for phase, buf in (
        (AG_STREAM0, X.at[0]), (AG_TOP, G.at[1]), (RS_OUT0, E),
        (AG_STREAM1, X.at[1]), (RS_IN1, EH), (AG_OUT0, G.at[0]),
    ):
        for h in HALVES:
            z_all(phase, buf, h).wait_send()
    for c in swaps + [x_far, h_far, g_far]:
        c.wait_send()

    @pl.when(core == 0)
    def _():
        q_far.wait_send()


def local(
    inputs,
    head_grad,
    noise_mask,
    lengths,
    rewards,
    groups,
    query_weight,
    key_weight,
    value_weight,
    out_weight,
):
    row_count, width = inputs.shape[1:]
    q_wide, k_wide = query_weight.shape[2] // 2, key_weight.shape[2] // 2
    cols = q_wide + 2 * k_wide
    wide = cols + LANES
    group = q_wide // k_wide

    bf16, f32 = jnp.bfloat16, jnp.float32
    any_space = pl.BlockSpec(memory_space=pl.ANY)
    rows = (2, SIDE, 2, 2, SUB)

    def scatter_bufs(ca, cb):
        return [
            pltpu.VMEM(shape, bf16)
            for shape in (
                rows + (2 * ca,),
                (2, SIDE, 2, SUB, 2 * ca),
                (2, SIDE, SIDE, SUB, cb),
                (2, 2, SUB, 2 * ca),
                (2, SIDE, SUB, cb),
                (2, SIDE, SUB, ca),
                (2, SIDE, SUB, cb),
            )
        ]

    return pl.pallas_call(
        kernel,
        out_shape=[
            pltpu.VMEM(w.shape, f32)
            for w in (query_weight, key_weight, value_weight, out_weight)
        ],
        in_specs=[any_space, any_space, pl.BlockSpec(memory_space=pltpu.VMEM)]
        + [pl.BlockSpec(memory_space=pltpu.SMEM)] * 3
        + [any_space] * 4,
        out_specs=[pl.BlockSpec(memory_space=pltpu.VMEM)] * 4,
        scratch_shapes=[
            pltpu.VMEM((2,) + rows + (width,), bf16),
            pltpu.VMEM((2,) + rows + (2 * q_wide,), bf16),
            pltpu.VMEM((2,) + rows + (width,), bf16),
            pltpu.VMEM((2,) + rows + (2 * wide,), bf16),
            pltpu.VMEM(rows + (width,), bf16),
            pltpu.VMEM(rows + (2 * q_wide,), bf16),
            pltpu.VMEM(rows + (width,), bf16),
            pltpu.VMEM(rows + (2 * wide,), bf16),
            pltpu.VMEM((2, 2, width, cols), bf16),
            pltpu.VMEM((2, 2 * q_wide, width), bf16),
            pltpu.VMEM(rows + (width,), bf16),
            pltpu.VMEM(rows + (width,), bf16),
            pltpu.VMEM(rows + (width,), bf16),
            pltpu.VMEM(rows + (width,), bf16),
            pltpu.VMEM((2, 2, SLOT, cols), bf16),
            pltpu.VMEM((2, 2, SLOT, LANES), f32),
            pltpu.VMEM((2, 2, group * SLOT, SLOT), f32),
            pltpu.VMEM((2, SLOT, q_wide), bf16),
            pltpu.VMEM((2, 2, 2, SUB, width), bf16),
        ]
        + scatter_bufs(wide, cols) * 2
        + scatter_bufs(q_wide, q_wide) * 2
        + [
            pltpu.SemaphoreType.DMA((9, 2, 4)),
            pltpu.SemaphoreType.DMA((9, 2, 4)),
            pltpu.SemaphoreType.DMA((6, 2)),
            pltpu.SemaphoreType.DMA((6, 2)),
            pltpu.SemaphoreType.DMA((11,)),
            pltpu.SemaphoreType.DMA((11,)),
            pltpu.SemaphoreType.DMA((9,)),
        ],
        compiler_params=pltpu.CompilerParams(
            collective_id=0, has_side_effects=True, vmem_limit_bytes=56 * 1024 * 1024
        ),
    )(
        inputs.reshape(2, 2, 2, 2, SUB, width),
        head_grad.reshape(2, 2, 2, 2, SUB, width),
        noise_mask,
        *(jnp.swapaxes(v, 1, 2) for v in (lengths, rewards, groups)),
        query_weight,
        key_weight,
        value_weight,
        out_weight,
    )


def solution(mesh):
    return jax.shard_map(
        local,
        mesh=mesh,
        in_specs=(
            P(None, "tp", "fsdp"),
            P(None, "tp", "fsdp"),
            P(None, "tp"),
            P(),
            P(),
            P(),
            P("pp", "fsdp", "tp"),
            P("pp", "fsdp", "tp"),
            P("pp", "fsdp", "tp"),
            P("pp", "tp", "fsdp"),
        ),
        out_specs=(
            P("pp", "fsdp", "tp"),
            P("pp", "fsdp", "tp"),
            P("pp", "fsdp", "tp"),
            P("pp", "tp", "fsdp"),
        ),
        check_vma=False,
    )
```

```python
import jax
import jax.numpy as jnp
from jax import lax
from jax.experimental import pallas as pl
from jax.experimental.pallas import tpu as pltpu
from jax.sharding import PartitionSpec as P

MODEL_WIDTH = 8192
HEAD_WIDTH = 128
SLOT = 32
LANES = 128

epsilon = 1e-06
masked_score = -1e30
MESH = pl.DeviceIdType.MESH
NN = ((1,), (0,))
NT = ((1,), (1,))
TN = ((0,), (0,))


def dot(a, b, contract):
    return lax.dot_general(a, b, (contract, ((), ())), preferred_element_type=jnp.float32)


RS_QKV0, RS_QKV1, RS_HEAD1, RS_HEAD0, AG_HEAD0, AG_GRAD1, AG_HEAD1, AG_GRAD0, AG_FAR0 = range(9)
AG_STREAM0, AG_TOP, RS_OUT0, AG_STREAM1, RS_IN1, AG_OUT0 = range(6)
HALVES = (0, 1)
PEERS = (2, 1, 3)
SIDE = 4
SUB = 16


def split_tile(first, second):
    lane = lax.broadcasted_iota(jnp.int32, first.shape[:-1] + (LANES,), first.ndim - 1)
    tile = jnp.zeros(lane.shape, jnp.float32)
    for i, column in enumerate((first, second)):
        high = column.astype(jnp.bfloat16).astype(jnp.float32)
        tile = jnp.where(lane == 2 * i, high, jnp.where(lane == 2 * i + 1, column - high, tile))
    return tile.astype(jnp.bfloat16)


def join_tile(tile):
    tile = tile.astype(jnp.float32)
    return tile[..., 0:1] + tile[..., 1:2], tile[..., 2:3] + tile[..., 3:4]


def token_weights(lengths, rewards, groups, noise, core, t):
    square = (LANES, LANES)
    micros, packed, slots = lengths.shape
    lane = lax.broadcasted_iota(jnp.int32, (1, LANES), 1)

    def row(ref):
        value = jnp.full((1, LANES), -1, jnp.int32)
        for m in range(micros):
            for s in range(slots):
                for c in range(packed):
                    value = jnp.where(lane == (m * slots + s) * packed + c, ref[m, c, s], value)
        return jnp.broadcast_to(value.astype(jnp.float32), square)

    group_row, reward_row, length_row = row(groups), row(rewards), row(lengths)
    member = (group_row == group_row.T).astype(jnp.float32)
    reward_column = reward_row.T
    count = jnp.sum(member, 0, keepdims=True)
    mean = jnp.sum(member * reward_column, 0, keepdims=True) / count
    centered = reward_column - mean
    variance = jnp.sum(member * centered * centered, 0, keepdims=True) / count
    advantage = (reward_row - mean) / jnp.maximum(jnp.sqrt(variance), 1.0)
    token = lax.broadcasted_iota(jnp.int32, square, 0)
    lanes = lax.broadcasted_iota(jnp.int32, square, 1)
    first = core * slots * packed + (t * (LANES // SLOT) + (token >> 5)) * packed
    length = jnp.sum(jnp.where(lanes == first, length_row, 0.0), -1, keepdims=True)
    position = (token & (SLOT - 1)).astype(jnp.float32)
    chosen = lanes == first + (position >= length).astype(jnp.int32)
    advantage = jnp.sum(jnp.where(chosen, advantage, 0.0), -1, keepdims=True)
    length = jnp.sum(jnp.where(chosen, length_row, 0.0), -1, keepdims=True)
    noise = jnp.broadcast_to(noise[pl.ds(core, 1), :].astype(jnp.float32), square).T
    return advantage * SLOT / length * noise[:, :1]


def kernel(
    x_in, g_in, noise, lengths, rewards, groups, wq, wk, wv, wo,
    dq_out, dk_out, dv_out, do_out,
    X, H, G, Q, FX, FH, FG, FQ, W, WO, D, E, DH, EH, ROWS, INV, PROBS, HG, GIN, *rest,
):
    scatter_bufs, (fs, fr, zs, zr, ss, sr, ls) = rest[:36], rest[36:]
    rs_bufs = {
        phase: scatter_bufs[9 * i : 9 * i + 9]
        for i, phase in enumerate((RS_QKV0, RS_QKV1, RS_HEAD1, RS_HEAD0))
    }
    core, f, t = lax.axis_index("pp"), lax.axis_index("fsdp"), lax.axis_index("tp")
    far = 1 - core
    y, x = f >> 2, f & 3
    j, g = x >> 1, x & 1
    ways = (((y + 1) & 3, (x + 1) & 3), ((y + 3) & 3, (x + 3) & 3))
    y_opp, x_opp = (y + 2) & 3, (x + 2) & 3
    q_wide = wq.shape[2] // 2
    k_wide = wk.shape[2] // 2
    cols = q_wide + 2 * k_wide
    wide = cols + LANES
    group = q_wide // HEAD_WIDTH
    scale = HEAD_WIDTH**-0.5

    def span(which, stride, width, at=0):
        return pl.ds(pl.multiple_of(which * stride + at, LANES), width)

    def other(mine, k):
        return (mine + k) & (SIDE - 1)

    def remote(src, dst, send, recv, **at):
        return pltpu.make_async_remote_copy(
            src_ref=src, dst_ref=dst, send_sem=send, recv_sem=recv,
            device_id=at, device_id_type=MESH,
        )

    cuts = [
        (w, gg * width, gg, at, width)
        for gg in (0, 1)
        for w, at, width in ((wq, 0, q_wide), (wk, q_wide, k_wide), (wv, q_wide + k_wide, k_wide))
    ]
    loads = [pltpu.make_async_copy(x_in.at[core], X.at[0, :, t], ls.at[0])] + [
        pltpu.make_async_copy(
            w.at[0, :, pl.ds(at, width)], W.at[core, gg, :, pl.ds(to, width)], ls.at[1 + i]
        )
        for i, (w, at, gg, to, width) in enumerate(cuts)
    ]
    loads += [
        pltpu.make_async_copy(wo.at[0], WO.at[core], ls.at[7]),
        pltpu.make_async_copy(g_in.at[core], GIN, ls.at[8]),
    ]
    for c in loads:
        c.start()

    barrier = pltpu.get_barrier_semaphore()
    for k in (1, 2, 3):
        for at in (
            {"fsdp": y * SIDE + other(x, k)},
            {"fsdp": other(y, k) * SIDE + x},
            {"pp": far, "fsdp": y * SIDE + other(x, k)},
            {"pp": far, "fsdp": other(y, k) * SIDE + x},
            {"tp": other(t, k)},
        ):
            pl.semaphore_signal(barrier, inc=1, device_id=at, device_id_type=MESH)
    pl.semaphore_signal(barrier, inc=1, device_id={"pp": far}, device_id_type=MESH)
    pl.semaphore_wait(barrier, 16)

    def z_gather(phase, buf, h):
        for k in PEERS:
            remote(buf.at[h, t], buf.at[h, t], zs.at[phase, h], zr.at[phase, h], tp=other(t, k)).start()

    def z_scatter(phase, send, recv, h):
        for k in PEERS:
            b = other(t, k)
            remote(send.at[h, b], recv.at[h, t], zs.at[phase, h], zr.at[phase, h], tp=b).start()

    def z_all(phase, buf, h):
        three = buf.at[h, pl.ds(0, SIDE - 1)]
        return remote(three, three, zs.at[phase, h], zr.at[phase, h], tp=t)

    def z_sum(phase, send, recv, h, total):
        z_all(phase, recv, h).wait_recv()
        total = total + send[h, t].astype(jnp.float32)
        for k in PEERS:
            total = total + recv[h, other(t, k)].astype(jnp.float32)
        return total.astype(jnp.bfloat16)

    def push(phase, h, kind, src, dst, **at):
        remote(src, dst, fs.at[phase, h, kind], fr.at[phase, h, kind], **at).start()

    def f_all(phase, h, kind):
        S, RA, RB, UA, UB, VA, VB, FA, FB = rs_bufs[
            {AG_HEAD0: RS_HEAD0, AG_HEAD1: RS_HEAD0, AG_GRAD0: RS_QKV0, AG_GRAD1: RS_QKV0}.get(phase, phase)
        ]
        three = pl.ds(0, SIDE - 1)
        refs = (RA.at[h], RB.at[h], VA.at[h, three], VB.at[h, three])
        if phase >= AG_HEAD0:
            refs = refs[2:] + refs[:2]
        ref = (refs + (FA.at[h], FB.at[h]))[kind]
        return remote(ref, ref, fs.at[phase, h, kind], fr.at[phase, h, kind], fsdp=f)

    def widths(buf_cols):
        return (wide, cols) if buf_cols == 2 * wide else (q_wide, q_wide)

    def rs_start(phase, h):
        S, RA, RB, UA, UB, VA, VB, FA, FB = rs_bufs[phase]
        ca, cb = widths(S.shape[-1])

        def second(x2, part):
            return S.at[h, pl.ds(2 * part, 2), x2 >> 1, 1, :, span(x2 & 1, ca, cb)]

        for d, (y2, x2) in enumerate(ways):
            push(phase, h, 4, S.at[h, y_opp, d, 0], FA.at[h, d], fsdp=y2 * SIDE + x)
            push(phase, h, 5, second(x_opp, d), FB.at[h, d], fsdp=y * SIDE + x2)
        for d, (y2, x2) in enumerate(ways):
            push(phase, h, 0, S.at[h, y2, 1 - d, 0], RA.at[h, d, 1 - d], fsdp=y2 * SIDE + x)
            push(
                phase, h, 1, second(x2, 1 - d), RB.at[h, d, pl.ds(2 * (1 - d), 2)], fsdp=y * SIDE + x2
            )

    def rs_pass(phase, h):
        S, RA, RB, UA, UB, VA, VB, FA, FB = rs_bufs[phase]
        ca, cb = widths(S.shape[-1])
        f_all(phase, h, 4).wait_recv()
        for d, (y2, x2) in enumerate(ways):
            total = S[h, y2, d, 0].astype(jnp.float32) + FA[h, d].astype(jnp.float32)
            S[h, y2, d, 0] = total.astype(jnp.bfloat16)
            push(phase, h, 0, S.at[h, y2, d, 0], RA.at[h, d, d], fsdp=y2 * SIDE + x)
        f_all(phase, h, 5).wait_recv()
        for d, (y2, x2) in enumerate(ways):
            at = (h, pl.ds(2 * d, 2), x2 >> 1, 1, slice(None), span(x2 & 1, ca, cb))
            S[at] = (S[at].astype(jnp.float32) + FB[h, d].astype(jnp.float32)).astype(jnp.bfloat16)
            push(phase, h, 1, S.at[at], RB.at[h, d, pl.ds(2 * d, 2)], fsdp=y * SIDE + x2)

    def rs_mid(phase, h):
        S, RA, RB, UA, UB, VA, VB, FA, FB = rs_bufs[phase]
        ca, cb = widths(S.shape[-1])
        f_all(phase, h, 0).wait_recv()
        total = S[h, y, :, 0].astype(jnp.float32)
        for d in (0, 1):
            total = total + RA[h, d].astype(jnp.float32)
        UA[h] = total.astype(jnp.bfloat16)
        for k in PEERS:
            x2 = other(x, k)
            push(
                phase, h, 2, UA.at[h, x2 >> 1, :, span(x2 & 1, ca, ca)], VA.at[h, x], fsdp=y * SIDE + x2
            )
        f_all(phase, h, 1).wait_recv()
        total = S[h, :, j, 1, :, span(g, ca, cb)].astype(jnp.float32)
        for d in (0, 1):
            total = total + RB[h, d].astype(jnp.float32)
        UB[h] = total.astype(jnp.bfloat16)
        for k in PEERS:
            y2 = other(y, k)
            push(phase, h, 3, UB.at[h, y2], VB.at[h, y], fsdp=y2 * SIDE + x)

    def rs_end(phase, h):
        S, RA, RB, UA, UB, VA, VB, FA, FB = rs_bufs[phase]
        ca, cb = widths(S.shape[-1])
        f_all(phase, h, 2).wait_recv()
        first = UA[h, j, :, span(g, ca, ca)].astype(jnp.float32)
        for k in PEERS:
            first = first + VA[h, other(x, k)].astype(jnp.float32)
        f_all(phase, h, 3).wait_recv()
        second = UB[h, y].astype(jnp.float32)
        for k in PEERS:
            second = second + VB[h, other(y, k)].astype(jnp.float32)
        return first, second

    def ag_start(phase, buf, h):
        ca, cb = widths(buf.shape[-1])
        first = buf.at[h, y, j, 0, :, span(g, ca, ca)]
        second = buf.at[h, y, j, 1, :, span(g, ca, cb)]
        for k in PEERS:
            push(phase, h, 0, first, first, fsdp=y * SIDE + other(x, k))
            push(phase, h, 1, second, second, fsdp=other(y, k) * SIDE + x)

    def ag_mid(phase, buf, h):
        ca, cb = widths(buf.shape[-1])
        first = buf.at[h, y, :, 0]
        f_all(phase, h, 0).wait_recv()
        for y2, _ in ways:
            push(phase, h, 2, first, first, fsdp=y2 * SIDE + x)
        second = buf.at[h, :, j, 1, :, span(g, ca, cb)]
        f_all(phase, h, 1).wait_recv()
        for _, x2 in ways:
            push(phase, h, 3, second, second, fsdp=y * SIDE + x2)

    def pass_first(phase, buf, h):
        for d, (y2, _) in enumerate(ways):
            ref = buf.at[h, ways[1 - d][0], d, 0]
            push(phase, h, 4, ref, ref, fsdp=y2 * SIDE + x)

    def pass_second(phase, buf, h):
        ca, cb = widths(buf.shape[-1])
        for d, (_, x2) in enumerate(ways):
            x3 = ways[1 - d][1]
            ref = buf.at[h, pl.ds(2 * d, 2), x3 >> 1, 1, :, span(x3 & 1, ca, cb)]
            push(phase, h, 5, ref, ref, fsdp=y * SIDE + x2)

    def ag_pass(phase, buf, h):
        f_all(phase, h, 2).wait_recv()
        pass_first(phase, buf, h)
        f_all(phase, h, 3).wait_recv()
        pass_second(phase, buf, h)

    def ag_end(phase, h):
        f_all(phase, h, 4).wait_recv()
        f_all(phase, h, 5).wait_recv()

    def last_mid(h):
        first, second = Q.at[0, h, y, :, 0], Q.at[0, h, :, j, 1, :, span(g, wide, cols)]
        first_far, second_far = FQ.at[h, y, :, 0], FQ.at[h, :, j, 1, :, span(g, wide, cols)]
        f_all(AG_GRAD0, h, 0).wait_recv()

        @pl.when(core == 0)
        def _():
            for y2, _ in ways:
                push(AG_GRAD0, h, 2, first, first, fsdp=y2 * SIDE + x)

        @pl.when(core == 1)
        def _():
            for y2 in (ways[0][0], ways[1][0], y):
                push(AG_FAR0, h, 2, first, first_far, pp=far, fsdp=y2 * SIDE + x)

        f_all(AG_GRAD0, h, 1).wait_recv()

        @pl.when(core == 0)
        def _():
            for _, x2 in ways:
                push(AG_GRAD0, h, 3, second, second, fsdp=y * SIDE + x2)

        @pl.when(core == 1)
        def _():
            for x2 in (ways[0][1], ways[1][1], x):
                push(AG_FAR0, h, 3, second, second_far, pp=far, fsdp=y * SIDE + x2)

    def far_all(h, kind):
        FA, FB = rs_bufs[RS_QKV0][7:]
        three = pl.ds(0, SIDE - 1)
        ref = {
            2: Q.at[0, h, three, :, 0],
            3: Q.at[0, h, three, :, :, :, pl.ds(0, cols)],
            4: FA.at[h],
            5: FB.at[h],
        }[kind]
        return remote(ref, ref, fs.at[AG_FAR0, h, kind], fr.at[AG_FAR0, h, kind], fsdp=f)

    def last_pass(h):
        ag_pass(AG_GRAD0, Q.at[0], h)
        far_all(h, 2).wait_recv()
        pass_first(AG_FAR0, FQ, h)
        far_all(h, 3).wait_recv()
        pass_second(AG_FAR0, FQ, h)

    def flat(value):
        return value.reshape(-1, value.shape[-1])

    def project(layer, gathered, phase, h):
        S = rs_bufs[phase][0]
        z_all(gathered, X.at[layer], h).wait_recv()
        rows = flat(X[layer, h])
        for gg in (0, 1):
            S[h, :, :, :, :, pl.ds(gg * wide, cols)] = (
                dot(rows, W[layer, gg], NN).astype(jnp.bfloat16).reshape(SIDE, 2, 2, SUB, cols)
            )
        squares = []
        for a in (0, 1):
            part = X[layer, h, :, :, a].astype(jnp.float32)
            squares.append(jnp.sum(part * part, -1, keepdims=True))
        tile = split_tile(*squares)
        for gg in (0, 1):
            S[h, :, :, 0, :, pl.ds(gg * wide + cols, LANES)] = tile
        rs_start(phase, h)

    def attend(layer, phase, h):
        first, second = rs_end(phase, h)
        squares = jnp.concatenate(join_tile(first[:, cols:]), 0)
        inv_rms = lax.rsqrt(squares / MODEL_WIDTH + epsilon)
        rows = (jnp.concatenate([first[:, :cols], second], 0) * inv_rms).astype(jnp.bfloat16)
        ROWS[layer, h] = rows
        INV[layer, h] = jnp.broadcast_to(inv_rms, (SLOT, LANES))
        queries = jnp.concatenate([rows[:, i * HEAD_WIDTH : (i + 1) * HEAD_WIDTH] for i in range(group)], 0)
        keys, values = rows[:, q_wide : q_wide + k_wide], rows[:, q_wide + k_wide :]
        scores = dot(queries, keys, NT) * scale
        cut = lengths[core, 0, y * SIDE + 2 * h + j]
        later = [
            ((lax.broadcasted_iota(jnp.int32, scores.shape, d) & (SLOT - 1)) >= cut).astype(jnp.int32)
            for d in (0, 1)
        ]
        scores = jnp.where(later[0] == later[1], scores, masked_score)
        raised = jnp.exp(scores - jnp.max(scores, -1, keepdims=True))
        probs = raised / jnp.sum(raised, -1, keepdims=True)
        PROBS[layer, h] = probs
        mixed = dot(probs.astype(jnp.bfloat16), values, NN).astype(jnp.bfloat16)
        for i in range(group):
            H[layer, h, y, j, :, :, span(g, q_wide, HEAD_WIDTH, i * HEAD_WIDTH)] = mixed[
                i * SLOT : (i + 1) * SLOT
            ].reshape(2, SUB, HEAD_WIDTH)

    def head_end(phase, h):
        first, second = rs_end(phase, h)
        HG[h] = jnp.concatenate([first, second], 0).astype(jnp.bfloat16)

    def attend_back(layer, h):
        rows, head_grad, inv_rms, probs = ROWS[layer, h], HG[h], INV[layer, h], PROBS[layer, h]

        def stacked(value):
            return jnp.concatenate(
                [value[:, i * HEAD_WIDTH : (i + 1) * HEAD_WIDTH] for i in range(group)], 0
            )

        queries, grads = stacked(rows), stacked(head_grad)
        keys, values = rows[:, q_wide : q_wide + k_wide], rows[:, q_wide + k_wide :]
        prob_grad = dot(grads, values, NT)
        value_grad = dot(probs.astype(jnp.bfloat16), grads, TN)
        score_grad = probs * (prob_grad - jnp.sum(prob_grad * probs, -1, keepdims=True))
        score_grad = score_grad.astype(jnp.bfloat16)
        query_grad = dot(score_grad, keys, NN) * scale
        key_grad = dot(score_grad, queries, TN) * scale
        total = jnp.zeros((SLOT, LANES), jnp.float32)
        parts = [query_grad[i * SLOT : (i + 1) * SLOT] for i in range(group)] + [key_grad, value_grad]
        for i, part in enumerate(parts):
            part = part.astype(jnp.bfloat16).astype(jnp.float32)
            total = total + part * rows[:, i * HEAD_WIDTH : (i + 1) * HEAD_WIDTH].astype(jnp.float32)
            Q[layer, h, y, j, :, :, span(g, wide, HEAD_WIDTH, i * HEAD_WIDTH)] = (
                (part * inv_rms).astype(jnp.bfloat16).reshape(2, SUB, HEAD_WIDTH)
            )
        share = inv_rms[:, :1] * inv_rms[:, :1] * jnp.sum(total, -1, keepdims=True) / MODEL_WIDTH
        Q[layer, h, y, j, 0, :, span(g, wide, LANES, cols)] = split_tile(share[:SUB], share[SUB:])

    def head_grads(layer, gathered, phase, h):
        S = rs_bufs[phase][0]
        z_all(gathered, G.at[layer], h).wait_recv()
        S[h] = dot(flat(G[layer, h]), WO[layer], NT).astype(jnp.bfloat16).reshape(S.shape[1:])
        rs_start(phase, h)

    def project_out(h):
        ag_end(AG_HEAD0, h)
        D[h] = dot(flat(H[0, h]), WO[0], NN).astype(jnp.bfloat16).reshape(D.shape[1:])
        z_scatter(RS_OUT0, D, E, h)

    def project_back(h):
        ag_end(AG_GRAD1, h)
        back = sum(
            dot(flat(Q[1, h, :, :, :, :, pl.ds(gg * wide, cols)]), W[1, gg], NT) for gg in (0, 1)
        ).reshape(DH.shape[1:])
        tiles = [
            Q[1, h, :, :, 0, :, pl.ds(gg * wide + cols, LANES)].astype(jnp.float32) for gg in (0, 1)
        ]
        shares = join_tile(tiles[0] + tiles[1])
        for a in (0, 1):
            term = back[:, :, a] - X[1, h, :, :, a].astype(jnp.float32) * shares[a]
            DH[h, :, :, a] = term.astype(jnp.bfloat16)
        z_scatter(RS_IN1, DH, EH, h)

    def hand_over(i, src, dst):
        return remote(src, dst, ss.at[i], sr.at[i], pp=far)

    x_far, h_far, g_far = hand_over(7, X.at[far], FX), hand_over(8, H.at[far], FH), hand_over(9, G.at[far], FG)
    q_far = hand_over(10, Q.at[1], FQ)
    def weight_grads(h):
        rows, far_rows = flat(X[core, h]), flat(FX[h])
        for gg in (0, 1):
            at = pl.ds(gg * wide, cols)
            term = dot(rows, flat(Q[core, h, :, :, :, :, at]), TN) + dot(
                far_rows, flat(FQ[h, :, :, :, :, at]), TN
            )
            for to, width, out in (
                (0, q_wide, dq_out), (q_wide, k_wide, dk_out), (q_wide + k_wide, k_wide, dv_out)
            ):
                to_at = pl.ds(gg * width, width)
                part = term[:, to : to + width]
                out[0, :, to_at] = part if h == 0 else out[0, :, to_at] + part

    loads[0].wait()
    for h in HALVES:
        z_gather(AG_STREAM0, X.at[0], h)
    swaps = [
        remote(
            w.at[0, :, pl.ds(at, width)], W.at[core, gg, :, pl.ds(to, width)], ss.at[i], sr.at[i], pp=far
        )
        for i, (w, at, gg, to, width) in enumerate(cuts)
    ] + [remote(wo.at[0], WO.at[core], ss.at[6], sr.at[6], pp=far)]
    for c in swaps[:6]:
        c.start()
    for c in loads[1:8]:
        c.wait()
    for c in swaps[:6]:
        c.wait_recv()
    for h in HALVES:
        project(0, AG_STREAM0, RS_QKV0, h)
    for h in HALVES:
        rs_pass(RS_QKV0, h)
    swaps[6].start()
    loads[8].wait()
    top = token_weights(lengths, rewards, groups, noise, core, t)
    top = (-top * flat(GIN[...]).astype(jnp.float32)).astype(jnp.bfloat16)
    G[1, :, t] = top.reshape(GIN.shape)
    for h in HALVES:
        z_gather(AG_TOP, G.at[1], h)
    for h in HALVES:
        rs_mid(RS_QKV0, h)
    for h in HALVES:
        attend(0, RS_QKV0, h)
        ag_start(AG_HEAD0, H.at[0], h)
    for h in HALVES:
        ag_mid(AG_HEAD0, H.at[0], h)
    for h in HALVES:
        ag_pass(AG_HEAD0, H.at[0], h)
    swaps[6].wait_recv()
    for h in HALVES:
        project_out(h)
    for h in HALVES:
        head_grads(1, AG_TOP, RS_HEAD1, h)
    for h in HALVES:
        X[1, h, t] = z_sum(RS_OUT0, D, E, h, X[0, h, t].astype(jnp.float32))
        z_gather(AG_STREAM1, X.at[1], h)
    for h in HALVES:
        rs_pass(RS_HEAD1, h)
    for h in HALVES:
        project(1, AG_STREAM1, RS_QKV1, h)
    for h in HALVES:
        rs_mid(RS_HEAD1, h)
    for h in HALVES:
        rs_pass(RS_QKV1, h)
    x_far.start()
    for h in HALVES:
        head_end(RS_HEAD1, h)
    for h in HALVES:
        rs_mid(RS_QKV1, h)
    for h in HALVES:
        attend(1, RS_QKV1, h)
        attend_back(1, h)
        ag_start(AG_GRAD1, Q.at[1], h)
    for h in HALVES:
        ag_mid(AG_GRAD1, Q.at[1], h)
    for h in HALVES:
        ag_pass(AG_GRAD1, Q.at[1], h)
    for h in HALVES:
        project_back(h)

    @pl.when(core == 0)
    def _():
        q_far.start()

    for h in HALVES:
        ag_start(AG_HEAD1, H.at[1], h)
    for h in HALVES:
        G[0, h, t] = z_sum(RS_IN1, DH, EH, h, G[1, h, t].astype(jnp.float32))
        z_gather(AG_OUT0, G.at[0], h)
    for h in HALVES:
        ag_mid(AG_HEAD1, H.at[1], h)
    for h in HALVES:
        head_grads(0, AG_OUT0, RS_HEAD0, h)
    g_far.start()
    for h in HALVES:
        ag_pass(AG_HEAD1, H.at[1], h)
    for h in HALVES:
        rs_pass(RS_HEAD0, h)
    for h in HALVES:
        ag_end(AG_HEAD1, h)
    h_far.start()
    do_out[0] = dot(flat(H[core]), flat(G[core]), TN)
    for h in HALVES:
        rs_mid(RS_HEAD0, h)
    for h in HALVES:
        head_end(RS_HEAD0, h)
        attend_back(0, h)
        ag_start(AG_GRAD0, Q.at[0], h)
    for h in HALVES:
        last_mid(h)

    @pl.when(core == 0)
    def _():
        for h in HALVES:
            last_pass(h)

    for c in (x_far, h_far, g_far):
        c.wait_recv()
    do_out[0] += dot(flat(FH[...]), flat(FG[...]), TN)
    for h in HALVES:

        @pl.when(core == 0)
        def _():
            ag_end(AG_GRAD0, h)
            far_all(h, 4).wait_recv()
            far_all(h, 5).wait_recv()

        if h == 0:

            @pl.when(core == 1)
            def _():
                q_far.wait_recv()

        weight_grads(h)

    for phase in range(AG_GRAD0):
        for h in HALVES:
            for kind in range(6):
                f_all(phase, h, kind).wait_send()
    for h in HALVES:
        for kind in (0, 1):
            f_all(AG_GRAD0, h, kind).wait_send()

        @pl.when(core == 0)
        def _():
            for kind in (2, 3, 4, 5):
                f_all(AG_GRAD0, h, kind).wait_send()
            for kind in (4, 5):
                far_all(h, kind).wait_send()

        @pl.when(core == 1)
        def _():
            for kind in (2, 3):
                far_all(h, kind).wait_send()

    for phase, buf in (
        (AG_STREAM0, X.at[0]), (AG_TOP, G.at[1]), (RS_OUT0, E),
        (AG_STREAM1, X.at[1]), (RS_IN1, EH), (AG_OUT0, G.at[0]),
    ):
        for h in HALVES:
            z_all(phase, buf, h).wait_send()
    for c in swaps + [x_far, h_far, g_far]:
        c.wait_send()

    @pl.when(core == 0)
    def _():
        q_far.wait_send()


def local(
    inputs,
    head_grad,
    noise_mask,
    lengths,
    rewards,
    groups,
    query_weight,
    key_weight,
    value_weight,
    out_weight,
):
    row_count, width = inputs.shape[1:]
    q_wide, k_wide = query_weight.shape[2] // 2, key_weight.shape[2] // 2
    cols = q_wide + 2 * k_wide
    wide = cols + LANES
    group = q_wide // k_wide

    bf16, f32 = jnp.bfloat16, jnp.float32
    any_space = pl.BlockSpec(memory_space=pl.ANY)
    rows = (2, SIDE, 2, 2, SUB)

    def scatter_bufs(ca, cb):
        return [
            pltpu.VMEM(shape, bf16)
            for shape in (
                rows + (2 * ca,),
                (2, 2, 2, SUB, 2 * ca),
                (2, 2, SIDE, SUB, cb),
                (2, 2, SUB, 2 * ca),
                (2, SIDE, SUB, cb),
                (2, SIDE, SUB, ca),
                (2, SIDE, SUB, cb),
                (2, 2, SUB, 2 * ca),
                (2, 2, 2, SUB, cb),
            )
        ]

    return pl.pallas_call(
        kernel,
        out_shape=[
            pltpu.VMEM(w.shape, f32)
            for w in (query_weight, key_weight, value_weight, out_weight)
        ],
        in_specs=[any_space, any_space, pl.BlockSpec(memory_space=pltpu.VMEM)]
        + [pl.BlockSpec(memory_space=pltpu.SMEM)] * 3
        + [any_space] * 4,
        out_specs=[pl.BlockSpec(memory_space=pltpu.VMEM)] * 4,
        scratch_shapes=[
            pltpu.VMEM((2,) + rows + (width,), bf16),
            pltpu.VMEM((2,) + rows + (2 * q_wide,), bf16),
            pltpu.VMEM((2,) + rows + (width,), bf16),
            pltpu.VMEM((2,) + rows + (2 * wide,), bf16),
            pltpu.VMEM(rows + (width,), bf16),
            pltpu.VMEM(rows + (2 * q_wide,), bf16),
            pltpu.VMEM(rows + (width,), bf16),
            pltpu.VMEM(rows + (2 * wide,), bf16),
            pltpu.VMEM((2, 2, width, cols), bf16),
            pltpu.VMEM((2, 2 * q_wide, width), bf16),
            pltpu.VMEM(rows + (width,), bf16),
            pltpu.VMEM(rows + (width,), bf16),
            pltpu.VMEM(rows + (width,), bf16),
            pltpu.VMEM(rows + (width,), bf16),
            pltpu.VMEM((2, 2, SLOT, cols), bf16),
            pltpu.VMEM((2, 2, SLOT, LANES), f32),
            pltpu.VMEM((2, 2, group * SLOT, SLOT), f32),
            pltpu.VMEM((2, SLOT, q_wide), bf16),
            pltpu.VMEM((2, 2, 2, SUB, width), bf16),
        ]
        + scatter_bufs(wide, cols) * 2
        + scatter_bufs(q_wide, q_wide) * 2
        + [
            pltpu.SemaphoreType.DMA((9, 2, 6)),
            pltpu.SemaphoreType.DMA((9, 2, 6)),
            pltpu.SemaphoreType.DMA((6, 2)),
            pltpu.SemaphoreType.DMA((6, 2)),
            pltpu.SemaphoreType.DMA((11,)),
            pltpu.SemaphoreType.DMA((11,)),
            pltpu.SemaphoreType.DMA((9,)),
        ],
        compiler_params=pltpu.CompilerParams(
            collective_id=0, has_side_effects=True, vmem_limit_bytes=56 * 1024 * 1024
        ),
    )(
        inputs.reshape(2, 2, 2, 2, SUB, width),
        head_grad.reshape(2, 2, 2, 2, SUB, width),
        noise_mask,
        *(jnp.swapaxes(v, 1, 2) for v in (lengths, rewards, groups)),
        query_weight,
        key_weight,
        value_weight,
        out_weight,
    )


def solution(mesh):
    return jax.shard_map(
        local,
        mesh=mesh,
        in_specs=(
            P(None, "tp", "fsdp"),
            P(None, "tp", "fsdp"),
            P(None, "tp"),
            P(),
            P(),
            P(),
            P("pp", "fsdp", "tp"),
            P("pp", "fsdp", "tp"),
            P("pp", "fsdp", "tp"),
            P("pp", "tp", "fsdp"),
        ),
        out_specs=(
            P("pp", "fsdp", "tp"),
            P("pp", "fsdp", "tp"),
            P("pp", "fsdp", "tp"),
            P("pp", "tp", "fsdp"),
        ),
        check_vma=False,
    )
```

```python
import jax
import jax.numpy as jnp
from jax import lax
from jax.experimental import pallas as pl
from jax.experimental.pallas import tpu as pltpu
from jax.sharding import PartitionSpec as P

MODEL_WIDTH = 8192
HEAD_WIDTH = 128
SLOT = 32
LANES = 128

epsilon = 1e-06
masked_score = -1e30
MESH = pl.DeviceIdType.MESH
NN = ((1,), (0,))
NT = ((1,), (1,))
TN = ((0,), (0,))


def dot(a, b, contract):
    return lax.dot_general(a, b, (contract, ((), ())), preferred_element_type=jnp.float32)


RS_QKV0, RS_QKV1, RS_HEAD1, RS_HEAD0, AG_HEAD0, AG_GRAD1, AG_HEAD1, AG_GRAD0, AG_FAR0 = range(9)
AG_STREAM0, AG_TOP, RS_OUT0, AG_STREAM1, RS_IN1, AG_OUT0 = range(6)
HALVES = (0, 1)
PEERS = (2, 1, 3)
SIDE = 4
SUB = 16


def split_tile(first, second):
    lane = lax.broadcasted_iota(jnp.int32, first.shape[:-1] + (LANES,), first.ndim - 1)
    tile = jnp.zeros(lane.shape, jnp.float32)
    for i, column in enumerate((first, second)):
        high = column.astype(jnp.bfloat16).astype(jnp.float32)
        tile = jnp.where(lane == 2 * i, high, jnp.where(lane == 2 * i + 1, column - high, tile))
    return tile.astype(jnp.bfloat16)


def join_tile(tile):
    tile = tile.astype(jnp.float32)
    return tile[..., 0:1] + tile[..., 1:2], tile[..., 2:3] + tile[..., 3:4]


def token_weights(lengths, rewards, groups, noise, core, t):
    square = (LANES, LANES)
    micros, packed, slots = lengths.shape
    lane = lax.broadcasted_iota(jnp.int32, (1, LANES), 1)

    def row(ref):
        value = jnp.full((1, LANES), -1, jnp.int32)
        for m in range(micros):
            for s in range(slots):
                for c in range(packed):
                    value = jnp.where(lane == (m * slots + s) * packed + c, ref[m, c, s], value)
        return jnp.broadcast_to(value.astype(jnp.float32), square)

    group_row, reward_row, length_row = row(groups), row(rewards), row(lengths)
    member = (group_row == group_row.T).astype(jnp.float32)
    reward_column = reward_row.T
    count = jnp.sum(member, 0, keepdims=True)
    mean = jnp.sum(member * reward_column, 0, keepdims=True) / count
    centered = reward_column - mean
    variance = jnp.sum(member * centered * centered, 0, keepdims=True) / count
    advantage = (reward_row - mean) / jnp.maximum(jnp.sqrt(variance), 1.0)
    token = lax.broadcasted_iota(jnp.int32, square, 0)
    lanes = lax.broadcasted_iota(jnp.int32, square, 1)
    first = core * slots * packed + (t * (LANES // SLOT) + (token >> 5)) * packed
    length = jnp.sum(jnp.where(lanes == first, length_row, 0.0), -1, keepdims=True)
    position = (token & (SLOT - 1)).astype(jnp.float32)
    chosen = lanes == first + (position >= length).astype(jnp.int32)
    advantage = jnp.sum(jnp.where(chosen, advantage, 0.0), -1, keepdims=True)
    length = jnp.sum(jnp.where(chosen, length_row, 0.0), -1, keepdims=True)
    noise = jnp.broadcast_to(noise[pl.ds(core, 1), :].astype(jnp.float32), square).T
    return advantage * SLOT / length * noise[:, :1]


def kernel(
    x_in, g_in, noise, lengths, rewards, groups, wq, wk, wv, wo,
    dq_out, dk_out, dv_out, do_out,
    X, H, G, Q0, Q1, FX, FH, FG, FQ, W, WO, D, E, DH, EH, ROWS, INV, PROBS, HG, GIN, *rest,
):
    scatter_bufs, (fs, fr, zs, zr, ss, sr, ls) = rest[:28], rest[28:]
    rs_bufs = {
        phase: scatter_bufs[7 * i : 7 * i + 7]
        for i, phase in enumerate((RS_QKV0, RS_QKV1, RS_HEAD1, RS_HEAD0))
    }
    core, f, t = lax.axis_index("pp"), lax.axis_index("fsdp"), lax.axis_index("tp")
    far = 1 - core
    y, x = f >> 2, f & 3
    j, g = x >> 1, x & 1
    q_wide = wq.shape[2] // 2
    k_wide = wk.shape[2] // 2
    cols = q_wide + 2 * k_wide
    wide = cols + LANES
    group = q_wide // HEAD_WIDTH
    scale = HEAD_WIDTH**-0.5

    def span(which, stride, width, at=0):
        return pl.ds(pl.multiple_of(which * stride + at, LANES), width)

    def other(mine, k):
        return (mine + k) & (SIDE - 1)

    def remote(src, dst, send, recv, **at):
        return pltpu.make_async_remote_copy(
            src_ref=src, dst_ref=dst, send_sem=send, recv_sem=recv,
            device_id=at, device_id_type=MESH,
        )

    cuts = [
        (w, gg * width, gg, at, width)
        for gg in (0, 1)
        for w, at, width in ((wq, 0, q_wide), (wk, q_wide, k_wide), (wv, q_wide + k_wide, k_wide))
    ]
    loads = [pltpu.make_async_copy(x_in.at[core], X.at[0, :, t], ls.at[0])] + [
        pltpu.make_async_copy(
            w.at[0, :, pl.ds(at, width)], W.at[core, gg, :, pl.ds(to, width)], ls.at[1 + i]
        )
        for i, (w, at, gg, to, width) in enumerate(cuts)
    ]
    loads += [
        pltpu.make_async_copy(wo.at[0], WO.at[core], ls.at[7]),
        pltpu.make_async_copy(g_in.at[core], GIN, ls.at[8]),
    ]
    for c in loads:
        c.start()

    barrier = pltpu.get_barrier_semaphore()
    for k in (1, 2, 3):
        for at in (
            {"fsdp": y * SIDE + other(x, k)},
            {"fsdp": other(y, k) * SIDE + x},
            {"pp": far, "fsdp": y * SIDE + other(x, k)},
            {"pp": far, "fsdp": other(y, k) * SIDE + x},
            {"tp": other(t, k)},
        ):
            pl.semaphore_signal(barrier, inc=1, device_id=at, device_id_type=MESH)
    pl.semaphore_signal(barrier, inc=1, device_id={"pp": far}, device_id_type=MESH)
    pl.semaphore_wait(barrier, 16)

    def z_gather(phase, buf, h, i):
        ref = buf.at[h, t, i]
        for k in PEERS:
            remote(ref, ref, zs.at[phase, h, i], zr.at[phase, h, i], tp=other(t, k)).start()

    def z_scatter(phase, send, recv, h, i):
        for k in PEERS:
            b = other(t, k)
            remote(
                send.at[h, b, i], recv.at[h, t, i], zs.at[phase, h, i], zr.at[phase, h, i], tp=b
            ).start()

    def z_all(phase, buf, h, i):
        three = buf.at[h, pl.ds(0, SIDE - 1), i]
        return remote(three, three, zs.at[phase, h, i], zr.at[phase, h, i], tp=t)

    def z_wait(phase, buf, h):
        for i in (0, 1):
            z_all(phase, buf, h, i).wait_recv()

    def z_sum(phase, send, recv, h, i, total):
        z_all(phase, recv, h, i).wait_recv()
        total = total + send[h, t, i].astype(jnp.float32)
        for k in PEERS:
            total = total + recv[h, other(t, k), i].astype(jnp.float32)
        return total.astype(jnp.bfloat16)

    def push(phase, h, kind, src, dst, **at):
        remote(src, dst, fs.at[phase, h, kind], fr.at[phase, h, kind], **at).start()

    def f_all(phase, h, kind):
        S, RA, RB, UA, UB, VA, VB = rs_bufs[
            {AG_HEAD0: RS_HEAD0, AG_HEAD1: RS_HEAD0, AG_GRAD0: RS_QKV0, AG_GRAD1: RS_QKV0}.get(phase, phase)
        ]
        order = (RA, RB, VA, VB) if phase < AG_HEAD0 else (VA, VB, RA, RB)
        if phase == AG_GRAD0:
            order = (VB, VB, RB, RB)
        three = order[kind].at[h, pl.ds(0, SIDE - 1)]
        return remote(three, three, fs.at[phase, h, kind], fr.at[phase, h, kind], fsdp=f)

    def widths(buf_cols):
        return (wide, cols) if buf_cols == 2 * wide else (buf_cols // 2, buf_cols // 2)

    def rs_start(phase, h):
        S, RA, RB, UA, UB, VA, VB = rs_bufs[phase]
        ca, cb = widths(S.shape[-1])
        for k in PEERS:
            y2, x2 = other(y, k), other(x, k)
            push(phase, h, 0, S.at[h, y2, :, 0], RA.at[h, y], fsdp=y2 * SIDE + x)
            push(
                phase, h, 1, S.at[h, :, x2 >> 1, 1, :, span(x2 & 1, ca, cb)], RB.at[h, x], fsdp=y * SIDE + x2
            )

    def rs_mid(phase, h):
        S, RA, RB, UA, UB, VA, VB = rs_bufs[phase]
        ca, cb = widths(S.shape[-1])
        f_all(phase, h, 0).wait_recv()
        total = S[h, y, :, 0].astype(jnp.float32)
        for k in PEERS:
            total = total + RA[h, other(y, k)].astype(jnp.float32)
        UA[h] = total.astype(jnp.bfloat16)
        for k in PEERS:
            x2 = other(x, k)
            push(
                phase, h, 2, UA.at[h, x2 >> 1, :, span(x2 & 1, ca, ca)], VA.at[h, x], fsdp=y * SIDE + x2
            )
        f_all(phase, h, 1).wait_recv()
        total = S[h, :, j, 1, :, span(g, ca, cb)].astype(jnp.float32)
        for k in PEERS:
            total = total + RB[h, other(x, k)].astype(jnp.float32)
        UB[h] = total.astype(jnp.bfloat16)
        for k in PEERS:
            y2 = other(y, k)
            push(phase, h, 3, UB.at[h, y2], VB.at[h, y], fsdp=y2 * SIDE + x)

    def rs_end(phase, h):
        S, RA, RB, UA, UB, VA, VB = rs_bufs[phase]
        ca, cb = widths(S.shape[-1])
        f_all(phase, h, 2).wait_recv()
        first = UA[h, j, :, span(g, ca, ca)].astype(jnp.float32)
        for k in PEERS:
            first = first + VA[h, other(x, k)].astype(jnp.float32)
        f_all(phase, h, 3).wait_recv()
        second = UB[h, y].astype(jnp.float32)
        for k in PEERS:
            second = second + VB[h, other(y, k)].astype(jnp.float32)
        return first, second

    def ag_start(phase, buf, h):
        ca, cb = widths(buf.shape[-1])
        first = buf.at[h, y, j, 0, :, span(g, ca, ca)]
        second = buf.at[h, y, j, 1, :, span(g, ca, cb)]
        for k in PEERS:
            push(phase, h, 0, first, first, fsdp=y * SIDE + other(x, k))
            push(phase, h, 1, second, second, fsdp=other(y, k) * SIDE + x)

    def ag_mid(phase, buf, h):
        ca, cb = widths(buf.shape[-1])
        first = buf.at[h, y, :, 0]
        f_all(phase, h, 0).wait_recv()
        for k in PEERS:
            push(phase, h, 2, first, first, fsdp=other(y, k) * SIDE + x)
        second = buf.at[h, :, j, 1, :, span(g, ca, cb)]
        f_all(phase, h, 1).wait_recv()
        for k in PEERS:
            push(phase, h, 3, second, second, fsdp=y * SIDE + other(x, k))

    def last_mid(h):
        first, second = Q0.at[h, y, :, 0], Q0.at[h, :, j, 1, :, span(g, cols, cols)]
        first_far, second_far = FQ.at[h, y, :, 0], FQ.at[h, :, j, 1, :, span(g, cols, cols)]
        f_all(AG_GRAD0, h, 0).wait_recv()

        @pl.when(core == 0)
        def _():
            for k in PEERS:
                push(AG_GRAD0, h, 2, first, first, fsdp=other(y, k) * SIDE + x)

        @pl.when(core == 1)
        def _():
            for k in PEERS + (0,):
                push(AG_FAR0, h, 2, first, first_far, pp=far, fsdp=other(y, k) * SIDE + x)

        f_all(AG_GRAD0, h, 1).wait_recv()

        @pl.when(core == 0)
        def _():
            for k in PEERS:
                push(AG_GRAD0, h, 3, second, second, fsdp=y * SIDE + other(x, k))

        @pl.when(core == 1)
        def _():
            for k in PEERS + (0,):
                push(AG_FAR0, h, 3, second, second_far, pp=far, fsdp=y * SIDE + other(x, k))

    def far_all(h, kind):
        four = rs_bufs[RS_QKV0][2].at[h]
        return remote(four, four, fs.at[AG_FAR0, h, kind], fr.at[AG_FAR0, h, kind], fsdp=f)

    def ag_end(phase, h):
        f_all(phase, h, 2).wait_recv()
        f_all(phase, h, 3).wait_recv()

    def flat(value):
        return value.reshape(-1, value.shape[-1])

    def project(layer, gathered, phase, h):
        S = rs_bufs[phase][0]
        z_wait(gathered, X.at[layer], h)
        rows = flat(X[layer, h])
        for gg in (0, 1):
            S[h, :, :, :, :, pl.ds(gg * wide, cols)] = (
                dot(rows, W[layer, gg], NN).astype(jnp.bfloat16).reshape(SIDE, 2, 2, SUB, cols)
            )
        squares = []
        for a in (0, 1):
            part = X[layer, h, :, :, a].astype(jnp.float32)
            squares.append(jnp.sum(part * part, -1, keepdims=True))
        tile = split_tile(*squares)
        for gg in (0, 1):
            S[h, :, :, 0, :, pl.ds(gg * wide + cols, LANES)] = tile
        rs_start(phase, h)

    def attend(layer, phase, h):
        first, second = rs_end(phase, h)
        squares = jnp.concatenate(join_tile(first[:, cols:]), 0)
        inv_rms = lax.rsqrt(squares / MODEL_WIDTH + epsilon)
        rows = (jnp.concatenate([first[:, :cols], second], 0) * inv_rms).astype(jnp.bfloat16)
        ROWS[layer, h] = rows
        INV[layer, h] = jnp.broadcast_to(inv_rms, (SLOT, LANES))
        queries = jnp.concatenate([rows[:, i * HEAD_WIDTH : (i + 1) * HEAD_WIDTH] for i in range(group)], 0)
        keys, values = rows[:, q_wide : q_wide + k_wide], rows[:, q_wide + k_wide :]
        scores = dot(queries, keys, NT) * scale
        cut = lengths[core, 0, y * SIDE + 2 * h + j]
        later = [
            ((lax.broadcasted_iota(jnp.int32, scores.shape, d) & (SLOT - 1)) >= cut).astype(jnp.int32)
            for d in (0, 1)
        ]
        scores = jnp.where(later[0] == later[1], scores, masked_score)
        raised = jnp.exp(scores - jnp.max(scores, -1, keepdims=True))
        probs = raised / jnp.sum(raised, -1, keepdims=True)
        PROBS[layer, h] = probs
        mixed = dot(probs.astype(jnp.bfloat16), values, NN).astype(jnp.bfloat16)
        for i in range(group):
            H[layer, h, y, j, :, :, span(g, q_wide, HEAD_WIDTH, i * HEAD_WIDTH)] = mixed[
                i * SLOT : (i + 1) * SLOT
            ].reshape(2, SUB, HEAD_WIDTH)

    def head_end(phase, h):
        first, second = rs_end(phase, h)
        HG[h] = jnp.concatenate([first, second], 0).astype(jnp.bfloat16)

    def attend_back(layer, h):
        Q, stride = ((Q0, cols), (Q1, wide))[layer]
        rows, head_grad, inv_rms, probs = ROWS[layer, h], HG[h], INV[layer, h], PROBS[layer, h]

        def stacked(value):
            return jnp.concatenate(
                [value[:, i * HEAD_WIDTH : (i + 1) * HEAD_WIDTH] for i in range(group)], 0
            )

        queries, grads = stacked(rows), stacked(head_grad)
        keys, values = rows[:, q_wide : q_wide + k_wide], rows[:, q_wide + k_wide :]
        prob_grad = dot(grads, values, NT)
        value_grad = dot(probs.astype(jnp.bfloat16), grads, TN)
        score_grad = probs * (prob_grad - jnp.sum(prob_grad * probs, -1, keepdims=True))
        score_grad = score_grad.astype(jnp.bfloat16)
        query_grad = dot(score_grad, keys, NN) * scale
        key_grad = dot(score_grad, queries, TN) * scale
        total = jnp.zeros((SLOT, LANES), jnp.float32)
        parts = [query_grad[i * SLOT : (i + 1) * SLOT] for i in range(group)] + [key_grad, value_grad]
        for i, part in enumerate(parts):
            part = part.astype(jnp.bfloat16).astype(jnp.float32)
            total = total + part * rows[:, i * HEAD_WIDTH : (i + 1) * HEAD_WIDTH].astype(jnp.float32)
            Q[h, y, j, :, :, span(g, stride, HEAD_WIDTH, i * HEAD_WIDTH)] = (
                (part * inv_rms).astype(jnp.bfloat16).reshape(2, SUB, HEAD_WIDTH)
            )
        if layer > 0:
            share = inv_rms[:, :1] * inv_rms[:, :1] * jnp.sum(total, -1, keepdims=True) / MODEL_WIDTH
            Q[h, y, j, 0, :, span(g, wide, LANES, cols)] = split_tile(share[:SUB], share[SUB:])

    def head_grads(layer, gathered, phase, h):
        S = rs_bufs[phase][0]
        z_wait(gathered, G.at[layer], h)
        S[h] = dot(flat(G[layer, h]), WO[layer], NT).astype(jnp.bfloat16).reshape(S.shape[1:])
        rs_start(phase, h)

    def project_out(h):
        ag_end(AG_HEAD0, h)
        D[h] = dot(flat(H[0, h]), WO[0], NN).astype(jnp.bfloat16).reshape(D.shape[1:])
        for i in (0, 1):
            z_scatter(RS_OUT0, D, E, h, i)

    def project_back(h):
        ag_end(AG_GRAD1, h)
        back = sum(
            dot(flat(Q1[h, :, :, :, :, pl.ds(gg * wide, cols)]), W[1, gg], NT) for gg in (0, 1)
        ).reshape(DH.shape[1:])
        tiles = [
            Q1[h, :, :, 0, :, pl.ds(gg * wide + cols, LANES)].astype(jnp.float32) for gg in (0, 1)
        ]
        shares = join_tile(tiles[0] + tiles[1])
        for a in (0, 1):
            term = back[:, :, a] - X[1, h, :, :, a].astype(jnp.float32) * shares[a]
            DH[h, :, :, a] = term.astype(jnp.bfloat16)
        for i in (0, 1):
            z_scatter(RS_IN1, DH, EH, h, i)

    def hand_over(i, src, dst):
        return remote(src, dst, ss.at[i], sr.at[i], pp=far)

    x_far, h_far, g_far = hand_over(7, X.at[far], FX), hand_over(8, H.at[far], FH), hand_over(9, G.at[far], FG)
    q_far = [
        hand_over(
            10 + gg, Q1.at[:, :, :, :, :, pl.ds(gg * wide, cols)], FQ.at[:, :, :, :, :, pl.ds(gg * cols, cols)]
        )
        for gg in (0, 1)
    ]
    def weight_grads(layer, h):
        Q, stride = ((Q0, cols), (Q1, wide))[layer]
        rows, far_rows = flat(X[layer, h]), flat(FX[h])
        for gg in (0, 1):
            term = dot(rows, flat(Q[h, :, :, :, :, pl.ds(gg * stride, cols)]), TN) + dot(
                far_rows, flat(FQ[h, :, :, :, :, pl.ds(gg * cols, cols)]), TN
            )
            for to, width, out in (
                (0, q_wide, dq_out), (q_wide, k_wide, dk_out), (q_wide + k_wide, k_wide, dv_out)
            ):
                to_at = pl.ds(gg * width, width)
                part = term[:, to : to + width]
                out[0, :, to_at] = part if h == 0 else out[0, :, to_at] + part

    loads[0].wait()
    for h in HALVES:
        for i in (0, 1):
            z_gather(AG_STREAM0, X.at[0], h, i)
    swaps = [
        remote(
            w.at[0, :, pl.ds(at, width)], W.at[core, gg, :, pl.ds(to, width)], ss.at[i], sr.at[i], pp=far
        )
        for i, (w, at, gg, to, width) in enumerate(cuts)
    ] + [remote(wo.at[0], WO.at[core], ss.at[6], sr.at[6], pp=far)]
    for c in swaps[:6]:
        c.start()
    for c in loads[1:8]:
        c.wait()
    for c in swaps[:6]:
        c.wait_recv()
    for h in HALVES:
        project(0, AG_STREAM0, RS_QKV0, h)
    swaps[6].start()
    loads[8].wait()
    top = token_weights(lengths, rewards, groups, noise, core, t)
    top = (-top * flat(GIN[...]).astype(jnp.float32)).astype(jnp.bfloat16)
    G[1, :, t] = top.reshape(GIN.shape)
    for h in HALVES:
        for i in (0, 1):
            z_gather(AG_TOP, G.at[1], h, i)
    for h in HALVES:
        rs_mid(RS_QKV0, h)
    for h in HALVES:
        attend(0, RS_QKV0, h)
        ag_start(AG_HEAD0, H.at[0], h)
    for h in HALVES:
        ag_mid(AG_HEAD0, H.at[0], h)
    swaps[6].wait_recv()
    for h in HALVES:
        project_out(h)
    for h in HALVES:
        head_grads(1, AG_TOP, RS_HEAD1, h)
    for h in HALVES:
        for i in (0, 1):
            X[1, h, t, i] = z_sum(RS_OUT0, D, E, h, i, X[0, h, t, i].astype(jnp.float32))
            z_gather(AG_STREAM1, X.at[1], h, i)
    for h in HALVES:
        rs_mid(RS_HEAD1, h)
    for h in HALVES:
        project(1, AG_STREAM1, RS_QKV1, h)
    x_far.start()
    for h in HALVES:
        head_end(RS_HEAD1, h)
    for h in HALVES:
        rs_mid(RS_QKV1, h)
    for h in HALVES:
        attend(1, RS_QKV1, h)
        attend_back(1, h)
        ag_start(AG_GRAD1, Q1, h)
    for h in HALVES:
        ag_mid(AG_GRAD1, Q1, h)
    for h in HALVES:
        project_back(h)

    @pl.when(core == 0)
    def _():
        for c in q_far:
            c.start()

    for h in HALVES:
        ag_start(AG_HEAD1, H.at[1], h)
    for h in HALVES:
        for i in (0, 1):
            G[0, h, t, i] = z_sum(RS_IN1, DH, EH, h, i, G[1, h, t, i].astype(jnp.float32))
            z_gather(AG_OUT0, G.at[0], h, i)
    for h in HALVES:
        ag_mid(AG_HEAD1, H.at[1], h)
    for h in HALVES:
        head_grads(0, AG_OUT0, RS_HEAD0, h)
    g_far.start()
    for h in HALVES:
        ag_end(AG_HEAD1, h)
    h_far.start()
    do_out[0] = dot(flat(H[core]), flat(G[core]), TN)
    for h in HALVES:
        rs_mid(RS_HEAD0, h)
    for h in HALVES:
        head_end(RS_HEAD0, h)
        attend_back(0, h)
        ag_start(AG_GRAD0, Q0, h)
    for h in HALVES:
        last_mid(h)
    for c in (x_far, h_far, g_far):
        c.wait_recv()
    do_out[0] += dot(flat(FH[...]), flat(FG[...]), TN)
    @pl.when(core == 0)
    def _():
        for h in HALVES:
            ag_end(AG_GRAD0, h)
            far_all(h, 2).wait_recv()
            far_all(h, 3).wait_recv()
            weight_grads(0, h)

    @pl.when(core == 1)
    def _():
        for c in q_far:
            c.wait_recv()
        for h in HALVES:
            weight_grads(1, h)

    for phase in range(AG_GRAD0):
        for h in HALVES:
            for kind in range(4):
                f_all(phase, h, kind).wait_send()
    for h in HALVES:
        for kind in (0, 1):
            f_all(AG_GRAD0, h, kind).wait_send()

        @pl.when(core == 0)
        def _():
            for kind in (2, 3):
                f_all(AG_GRAD0, h, kind).wait_send()

        @pl.when(core == 1)
        def _():
            for kind in (2, 3):
                far_all(h, kind).wait_send()

    for phase, buf in (
        (AG_STREAM0, X.at[0]), (AG_TOP, G.at[1]), (RS_OUT0, E),
        (AG_STREAM1, X.at[1]), (RS_IN1, EH), (AG_OUT0, G.at[0]),
    ):
        for h in HALVES:
            for i in (0, 1):
                z_all(phase, buf, h, i).wait_send()
    for c in swaps + [x_far, h_far, g_far]:
        c.wait_send()

    @pl.when(core == 0)
    def _():
        for c in q_far:
            c.wait_send()


def write_out(*refs):
    *pairs, sems = refs
    count = len(pairs) // 2
    copies = [
        pltpu.make_async_copy(src, dst, sems.at[i])
        for i, (src, dst) in enumerate(zip(pairs[:count], pairs[count:]))
    ]
    for c in copies:
        c.start()
    for c in copies:
        c.wait()


def local(
    inputs,
    head_grad,
    noise_mask,
    lengths,
    rewards,
    groups,
    query_weight,
    key_weight,
    value_weight,
    out_weight,
):
    row_count, width = inputs.shape[1:]
    q_wide, k_wide = query_weight.shape[2] // 2, key_weight.shape[2] // 2
    cols = q_wide + 2 * k_wide
    wide = cols + LANES
    group = q_wide // k_wide

    bf16, f32 = jnp.bfloat16, jnp.float32
    any_space = pl.BlockSpec(memory_space=pl.ANY)
    rows = (2, SIDE, 2, 2, SUB)

    def scatter_bufs(ca, cb):
        return [
            pltpu.VMEM(shape, bf16)
            for shape in (
                rows + (2 * ca,),
                (2, SIDE, 2, SUB, 2 * ca),
                (2, SIDE, SIDE, SUB, cb),
                (2, 2, SUB, 2 * ca),
                (2, SIDE, SUB, cb),
                (2, SIDE, SUB, ca),
                (2, SIDE, SUB, cb),
            )
        ]

    results = pl.pallas_call(
        kernel,
        out_shape=[
            pltpu.VMEM(w.shape, f32)
            for w in (query_weight, key_weight, value_weight, out_weight)
        ],
        in_specs=[any_space, any_space, pl.BlockSpec(memory_space=pltpu.VMEM)]
        + [pl.BlockSpec(memory_space=pltpu.SMEM)] * 3
        + [any_space] * 4,
        out_specs=[pl.BlockSpec(memory_space=pltpu.VMEM)] * 4,
        scratch_shapes=[
            pltpu.VMEM((2,) + rows + (width,), bf16),
            pltpu.VMEM((2,) + rows + (2 * q_wide,), bf16),
            pltpu.VMEM((2,) + rows + (width,), bf16),
            pltpu.VMEM(rows + (2 * cols,), bf16),
            pltpu.VMEM(rows + (2 * wide,), bf16),
            pltpu.VMEM(rows + (width,), bf16),
            pltpu.VMEM(rows + (2 * q_wide,), bf16),
            pltpu.VMEM(rows + (width,), bf16),
            pltpu.VMEM(rows + (2 * cols,), bf16),
            pltpu.VMEM((2, 2, width, cols), bf16),
            pltpu.VMEM((2, 2 * q_wide, width), bf16),
            pltpu.VMEM(rows + (width,), bf16),
            pltpu.VMEM(rows + (width,), bf16),
            pltpu.VMEM(rows + (width,), bf16),
            pltpu.VMEM(rows + (width,), bf16),
            pltpu.VMEM((2, 2, SLOT, cols), bf16),
            pltpu.VMEM((2, 2, SLOT, LANES), f32),
            pltpu.VMEM((2, 2, group * SLOT, SLOT), f32),
            pltpu.VMEM((2, SLOT, q_wide), bf16),
            pltpu.VMEM((2, 2, 2, SUB, width), bf16),
        ]
        + scatter_bufs(wide, cols) * 2
        + scatter_bufs(q_wide, q_wide) * 2
        + [
            pltpu.SemaphoreType.DMA((9, 2, 4)),
            pltpu.SemaphoreType.DMA((9, 2, 4)),
            pltpu.SemaphoreType.DMA((6, 2, 2)),
            pltpu.SemaphoreType.DMA((6, 2, 2)),
            pltpu.SemaphoreType.DMA((12,)),
            pltpu.SemaphoreType.DMA((12,)),
            pltpu.SemaphoreType.DMA((9,)),
        ],
        compiler_params=pltpu.CompilerParams(
            collective_id=0, has_side_effects=True, vmem_limit_bytes=56 * 1024 * 1024
        ),
    )(
        inputs.reshape(2, 2, 2, 2, SUB, width),
        head_grad.reshape(2, 2, 2, 2, SUB, width),
        noise_mask,
        *(jnp.swapaxes(v, 1, 2) for v in (lengths, rewards, groups)),
        query_weight,
        key_weight,
        value_weight,
        out_weight,
    )
    return pl.pallas_call(
        write_out,
        out_shape=[jax.ShapeDtypeStruct(r.shape, r.dtype) for r in results],
        in_specs=[any_space] * 4,
        out_specs=[any_space] * 4,
        scratch_shapes=[pltpu.SemaphoreType.DMA((4,))],
        compiler_params=pltpu.CompilerParams(vmem_limit_bytes=1024 * 1024),
    )(*results)


def solution(mesh):
    return jax.shard_map(
        local,
        mesh=mesh,
        in_specs=(
            P(None, "tp", "fsdp"),
            P(None, "tp", "fsdp"),
            P(None, "tp"),
            P(),
            P(),
            P(),
            P("pp", "fsdp", "tp"),
            P("pp", "fsdp", "tp"),
            P("pp", "fsdp", "tp"),
            P("pp", "tp", "fsdp"),
        ),
        out_specs=(
            P("pp", "fsdp", "tp"),
            P("pp", "fsdp", "tp"),
            P("pp", "fsdp", "tp"),
            P("pp", "tp", "fsdp"),
        ),
        check_vma=False,
    )
```

```python
import jax
import jax.numpy as jnp
from jax import lax
from jax.experimental import pallas as pl
from jax.experimental.pallas import tpu as pltpu
from jax.sharding import PartitionSpec as P

MODEL_WIDTH = 8192
HEAD_WIDTH = 128
SLOT = 32
LANES = 128

epsilon = 1e-06
masked_score = -1e30
MESH = pl.DeviceIdType.MESH
NN = ((1,), (0,))
NT = ((1,), (1,))
TN = ((0,), (0,))


def dot(a, b, contract):
    return lax.dot_general(a, b, (contract, ((), ())), preferred_element_type=jnp.float32)


RS_QKV0, RS_QKV1, RS_HEAD1, RS_HEAD0, AG_HEAD0, AG_GRAD1, AG_HEAD1, AG_GRAD0, AG_FAR0 = range(9)
AG_STREAM0, AG_TOP, RS_OUT0, AG_STREAM1, RS_IN1, AG_OUT0 = range(6)
HALVES = (0, 1)
PEERS = (2, 1, 3)
SIDE = 4
SUB = 16


def split_tile(first, second):
    lane = lax.broadcasted_iota(jnp.int32, first.shape[:-1] + (LANES,), first.ndim - 1)
    tile = jnp.zeros(lane.shape, jnp.float32)
    for i, column in enumerate((first, second)):
        high = column.astype(jnp.bfloat16).astype(jnp.float32)
        tile = jnp.where(lane == 2 * i, high, jnp.where(lane == 2 * i + 1, column - high, tile))
    return tile.astype(jnp.bfloat16)


def join_tile(tile):
    tile = tile.astype(jnp.float32)
    return tile[..., 0:1] + tile[..., 1:2], tile[..., 2:3] + tile[..., 3:4]


def token_weights(lengths, rewards, groups, noise, core, t):
    square = (LANES, LANES)
    micros, packed, slots = lengths.shape
    lane = lax.broadcasted_iota(jnp.int32, (1, LANES), 1)

    def row(ref):
        value = jnp.full((1, LANES), -1, jnp.int32)
        for m in range(micros):
            for s in range(slots):
                for c in range(packed):
                    value = jnp.where(lane == (m * slots + s) * packed + c, ref[m, c, s], value)
        return jnp.broadcast_to(value.astype(jnp.float32), square)

    group_row, reward_row, length_row = row(groups), row(rewards), row(lengths)
    member = (group_row == group_row.T).astype(jnp.float32)
    reward_column = reward_row.T
    count = jnp.sum(member, 0, keepdims=True)
    mean = jnp.sum(member * reward_column, 0, keepdims=True) / count
    centered = reward_column - mean
    variance = jnp.sum(member * centered * centered, 0, keepdims=True) / count
    advantage = (reward_row - mean) / jnp.maximum(jnp.sqrt(variance), 1.0)
    token = lax.broadcasted_iota(jnp.int32, square, 0)
    lanes = lax.broadcasted_iota(jnp.int32, square, 1)
    first = core * slots * packed + (t * (LANES // SLOT) + (token >> 5)) * packed
    length = jnp.sum(jnp.where(lanes == first, length_row, 0.0), -1, keepdims=True)
    position = (token & (SLOT - 1)).astype(jnp.float32)
    chosen = lanes == first + (position >= length).astype(jnp.int32)
    advantage = jnp.sum(jnp.where(chosen, advantage, 0.0), -1, keepdims=True)
    length = jnp.sum(jnp.where(chosen, length_row, 0.0), -1, keepdims=True)
    noise = jnp.broadcast_to(noise[pl.ds(core, 1), :].astype(jnp.float32), square).T
    return advantage * SLOT / length * noise[:, :1]


def kernel(
    x_in, g_in, noise, lengths, rewards, groups, wq, wk, wv, wo,
    dq_out, dk_out, dv_out, do_out,
    X, H, G, Q0, Q1, FX, FH, FG, FQ, W, WO, D, E, DH, EH, ROWS, INV, PROBS, HG, GIN, *rest,
):
    scatter_bufs, (fs, fr, zs, zr, ss, sr, ls) = rest[:28], rest[28:]
    rs_bufs = {
        phase: scatter_bufs[7 * i : 7 * i + 7]
        for i, phase in enumerate((RS_QKV0, RS_QKV1, RS_HEAD1, RS_HEAD0))
    }
    core, f, t = lax.axis_index("pp"), lax.axis_index("fsdp"), lax.axis_index("tp")
    far = 1 - core
    y, x = f >> 2, f & 3
    j, g = x >> 1, x & 1
    q_wide = wq.shape[2] // 2
    k_wide = wk.shape[2] // 2
    cols = q_wide + 2 * k_wide
    wide = cols + LANES
    group = q_wide // HEAD_WIDTH
    scale = HEAD_WIDTH**-0.5

    def span(which, stride, width, at=0):
        return pl.ds(pl.multiple_of(which * stride + at, LANES), width)

    def other(mine, k):
        return (mine + k) & (SIDE - 1)

    def remote(src, dst, send, recv, **at):
        return pltpu.make_async_remote_copy(
            src_ref=src, dst_ref=dst, send_sem=send, recv_sem=recv,
            device_id=at, device_id_type=MESH,
        )

    cuts = [
        (w, gg * width, gg, at, width)
        for gg in (0, 1)
        for w, at, width in ((wq, 0, q_wide), (wk, q_wide, k_wide), (wv, q_wide + k_wide, k_wide))
    ]
    loads = [pltpu.make_async_copy(x_in.at[core], X.at[0, :, t], ls.at[0])] + [
        pltpu.make_async_copy(
            w.at[0, :, pl.ds(at, width)], W.at[core, gg, :, pl.ds(to, width)], ls.at[1 + i]
        )
        for i, (w, at, gg, to, width) in enumerate(cuts)
    ]
    loads += [
        pltpu.make_async_copy(wo.at[0], WO.at[core], ls.at[7]),
        pltpu.make_async_copy(g_in.at[core], GIN, ls.at[8]),
    ]
    for c in loads:
        c.start()

    barrier = pltpu.get_barrier_semaphore()
    for k in (1, 2, 3):
        for at in (
            {"fsdp": y * SIDE + other(x, k)},
            {"fsdp": other(y, k) * SIDE + x},
            {"pp": far, "fsdp": y * SIDE + other(x, k)},
            {"pp": far, "fsdp": other(y, k) * SIDE + x},
            {"tp": other(t, k)},
        ):
            pl.semaphore_signal(barrier, inc=1, device_id=at, device_id_type=MESH)
    pl.semaphore_signal(barrier, inc=1, device_id={"pp": far}, device_id_type=MESH)
    pl.semaphore_wait(barrier, 16)

    def z_gather(phase, buf, h, i):
        ref = buf.at[h, t, i]
        for k in PEERS:
            remote(ref, ref, zs.at[phase, h, i], zr.at[phase, h, i], tp=other(t, k)).start()

    def z_scatter(phase, send, recv, h, i):
        for k in PEERS:
            b = other(t, k)
            remote(
                send.at[h, b, i], recv.at[h, t, i], zs.at[phase, h, i], zr.at[phase, h, i], tp=b
            ).start()

    def z_all(phase, buf, h, i):
        three = buf.at[h, pl.ds(0, SIDE - 1), i]
        return remote(three, three, zs.at[phase, h, i], zr.at[phase, h, i], tp=t)

    def z_wait(phase, buf, h):
        for i in (0, 1):
            z_all(phase, buf, h, i).wait_recv()

    def z_sum(phase, send, recv, h, i, total):
        z_all(phase, recv, h, i).wait_recv()
        total = total + send[h, t, i].astype(jnp.float32)
        for k in PEERS:
            total = total + recv[h, other(t, k), i].astype(jnp.float32)
        return total.astype(jnp.bfloat16)

    def push(phase, h, kind, src, dst, **at):
        remote(src, dst, fs.at[phase, h, kind], fr.at[phase, h, kind], **at).start()

    def f_all(phase, h, kind):
        S, RA, RB, UA, UB, VA, VB = rs_bufs[
            {AG_HEAD0: RS_HEAD0, AG_HEAD1: RS_HEAD0, AG_GRAD0: RS_QKV0, AG_GRAD1: RS_QKV0}.get(phase, phase)
        ]
        order = (RA, RB, VA, VB) if phase < AG_HEAD0 else (VA, VB, RA, RB)
        if phase == AG_GRAD0:
            order = (VB, VB, RB, RB)
        three = order[kind].at[h, pl.ds(0, SIDE - 1)]
        return remote(three, three, fs.at[phase, h, kind], fr.at[phase, h, kind], fsdp=f)

    def widths(buf_cols):
        return (wide, cols) if buf_cols == 2 * wide else (buf_cols // 2, buf_cols // 2)

    def rs_start(phase, h):
        S, RA, RB, UA, UB, VA, VB = rs_bufs[phase]
        ca, cb = widths(S.shape[-1])
        for k in PEERS:
            y2, x2 = other(y, k), other(x, k)
            push(phase, h, 0, S.at[h, y2, :, 0], RA.at[h, y], fsdp=y2 * SIDE + x)
            push(
                phase, h, 1, S.at[h, :, x2 >> 1, 1, :, span(x2 & 1, ca, cb)], RB.at[h, x], fsdp=y * SIDE + x2
            )

    def rs_mid(phase, h):
        S, RA, RB, UA, UB, VA, VB = rs_bufs[phase]
        ca, cb = widths(S.shape[-1])
        f_all(phase, h, 0).wait_recv()
        total = S[h, y, :, 0].astype(jnp.float32)
        for k in PEERS:
            total = total + RA[h, other(y, k)].astype(jnp.float32)
        UA[h] = total.astype(jnp.bfloat16)
        for k in PEERS:
            x2 = other(x, k)
            push(
                phase, h, 2, UA.at[h, x2 >> 1, :, span(x2 & 1, ca, ca)], VA.at[h, x], fsdp=y * SIDE + x2
            )
        f_all(phase, h, 1).wait_recv()
        total = S[h, :, j, 1, :, span(g, ca, cb)].astype(jnp.float32)
        for k in PEERS:
            total = total + RB[h, other(x, k)].astype(jnp.float32)
        UB[h] = total.astype(jnp.bfloat16)
        for k in PEERS:
            y2 = other(y, k)
            push(phase, h, 3, UB.at[h, y2], VB.at[h, y], fsdp=y2 * SIDE + x)

    def rs_end(phase, h):
        S, RA, RB, UA, UB, VA, VB = rs_bufs[phase]
        ca, cb = widths(S.shape[-1])
        f_all(phase, h, 2).wait_recv()
        first = UA[h, j, :, span(g, ca, ca)].astype(jnp.float32)
        for k in PEERS:
            first = first + VA[h, other(x, k)].astype(jnp.float32)
        f_all(phase, h, 3).wait_recv()
        second = UB[h, y].astype(jnp.float32)
        for k in PEERS:
            second = second + VB[h, other(y, k)].astype(jnp.float32)
        return first, second

    def ag_start(phase, buf, h):
        ca, cb = widths(buf.shape[-1])
        first = buf.at[h, y, j, 0, :, span(g, ca, ca)]
        second = buf.at[h, y, j, 1, :, span(g, ca, cb)]
        for k in PEERS:
            push(phase, h, 0, first, first, fsdp=y * SIDE + other(x, k))
            push(phase, h, 1, second, second, fsdp=other(y, k) * SIDE + x)

    def ag_mid(phase, buf, h):
        ca, cb = widths(buf.shape[-1])
        first = buf.at[h, y, :, 0]
        f_all(phase, h, 0).wait_recv()
        for k in PEERS:
            push(phase, h, 2, first, first, fsdp=other(y, k) * SIDE + x)
        second = buf.at[h, :, j, 1, :, span(g, ca, cb)]
        f_all(phase, h, 1).wait_recv()
        for k in PEERS:
            push(phase, h, 3, second, second, fsdp=y * SIDE + other(x, k))

    def last_mid(h):
        first, second = Q0.at[h, y, :, 0], Q0.at[h, :, j, 1, :, span(g, cols, cols)]
        first_far, second_far = FQ.at[h, y, :, 0], FQ.at[h, :, j, 1, :, span(g, cols, cols)]
        f_all(AG_GRAD0, h, 0).wait_recv()

        @pl.when(core == 0)
        def _():
            for k in PEERS:
                push(AG_GRAD0, h, 2, first, first, fsdp=other(y, k) * SIDE + x)

        @pl.when(core == 1)
        def _():
            for k in PEERS + (0,):
                push(AG_FAR0, h, 2, first, first_far, pp=far, fsdp=other(y, k) * SIDE + x)

        f_all(AG_GRAD0, h, 1).wait_recv()

        @pl.when(core == 0)
        def _():
            for k in PEERS:
                push(AG_GRAD0, h, 3, second, second, fsdp=y * SIDE + other(x, k))

        @pl.when(core == 1)
        def _():
            for k in PEERS + (0,):
                push(AG_FAR0, h, 3, second, second_far, pp=far, fsdp=y * SIDE + other(x, k))

    def far_all(h, kind):
        four = rs_bufs[RS_QKV0][2].at[h]
        return remote(four, four, fs.at[AG_FAR0, h, kind], fr.at[AG_FAR0, h, kind], fsdp=f)

    def ag_end(phase, h):
        f_all(phase, h, 2).wait_recv()
        f_all(phase, h, 3).wait_recv()

    def flat(value):
        return value.reshape(-1, value.shape[-1])

    def project(layer, gathered, phase, h):
        S = rs_bufs[phase][0]
        z_wait(gathered, X.at[layer], h)
        rows = flat(X[layer, h])
        for gg in (0, 1):
            S[h, :, :, :, :, pl.ds(gg * wide, cols)] = (
                dot(rows, W[layer, gg], NN).astype(jnp.bfloat16).reshape(SIDE, 2, 2, SUB, cols)
            )
        squares = []
        for a in (0, 1):
            part = X[layer, h, :, :, a].astype(jnp.float32)
            squares.append(jnp.sum(part * part, -1, keepdims=True))
        tile = split_tile(*squares)
        for gg in (0, 1):
            S[h, :, :, 0, :, pl.ds(gg * wide + cols, LANES)] = tile
        rs_start(phase, h)

    def attend(layer, phase, h):
        first, second = rs_end(phase, h)
        squares = jnp.concatenate(join_tile(first[:, cols:]), 0)
        inv_rms = lax.rsqrt(squares / MODEL_WIDTH + epsilon)
        rows = (jnp.concatenate([first[:, :cols], second], 0) * inv_rms).astype(jnp.bfloat16)
        ROWS[layer, h] = rows
        INV[layer, h] = jnp.broadcast_to(inv_rms, (SLOT, LANES))
        queries = jnp.concatenate([rows[:, i * HEAD_WIDTH : (i + 1) * HEAD_WIDTH] for i in range(group)], 0)
        keys, values = rows[:, q_wide : q_wide + k_wide], rows[:, q_wide + k_wide :]
        scores = dot(queries, keys, NT) * scale
        cut = lengths[core, 0, y * SIDE + 2 * h + j]
        later = [
            ((lax.broadcasted_iota(jnp.int32, scores.shape, d) & (SLOT - 1)) >= cut).astype(jnp.int32)
            for d in (0, 1)
        ]
        scores = jnp.where(later[0] == later[1], scores, masked_score)
        raised = jnp.exp(scores - jnp.max(scores, -1, keepdims=True))
        probs = raised / jnp.sum(raised, -1, keepdims=True)
        PROBS[layer, h] = probs
        mixed = dot(probs.astype(jnp.bfloat16), values, NN).astype(jnp.bfloat16)
        for i in range(group):
            H[layer, h, y, j, :, :, span(g, q_wide, HEAD_WIDTH, i * HEAD_WIDTH)] = mixed[
                i * SLOT : (i + 1) * SLOT
            ].reshape(2, SUB, HEAD_WIDTH)

    def head_end(phase, h):
        first, second = rs_end(phase, h)
        HG[h] = jnp.concatenate([first, second], 0).astype(jnp.bfloat16)

    def attend_back(layer, h):
        Q, stride = ((Q0, cols), (Q1, wide))[layer]
        rows, head_grad, inv_rms, probs = ROWS[layer, h], HG[h], INV[layer, h], PROBS[layer, h]

        def stacked(value):
            return jnp.concatenate(
                [value[:, i * HEAD_WIDTH : (i + 1) * HEAD_WIDTH] for i in range(group)], 0
            )

        queries, grads = stacked(rows), stacked(head_grad)
        keys, values = rows[:, q_wide : q_wide + k_wide], rows[:, q_wide + k_wide :]
        prob_grad = dot(grads, values, NT)
        value_grad = dot(probs.astype(jnp.bfloat16), grads, TN)
        score_grad = probs * (prob_grad - jnp.sum(prob_grad * probs, -1, keepdims=True))
        score_grad = score_grad.astype(jnp.bfloat16)
        query_grad = dot(score_grad, keys, NN) * scale
        key_grad = dot(score_grad, queries, TN) * scale
        total = jnp.zeros((SLOT, LANES), jnp.float32)
        parts = [query_grad[i * SLOT : (i + 1) * SLOT] for i in range(group)] + [key_grad, value_grad]
        for i, part in enumerate(parts):
            part = part.astype(jnp.bfloat16).astype(jnp.float32)
            total = total + part * rows[:, i * HEAD_WIDTH : (i + 1) * HEAD_WIDTH].astype(jnp.float32)
            Q[h, y, j, :, :, span(g, stride, HEAD_WIDTH, i * HEAD_WIDTH)] = (
                (part * inv_rms).astype(jnp.bfloat16).reshape(2, SUB, HEAD_WIDTH)
            )
        if layer > 0:
            share = inv_rms[:, :1] * inv_rms[:, :1] * jnp.sum(total, -1, keepdims=True) / MODEL_WIDTH
            Q[h, y, j, 0, :, span(g, wide, LANES, cols)] = split_tile(share[:SUB], share[SUB:])

    def head_grads(layer, gathered, phase, h):
        S = rs_bufs[phase][0]
        z_wait(gathered, G.at[layer], h)
        S[h] = dot(flat(G[layer, h]), WO[layer], NT).astype(jnp.bfloat16).reshape(S.shape[1:])
        rs_start(phase, h)

    def project_out(h):
        ag_end(AG_HEAD0, h)
        D[h] = dot(flat(H[0, h]), WO[0], NN).astype(jnp.bfloat16).reshape(D.shape[1:])
        for i in (0, 1):
            z_scatter(RS_OUT0, D, E, h, i)

    def project_back(h):
        ag_end(AG_GRAD1, h)
        back = sum(
            dot(flat(Q1[h, :, :, :, :, pl.ds(gg * wide, cols)]), W[1, gg], NT) for gg in (0, 1)
        ).reshape(DH.shape[1:])
        tiles = [
            Q1[h, :, :, 0, :, pl.ds(gg * wide + cols, LANES)].astype(jnp.float32) for gg in (0, 1)
        ]
        shares = join_tile(tiles[0] + tiles[1])
        for a in (0, 1):
            term = back[:, :, a] - X[1, h, :, :, a].astype(jnp.float32) * shares[a]
            DH[h, :, :, a] = term.astype(jnp.bfloat16)
        for i in (0, 1):
            z_scatter(RS_IN1, DH, EH, h, i)

    def hand_over(i, src, dst):
        return remote(src, dst, ss.at[i], sr.at[i], pp=far)

    x_far, h_far, g_far = hand_over(7, X.at[far], FX), hand_over(8, H.at[far], FH), hand_over(9, G.at[far], FG)
    q_far = [
        hand_over(
            10 + gg, Q1.at[:, :, :, :, :, pl.ds(gg * wide, cols)], FQ.at[:, :, :, :, :, pl.ds(gg * cols, cols)]
        )
        for gg in (0, 1)
    ]
    def weight_grads(layer, h):
        Q, stride = ((Q0, cols), (Q1, wide))[layer]
        rows, far_rows = flat(X[layer, h]), flat(FX[h])
        for gg in (0, 1):
            term = dot(rows, flat(Q[h, :, :, :, :, pl.ds(gg * stride, cols)]), TN) + dot(
                far_rows, flat(FQ[h, :, :, :, :, pl.ds(gg * cols, cols)]), TN
            )
            for to, width, out in (
                (0, q_wide, dq_out), (q_wide, k_wide, dk_out), (q_wide + k_wide, k_wide, dv_out)
            ):
                to_at = pl.ds(gg * width, width)
                part = term[:, to : to + width]
                out[0, :, to_at] = part if h == 0 else out[0, :, to_at] + part

    loads[0].wait()
    for h in HALVES:
        for i in (0, 1):
            z_gather(AG_STREAM0, X.at[0], h, i)
    swaps = [
        remote(
            w.at[0, :, pl.ds(at, width)], W.at[core, gg, :, pl.ds(to, width)], ss.at[i], sr.at[i], pp=far
        )
        for i, (w, at, gg, to, width) in enumerate(cuts)
    ] + [remote(wo.at[0], WO.at[core], ss.at[6], sr.at[6], pp=far)]
    for c in swaps[:6]:
        c.start()
    for c in loads[1:8]:
        c.wait()
    for c in swaps[:6]:
        c.wait_recv()
    for h in HALVES:
        project(0, AG_STREAM0, RS_QKV0, h)
    swaps[6].start()
    loads[8].wait()
    top = token_weights(lengths, rewards, groups, noise, core, t)
    top = (-top * flat(GIN[...]).astype(jnp.float32)).astype(jnp.bfloat16)
    G[1, :, t] = top.reshape(GIN.shape)
    for h in HALVES:
        for i in (0, 1):
            z_gather(AG_TOP, G.at[1], h, i)
    for h in HALVES:
        rs_mid(RS_QKV0, h)
    for h in HALVES:
        attend(0, RS_QKV0, h)
        ag_start(AG_HEAD0, H.at[0], h)
    for h in HALVES:
        ag_mid(AG_HEAD0, H.at[0], h)
    swaps[6].wait_recv()
    for h in HALVES:
        head_grads(1, AG_TOP, RS_HEAD1, h)
    for h in HALVES:
        project_out(h)
    for h in HALVES:
        for i in (0, 1):
            X[1, h, t, i] = z_sum(RS_OUT0, D, E, h, i, X[0, h, t, i].astype(jnp.float32))
            z_gather(AG_STREAM1, X.at[1], h, i)
    for h in HALVES:
        rs_mid(RS_HEAD1, h)
    for h in HALVES:
        project(1, AG_STREAM1, RS_QKV1, h)
    x_far.start()
    for h in HALVES:
        head_end(RS_HEAD1, h)
    for h in HALVES:
        rs_mid(RS_QKV1, h)
    for h in HALVES:
        attend(1, RS_QKV1, h)
        attend_back(1, h)
        ag_start(AG_GRAD1, Q1, h)
    for h in HALVES:
        ag_mid(AG_GRAD1, Q1, h)
    for h in HALVES:
        project_back(h)

    @pl.when(core == 0)
    def _():
        for c in q_far:
            c.start()

    for h in HALVES:
        ag_start(AG_HEAD1, H.at[1], h)
    for h in HALVES:
        for i in (0, 1):
            G[0, h, t, i] = z_sum(RS_IN1, DH, EH, h, i, G[1, h, t, i].astype(jnp.float32))
            z_gather(AG_OUT0, G.at[0], h, i)
    for h in HALVES:
        ag_mid(AG_HEAD1, H.at[1], h)
    for h in HALVES:
        head_grads(0, AG_OUT0, RS_HEAD0, h)
    g_far.start()
    for h in HALVES:
        ag_end(AG_HEAD1, h)
    h_far.start()
    do_out[0] = dot(flat(H[core]), flat(G[core]), TN)
    for h in HALVES:
        rs_mid(RS_HEAD0, h)
    for h in HALVES:
        head_end(RS_HEAD0, h)
        attend_back(0, h)
        ag_start(AG_GRAD0, Q0, h)
    for h in HALVES:
        last_mid(h)
    for c in (x_far, h_far, g_far):
        c.wait_recv()
    do_out[0] += dot(flat(FH[...]), flat(FG[...]), TN)
    @pl.when(core == 0)
    def _():
        for h in HALVES:
            ag_end(AG_GRAD0, h)
            far_all(h, 2).wait_recv()
            far_all(h, 3).wait_recv()
            weight_grads(0, h)

    @pl.when(core == 1)
    def _():
        for c in q_far:
            c.wait_recv()
        for h in HALVES:
            weight_grads(1, h)

    for phase in range(AG_GRAD0):
        for h in HALVES:
            for kind in range(4):
                f_all(phase, h, kind).wait_send()
    for h in HALVES:
        for kind in (0, 1):
            f_all(AG_GRAD0, h, kind).wait_send()

        @pl.when(core == 0)
        def _():
            for kind in (2, 3):
                f_all(AG_GRAD0, h, kind).wait_send()

        @pl.when(core == 1)
        def _():
            for kind in (2, 3):
                far_all(h, kind).wait_send()

    for phase, buf in (
        (AG_STREAM0, X.at[0]), (AG_TOP, G.at[1]), (RS_OUT0, E),
        (AG_STREAM1, X.at[1]), (RS_IN1, EH), (AG_OUT0, G.at[0]),
    ):
        for h in HALVES:
            for i in (0, 1):
                z_all(phase, buf, h, i).wait_send()
    for c in swaps + [x_far, h_far, g_far]:
        c.wait_send()

    @pl.when(core == 0)
    def _():
        for c in q_far:
            c.wait_send()


def write_out(*refs):
    *pairs, sems = refs
    count = len(pairs) // 2
    copies = [
        pltpu.make_async_copy(src, dst, sems.at[i])
        for i, (src, dst) in enumerate(zip(pairs[:count], pairs[count:]))
    ]
    for c in copies:
        c.start()
    for c in copies:
        c.wait()


def local(
    inputs,
    head_grad,
    noise_mask,
    lengths,
    rewards,
    groups,
    query_weight,
    key_weight,
    value_weight,
    out_weight,
):
    row_count, width = inputs.shape[1:]
    q_wide, k_wide = query_weight.shape[2] // 2, key_weight.shape[2] // 2
    cols = q_wide + 2 * k_wide
    wide = cols + LANES
    group = q_wide // k_wide

    bf16, f32 = jnp.bfloat16, jnp.float32
    any_space = pl.BlockSpec(memory_space=pl.ANY)
    rows = (2, SIDE, 2, 2, SUB)

    def scatter_bufs(ca, cb):
        return [
            pltpu.VMEM(shape, bf16)
            for shape in (
                rows + (2 * ca,),
                (2, SIDE, 2, SUB, 2 * ca),
                (2, SIDE, SIDE, SUB, cb),
                (2, 2, SUB, 2 * ca),
                (2, SIDE, SUB, cb),
                (2, SIDE, SUB, ca),
                (2, SIDE, SUB, cb),
            )
        ]

    results = pl.pallas_call(
        kernel,
        out_shape=[
            pltpu.VMEM(w.shape, f32)
            for w in (query_weight, key_weight, value_weight, out_weight)
        ],
        in_specs=[any_space, any_space, pl.BlockSpec(memory_space=pltpu.VMEM)]
        + [pl.BlockSpec(memory_space=pltpu.SMEM)] * 3
        + [any_space] * 4,
        out_specs=[pl.BlockSpec(memory_space=pltpu.VMEM)] * 4,
        scratch_shapes=[
            pltpu.VMEM((2,) + rows + (width,), bf16),
            pltpu.VMEM((2,) + rows + (2 * q_wide,), bf16),
            pltpu.VMEM((2,) + rows + (width,), bf16),
            pltpu.VMEM(rows + (2 * cols,), bf16),
            pltpu.VMEM(rows + (2 * wide,), bf16),
            pltpu.VMEM(rows + (width,), bf16),
            pltpu.VMEM(rows + (2 * q_wide,), bf16),
            pltpu.VMEM(rows + (width,), bf16),
            pltpu.VMEM(rows + (2 * cols,), bf16),
            pltpu.VMEM((2, 2, width, cols), bf16),
            pltpu.VMEM((2, 2 * q_wide, width), bf16),
            pltpu.VMEM(rows + (width,), bf16),
            pltpu.VMEM(rows + (width,), bf16),
            pltpu.VMEM(rows + (width,), bf16),
            pltpu.VMEM(rows + (width,), bf16),
            pltpu.VMEM((2, 2, SLOT, cols), bf16),
            pltpu.VMEM((2, 2, SLOT, LANES), f32),
            pltpu.VMEM((2, 2, group * SLOT, SLOT), f32),
            pltpu.VMEM((2, SLOT, q_wide), bf16),
            pltpu.VMEM((2, 2, 2, SUB, width), bf16),
        ]
        + scatter_bufs(wide, cols) * 2
        + scatter_bufs(q_wide, q_wide) * 2
        + [
            pltpu.SemaphoreType.DMA((9, 2, 4)),
            pltpu.SemaphoreType.DMA((9, 2, 4)),
            pltpu.SemaphoreType.DMA((6, 2, 2)),
            pltpu.SemaphoreType.DMA((6, 2, 2)),
            pltpu.SemaphoreType.DMA((12,)),
            pltpu.SemaphoreType.DMA((12,)),
            pltpu.SemaphoreType.DMA((9,)),
        ],
        compiler_params=pltpu.CompilerParams(
            collective_id=0, has_side_effects=True, vmem_limit_bytes=56 * 1024 * 1024
        ),
    )(
        inputs.reshape(2, 2, 2, 2, SUB, width),
        head_grad.reshape(2, 2, 2, 2, SUB, width),
        noise_mask,
        *(jnp.swapaxes(v, 1, 2) for v in (lengths, rewards, groups)),
        query_weight,
        key_weight,
        value_weight,
        out_weight,
    )
    return pl.pallas_call(
        write_out,
        out_shape=[jax.ShapeDtypeStruct(r.shape, r.dtype) for r in results],
        in_specs=[any_space] * 4,
        out_specs=[any_space] * 4,
        scratch_shapes=[pltpu.SemaphoreType.DMA((4,))],
        compiler_params=pltpu.CompilerParams(vmem_limit_bytes=1024 * 1024),
    )(*results)


def solution(mesh):
    return jax.shard_map(
        local,
        mesh=mesh,
        in_specs=(
            P(None, "tp", "fsdp"),
            P(None, "tp", "fsdp"),
            P(None, "tp"),
            P(),
            P(),
            P(),
            P("pp", "fsdp", "tp"),
            P("pp", "fsdp", "tp"),
            P("pp", "fsdp", "tp"),
            P("pp", "tp", "fsdp"),
        ),
        out_specs=(
            P("pp", "fsdp", "tp"),
            P("pp", "fsdp", "tp"),
            P("pp", "fsdp", "tp"),
            P("pp", "tp", "fsdp"),
        ),
        check_vma=False,
    )
```

```python
import jax
import jax.numpy as jnp
from jax import lax
from jax.experimental import pallas as pl
from jax.experimental.pallas import tpu as pltpu
from jax.sharding import PartitionSpec as P

MODEL_WIDTH = 8192
HEAD_WIDTH = 128
SLOT = 32
LANES = 128

epsilon = 1e-06
masked_score = -1e30
MESH = pl.DeviceIdType.MESH
NN = ((1,), (0,))
NT = ((1,), (1,))
TN = ((0,), (0,))


def dot(a, b, contract):
    return lax.dot_general(a, b, (contract, ((), ())), preferred_element_type=jnp.float32)


RS_QKV0, RS_QKV1, RS_HEAD1, RS_HEAD0, AG_HEAD0, AG_GRAD1, AG_HEAD1, AG_GRAD0, AG_FAR0 = range(9)
AG_STREAM0, AG_TOP, RS_OUT0, AG_STREAM1, RS_IN1, AG_OUT0 = range(6)
HALVES = (0, 1)
PEERS = (2, 1, 3)
SIDE = 4
SUB = 16


def split_tile(first, second):
    lane = lax.broadcasted_iota(jnp.int32, first.shape[:-1] + (LANES,), first.ndim - 1)
    tile = jnp.zeros(lane.shape, jnp.float32)
    for i, column in enumerate((first, second)):
        high = column.astype(jnp.bfloat16).astype(jnp.float32)
        tile = jnp.where(lane == 2 * i, high, jnp.where(lane == 2 * i + 1, column - high, tile))
    return tile.astype(jnp.bfloat16)


def join_tile(tile):
    tile = tile.astype(jnp.float32)
    return tile[..., 0:1] + tile[..., 1:2], tile[..., 2:3] + tile[..., 3:4]


def token_weights(lengths, rewards, groups, noise, core, t):
    square = (LANES, LANES)
    micros, packed, slots = lengths.shape
    lane = lax.broadcasted_iota(jnp.int32, (1, LANES), 1)

    def row(ref):
        value = jnp.full((1, LANES), -1, jnp.int32)
        for m in range(micros):
            for s in range(slots):
                for c in range(packed):
                    value = jnp.where(lane == (m * slots + s) * packed + c, ref[m, c, s], value)
        return jnp.broadcast_to(value.astype(jnp.float32), square)

    group_row, reward_row, length_row = row(groups), row(rewards), row(lengths)
    member = (group_row == group_row.T).astype(jnp.float32)
    reward_column = reward_row.T
    count = jnp.sum(member, 0, keepdims=True)
    mean = jnp.sum(member * reward_column, 0, keepdims=True) / count
    centered = reward_column - mean
    variance = jnp.sum(member * centered * centered, 0, keepdims=True) / count
    advantage = (reward_row - mean) / jnp.maximum(jnp.sqrt(variance), 1.0)
    token = lax.broadcasted_iota(jnp.int32, square, 0)
    lanes = lax.broadcasted_iota(jnp.int32, square, 1)
    first = core * slots * packed + (t * (LANES // SLOT) + (token >> 5)) * packed
    length = jnp.sum(jnp.where(lanes == first, length_row, 0.0), -1, keepdims=True)
    position = (token & (SLOT - 1)).astype(jnp.float32)
    chosen = lanes == first + (position >= length).astype(jnp.int32)
    advantage = jnp.sum(jnp.where(chosen, advantage, 0.0), -1, keepdims=True)
    length = jnp.sum(jnp.where(chosen, length_row, 0.0), -1, keepdims=True)
    noise = jnp.broadcast_to(noise[pl.ds(core, 1), :].astype(jnp.float32), square).T
    return advantage * SLOT / length * noise[:, :1]


def kernel(
    x_in, g_in, noise, lengths, rewards, groups, wq, wk, wv, wo,
    dq_out, dk_out, dv_out, do_out,
    X, H, G, Q0, Q1, FX, FH, FG, FQ, W, WO, D, E, DH, EH, ROWS, INV, PROBS, HG, GIN, *rest,
):
    scatter_bufs, (fs, fr, zs, zr, ss, sr, ls) = rest[:28], rest[28:]
    rs_bufs = {
        phase: scatter_bufs[7 * i : 7 * i + 7]
        for i, phase in enumerate((RS_QKV0, RS_QKV1, RS_HEAD1, RS_HEAD0))
    }
    core, f, t = lax.axis_index("pp"), lax.axis_index("fsdp"), lax.axis_index("tp")
    far = 1 - core
    y, x = f >> 2, f & 3
    j, g = x >> 1, x & 1
    q_wide = wq.shape[2] // 2
    k_wide = wk.shape[2] // 2
    cols = q_wide + 2 * k_wide
    wide = cols + LANES
    group = q_wide // HEAD_WIDTH
    scale = HEAD_WIDTH**-0.5

    def span(which, stride, width, at=0):
        return pl.ds(pl.multiple_of(which * stride + at, LANES), width)

    def other(mine, k):
        return (mine + k) & (SIDE - 1)

    def remote(src, dst, send, recv, **at):
        return pltpu.make_async_remote_copy(
            src_ref=src, dst_ref=dst, send_sem=send, recv_sem=recv,
            device_id=at, device_id_type=MESH,
        )

    cuts = [
        (w, gg * width, gg, at, width)
        for gg in (0, 1)
        for w, at, width in ((wq, 0, q_wide), (wk, q_wide, k_wide), (wv, q_wide + k_wide, k_wide))
    ]
    loads = [pltpu.make_async_copy(x_in.at[core], X.at[0, :, t], ls.at[0])] + [
        pltpu.make_async_copy(
            w.at[0, :, pl.ds(at, width)], W.at[core, gg, :, pl.ds(to, width)], ls.at[1 + i]
        )
        for i, (w, at, gg, to, width) in enumerate(cuts)
    ]
    loads += [
        pltpu.make_async_copy(wo.at[0], WO.at[core], ls.at[7]),
        pltpu.make_async_copy(g_in.at[core], GIN, ls.at[8]),
    ]
    for c in loads:
        c.start()

    barrier = pltpu.get_barrier_semaphore()
    for k in (1, 2, 3):
        for at in (
            {"fsdp": y * SIDE + other(x, k)},
            {"fsdp": other(y, k) * SIDE + x},
            {"pp": far, "fsdp": y * SIDE + other(x, k)},
            {"pp": far, "fsdp": other(y, k) * SIDE + x},
            {"tp": other(t, k)},
        ):
            pl.semaphore_signal(barrier, inc=1, device_id=at, device_id_type=MESH)
    pl.semaphore_signal(barrier, inc=1, device_id={"pp": far}, device_id_type=MESH)
    pl.semaphore_wait(barrier, 16)

    def z_gather(phase, buf, h, i):
        ref = buf.at[h, t, i]
        for k in ((2, 1, 3), (2, 3, 1))[h]:
            remote(ref, ref, zs.at[phase, h, i], zr.at[phase, h, i], tp=other(t, k)).start()

    def z_scatter(phase, send, recv, h, i):
        for k in ((2, 1, 3), (2, 3, 1))[h]:
            b = other(t, k)
            remote(
                send.at[h, b, i], recv.at[h, t, i], zs.at[phase, h, i], zr.at[phase, h, i], tp=b
            ).start()

    def z_all(phase, buf, h, i):
        three = buf.at[h, pl.ds(0, SIDE - 1), i]
        return remote(three, three, zs.at[phase, h, i], zr.at[phase, h, i], tp=t)

    def z_wait(phase, buf, h):
        for i in (0, 1):
            z_all(phase, buf, h, i).wait_recv()

    def z_sum(phase, send, recv, h, i, total):
        z_all(phase, recv, h, i).wait_recv()
        total = total + send[h, t, i].astype(jnp.float32)
        for k in ((2, 1, 3), (2, 3, 1))[h]:
            total = total + recv[h, other(t, k), i].astype(jnp.float32)
        return total.astype(jnp.bfloat16)

    def push(phase, h, kind, src, dst, **at):
        remote(src, dst, fs.at[phase, h, kind], fr.at[phase, h, kind], **at).start()

    def f_all(phase, h, kind):
        S, RA, RB, UA, UB, VA, VB = rs_bufs[
            {AG_HEAD0: RS_HEAD0, AG_HEAD1: RS_HEAD0, AG_GRAD0: RS_QKV0, AG_GRAD1: RS_QKV0}.get(phase, phase)
        ]
        order = (RA, RB, VA, VB) if phase < AG_HEAD0 else (VA, VB, RA, RB)
        if phase == AG_GRAD0:
            order = (VB, VB, RB, RB)
        three = order[kind].at[h, pl.ds(0, SIDE - 1)]
        return remote(three, three, fs.at[phase, h, kind], fr.at[phase, h, kind], fsdp=f)

    def widths(buf_cols):
        return (wide, cols) if buf_cols == 2 * wide else (buf_cols // 2, buf_cols // 2)

    def rs_start(phase, h):
        S, RA, RB, UA, UB, VA, VB = rs_bufs[phase]
        ca, cb = widths(S.shape[-1])
        for k in ((2, 1, 3), (2, 3, 1))[h]:
            y2, x2 = other(y, k), other(x, k)
            push(phase, h, 0, S.at[h, y2, :, 0], RA.at[h, y], fsdp=y2 * SIDE + x)
            push(
                phase, h, 1, S.at[h, :, x2 >> 1, 1, :, span(x2 & 1, ca, cb)], RB.at[h, x], fsdp=y * SIDE + x2
            )

    def rs_mid(phase, h):
        S, RA, RB, UA, UB, VA, VB = rs_bufs[phase]
        ca, cb = widths(S.shape[-1])
        f_all(phase, h, 0).wait_recv()
        total = S[h, y, :, 0].astype(jnp.float32)
        for k in ((2, 1, 3), (2, 3, 1))[h]:
            total = total + RA[h, other(y, k)].astype(jnp.float32)
        UA[h] = total.astype(jnp.bfloat16)
        for k in ((2, 1, 3), (2, 3, 1))[h]:
            x2 = other(x, k)
            push(
                phase, h, 2, UA.at[h, x2 >> 1, :, span(x2 & 1, ca, ca)], VA.at[h, x], fsdp=y * SIDE + x2
            )
        f_all(phase, h, 1).wait_recv()
        total = S[h, :, j, 1, :, span(g, ca, cb)].astype(jnp.float32)
        for k in ((2, 1, 3), (2, 3, 1))[h]:
            total = total + RB[h, other(x, k)].astype(jnp.float32)
        UB[h] = total.astype(jnp.bfloat16)
        for k in ((2, 1, 3), (2, 3, 1))[h]:
            y2 = other(y, k)
            push(phase, h, 3, UB.at[h, y2], VB.at[h, y], fsdp=y2 * SIDE + x)

    def rs_end(phase, h):
        S, RA, RB, UA, UB, VA, VB = rs_bufs[phase]
        ca, cb = widths(S.shape[-1])
        f_all(phase, h, 2).wait_recv()
        first = UA[h, j, :, span(g, ca, ca)].astype(jnp.float32)
        for k in ((2, 1, 3), (2, 3, 1))[h]:
            first = first + VA[h, other(x, k)].astype(jnp.float32)
        f_all(phase, h, 3).wait_recv()
        second = UB[h, y].astype(jnp.float32)
        for k in ((2, 1, 3), (2, 3, 1))[h]:
            second = second + VB[h, other(y, k)].astype(jnp.float32)
        return first, second

    def ag_start(phase, buf, h):
        ca, cb = widths(buf.shape[-1])
        first = buf.at[h, y, j, 0, :, span(g, ca, ca)]
        second = buf.at[h, y, j, 1, :, span(g, ca, cb)]
        for k in ((2, 1, 3), (2, 3, 1))[h]:
            push(phase, h, 0, first, first, fsdp=y * SIDE + other(x, k))
            push(phase, h, 1, second, second, fsdp=other(y, k) * SIDE + x)

    def ag_mid(phase, buf, h):
        ca, cb = widths(buf.shape[-1])
        first = buf.at[h, y, :, 0]
        f_all(phase, h, 0).wait_recv()
        for k in ((2, 1, 3), (2, 3, 1))[h]:
            push(phase, h, 2, first, first, fsdp=other(y, k) * SIDE + x)
        second = buf.at[h, :, j, 1, :, span(g, ca, cb)]
        f_all(phase, h, 1).wait_recv()
        for k in ((2, 1, 3), (2, 3, 1))[h]:
            push(phase, h, 3, second, second, fsdp=y * SIDE + other(x, k))

    def last_mid(h):
        first, second = Q0.at[h, y, :, 0], Q0.at[h, :, j, 1, :, span(g, cols, cols)]
        first_far, second_far = FQ.at[h, y, :, 0], FQ.at[h, :, j, 1, :, span(g, cols, cols)]
        f_all(AG_GRAD0, h, 0).wait_recv()

        @pl.when(core == 0)
        def _():
            for k in ((2, 1, 3), (2, 3, 1))[h]:
                push(AG_GRAD0, h, 2, first, first, fsdp=other(y, k) * SIDE + x)

        @pl.when(core == 1)
        def _():
            for k in PEERS + (0,):
                push(AG_FAR0, h, 2, first, first_far, pp=far, fsdp=other(y, k) * SIDE + x)

        f_all(AG_GRAD0, h, 1).wait_recv()

        @pl.when(core == 0)
        def _():
            for k in ((2, 1, 3), (2, 3, 1))[h]:
                push(AG_GRAD0, h, 3, second, second, fsdp=y * SIDE + other(x, k))

        @pl.when(core == 1)
        def _():
            for k in PEERS + (0,):
                push(AG_FAR0, h, 3, second, second_far, pp=far, fsdp=y * SIDE + other(x, k))

    def far_all(h, kind):
        four = rs_bufs[RS_QKV0][2].at[h]
        return remote(four, four, fs.at[AG_FAR0, h, kind], fr.at[AG_FAR0, h, kind], fsdp=f)

    def ag_end(phase, h):
        f_all(phase, h, 2).wait_recv()
        f_all(phase, h, 3).wait_recv()

    def flat(value):
        return value.reshape(-1, value.shape[-1])

    def project(layer, gathered, phase, h):
        S = rs_bufs[phase][0]
        z_wait(gathered, X.at[layer], h)
        rows = flat(X[layer, h])
        for gg in (0, 1):
            S[h, :, :, :, :, pl.ds(gg * wide, cols)] = (
                dot(rows, W[layer, gg], NN).astype(jnp.bfloat16).reshape(SIDE, 2, 2, SUB, cols)
            )
        squares = []
        for a in (0, 1):
            part = X[layer, h, :, :, a].astype(jnp.float32)
            squares.append(jnp.sum(part * part, -1, keepdims=True))
        tile = split_tile(*squares)
        for gg in (0, 1):
            S[h, :, :, 0, :, pl.ds(gg * wide + cols, LANES)] = tile
        rs_start(phase, h)

    def attend(layer, phase, h):
        first, second = rs_end(phase, h)
        squares = jnp.concatenate(join_tile(first[:, cols:]), 0)
        inv_rms = lax.rsqrt(squares / MODEL_WIDTH + epsilon)
        rows = (jnp.concatenate([first[:, :cols], second], 0) * inv_rms).astype(jnp.bfloat16)
        ROWS[layer, h] = rows
        INV[layer, h] = jnp.broadcast_to(inv_rms, (SLOT, LANES))
        queries = jnp.concatenate([rows[:, i * HEAD_WIDTH : (i + 1) * HEAD_WIDTH] for i in range(group)], 0)
        keys, values = rows[:, q_wide : q_wide + k_wide], rows[:, q_wide + k_wide :]
        scores = dot(queries, keys, NT) * scale
        cut = lengths[core, 0, y * SIDE + 2 * h + j]
        later = [
            ((lax.broadcasted_iota(jnp.int32, scores.shape, d) & (SLOT - 1)) >= cut).astype(jnp.int32)
            for d in (0, 1)
        ]
        scores = jnp.where(later[0] == later[1], scores, masked_score)
        raised = jnp.exp(scores - jnp.max(scores, -1, keepdims=True))
        probs = raised / jnp.sum(raised, -1, keepdims=True)
        PROBS[layer, h] = probs
        mixed = dot(probs.astype(jnp.bfloat16), values, NN).astype(jnp.bfloat16)
        for i in range(group):
            H[layer, h, y, j, :, :, span(g, q_wide, HEAD_WIDTH, i * HEAD_WIDTH)] = mixed[
                i * SLOT : (i + 1) * SLOT
            ].reshape(2, SUB, HEAD_WIDTH)

    def head_end(phase, h):
        first, second = rs_end(phase, h)
        HG[h] = jnp.concatenate([first, second], 0).astype(jnp.bfloat16)

    def attend_back(layer, h):
        Q, stride = ((Q0, cols), (Q1, wide))[layer]
        rows, head_grad, inv_rms, probs = ROWS[layer, h], HG[h], INV[layer, h], PROBS[layer, h]

        def stacked(value):
            return jnp.concatenate(
                [value[:, i * HEAD_WIDTH : (i + 1) * HEAD_WIDTH] for i in range(group)], 0
            )

        queries, grads = stacked(rows), stacked(head_grad)
        keys, values = rows[:, q_wide : q_wide + k_wide], rows[:, q_wide + k_wide :]
        prob_grad = dot(grads, values, NT)
        value_grad = dot(probs.astype(jnp.bfloat16), grads, TN)
        score_grad = probs * (prob_grad - jnp.sum(prob_grad * probs, -1, keepdims=True))
        score_grad = score_grad.astype(jnp.bfloat16)
        query_grad = dot(score_grad, keys, NN) * scale
        key_grad = dot(score_grad, queries, TN) * scale
        total = jnp.zeros((SLOT, LANES), jnp.float32)
        parts = [query_grad[i * SLOT : (i + 1) * SLOT] for i in range(group)] + [key_grad, value_grad]
        for i, part in enumerate(parts):
            part = part.astype(jnp.bfloat16).astype(jnp.float32)
            total = total + part * rows[:, i * HEAD_WIDTH : (i + 1) * HEAD_WIDTH].astype(jnp.float32)
            Q[h, y, j, :, :, span(g, stride, HEAD_WIDTH, i * HEAD_WIDTH)] = (
                (part * inv_rms).astype(jnp.bfloat16).reshape(2, SUB, HEAD_WIDTH)
            )
        if layer > 0:
            share = inv_rms[:, :1] * inv_rms[:, :1] * jnp.sum(total, -1, keepdims=True) / MODEL_WIDTH
            Q[h, y, j, 0, :, span(g, wide, LANES, cols)] = split_tile(share[:SUB], share[SUB:])

    def head_grads(layer, gathered, phase, h):
        S = rs_bufs[phase][0]
        z_wait(gathered, G.at[layer], h)
        S[h] = dot(flat(G[layer, h]), WO[layer], NT).astype(jnp.bfloat16).reshape(S.shape[1:])
        rs_start(phase, h)

    def project_out(h):
        ag_end(AG_HEAD0, h)
        D[h] = dot(flat(H[0, h]), WO[0], NN).astype(jnp.bfloat16).reshape(D.shape[1:])
        for i in (0, 1):
            z_scatter(RS_OUT0, D, E, h, i)

    def project_back(h):
        ag_end(AG_GRAD1, h)
        back = sum(
            dot(flat(Q1[h, :, :, :, :, pl.ds(gg * wide, cols)]), W[1, gg], NT) for gg in (0, 1)
        ).reshape(DH.shape[1:])
        tiles = [
            Q1[h, :, :, 0, :, pl.ds(gg * wide + cols, LANES)].astype(jnp.float32) for gg in (0, 1)
        ]
        shares = join_tile(tiles[0] + tiles[1])
        for a in (0, 1):
            term = back[:, :, a] - X[1, h, :, :, a].astype(jnp.float32) * shares[a]
            DH[h, :, :, a] = term.astype(jnp.bfloat16)
        for i in (0, 1):
            z_scatter(RS_IN1, DH, EH, h, i)

    def hand_over(i, src, dst):
        return remote(src, dst, ss.at[i], sr.at[i], pp=far)

    x_far, h_far, g_far = hand_over(7, X.at[far], FX), hand_over(8, H.at[far], FH), hand_over(9, G.at[far], FG)
    q_far = [
        hand_over(
            10 + gg, Q1.at[:, :, :, :, :, pl.ds(gg * wide, cols)], FQ.at[:, :, :, :, :, pl.ds(gg * cols, cols)]
        )
        for gg in (0, 1)
    ]
    def weight_grads(layer, h):
        Q, stride = ((Q0, cols), (Q1, wide))[layer]
        rows, far_rows = flat(X[layer, h]), flat(FX[h])
        for gg in (0, 1):
            term = dot(rows, flat(Q[h, :, :, :, :, pl.ds(gg * stride, cols)]), TN) + dot(
                far_rows, flat(FQ[h, :, :, :, :, pl.ds(gg * cols, cols)]), TN
            )
            for to, width, out in (
                (0, q_wide, dq_out), (q_wide, k_wide, dk_out), (q_wide + k_wide, k_wide, dv_out)
            ):
                to_at = pl.ds(gg * width, width)
                part = term[:, to : to + width]
                out[0, :, to_at] = part if h == 0 else out[0, :, to_at] + part

    loads[0].wait()
    for h in HALVES:
        for i in (0, 1):
            z_gather(AG_STREAM0, X.at[0], h, i)
    swaps = [
        remote(
            w.at[0, :, pl.ds(at, width)], W.at[core, gg, :, pl.ds(to, width)], ss.at[i], sr.at[i], pp=far
        )
        for i, (w, at, gg, to, width) in enumerate(cuts)
    ] + [remote(wo.at[0], WO.at[core], ss.at[6], sr.at[6], pp=far)]
    for c in swaps[:6]:
        c.start()
    for c in loads[1:8]:
        c.wait()

    @pl.when(core == 1)
    def _():
        for c in swaps[:6]:
            c.wait_recv()

    for h in HALVES:
        project(0, AG_STREAM0, RS_QKV0, h)
    swaps[6].start()
    loads[8].wait()
    top = token_weights(lengths, rewards, groups, noise, core, t)
    top = (-top * flat(GIN[...]).astype(jnp.float32)).astype(jnp.bfloat16)
    G[1, :, t] = top.reshape(GIN.shape)
    for h in HALVES:
        for i in (0, 1):
            z_gather(AG_TOP, G.at[1], h, i)
    for h in HALVES:
        rs_mid(RS_QKV0, h)
    for h in HALVES:
        attend(0, RS_QKV0, h)
        ag_start(AG_HEAD0, H.at[0], h)
    for h in HALVES:
        ag_mid(AG_HEAD0, H.at[0], h)
    swaps[6].wait_recv()
    for h in HALVES:
        head_grads(1, AG_TOP, RS_HEAD1, h)
    for h in HALVES:
        project_out(h)
    for h in HALVES:
        for i in (0, 1):
            X[1, h, t, i] = z_sum(RS_OUT0, D, E, h, i, X[0, h, t, i].astype(jnp.float32))
            z_gather(AG_STREAM1, X.at[1], h, i)
    for h in HALVES:
        rs_mid(RS_HEAD1, h)
    @pl.when(core == 0)
    def _():
        for c in swaps[:6]:
            c.wait_recv()

    for h in HALVES:
        project(1, AG_STREAM1, RS_QKV1, h)
    x_far.start()
    for h in HALVES:
        head_end(RS_HEAD1, h)
    for h in HALVES:
        rs_mid(RS_QKV1, h)
    for h in HALVES:
        attend(1, RS_QKV1, h)
        attend_back(1, h)
        ag_start(AG_GRAD1, Q1, h)
    for h in HALVES:
        ag_mid(AG_GRAD1, Q1, h)
    for h in HALVES:
        project_back(h)

    @pl.when(core == 0)
    def _():
        for c in q_far:
            c.start()

    for h in HALVES:
        ag_start(AG_HEAD1, H.at[1], h)
    for h in HALVES:
        for i in (0, 1):
            G[0, h, t, i] = z_sum(RS_IN1, DH, EH, h, i, G[1, h, t, i].astype(jnp.float32))
            z_gather(AG_OUT0, G.at[0], h, i)
    for h in HALVES:
        ag_mid(AG_HEAD1, H.at[1], h)
    for h in HALVES:
        head_grads(0, AG_OUT0, RS_HEAD0, h)
    g_far.start()
    for h in HALVES:
        ag_end(AG_HEAD1, h)
    h_far.start()
    do_out[0] = dot(flat(H[core]), flat(G[core]), TN)
    for h in HALVES:
        rs_mid(RS_HEAD0, h)
    for h in HALVES:
        head_end(RS_HEAD0, h)
        attend_back(0, h)
        ag_start(AG_GRAD0, Q0, h)
    for h in HALVES:
        last_mid(h)
    for c in (x_far, h_far, g_far):
        c.wait_recv()
    do_out[0] += dot(flat(FH[...]), flat(FG[...]), TN)
    @pl.when(core == 0)
    def _():
        for h in HALVES:
            ag_end(AG_GRAD0, h)
            far_all(h, 2).wait_recv()
            far_all(h, 3).wait_recv()
            weight_grads(0, h)

    @pl.when(core == 1)
    def _():
        for c in q_far:
            c.wait_recv()
        for h in HALVES:
            weight_grads(1, h)

    for phase in range(AG_GRAD0):
        for h in HALVES:
            for kind in range(4):
                f_all(phase, h, kind).wait_send()
    for h in HALVES:
        for kind in (0, 1):
            f_all(AG_GRAD0, h, kind).wait_send()

        @pl.when(core == 0)
        def _():
            for kind in (2, 3):
                f_all(AG_GRAD0, h, kind).wait_send()

        @pl.when(core == 1)
        def _():
            for kind in (2, 3):
                far_all(h, kind).wait_send()

    for phase, buf in (
        (AG_STREAM0, X.at[0]), (AG_TOP, G.at[1]), (RS_OUT0, E),
        (AG_STREAM1, X.at[1]), (RS_IN1, EH), (AG_OUT0, G.at[0]),
    ):
        for h in HALVES:
            for i in (0, 1):
                z_all(phase, buf, h, i).wait_send()
    for c in swaps + [x_far, h_far, g_far]:
        c.wait_send()

    @pl.when(core == 0)
    def _():
        for c in q_far:
            c.wait_send()


def write_out(*refs):
    *pairs, sems = refs
    count = len(pairs) // 2
    copies = [
        pltpu.make_async_copy(src, dst, sems.at[i])
        for i, (src, dst) in enumerate(zip(pairs[:count], pairs[count:]))
    ]
    for c in copies:
        c.start()
    for c in copies:
        c.wait()


def local(
    inputs,
    head_grad,
    noise_mask,
    lengths,
    rewards,
    groups,
    query_weight,
    key_weight,
    value_weight,
    out_weight,
):
    row_count, width = inputs.shape[1:]
    q_wide, k_wide = query_weight.shape[2] // 2, key_weight.shape[2] // 2
    cols = q_wide + 2 * k_wide
    wide = cols + LANES
    group = q_wide // k_wide

    bf16, f32 = jnp.bfloat16, jnp.float32
    any_space = pl.BlockSpec(memory_space=pl.ANY)
    rows = (2, SIDE, 2, 2, SUB)

    def scatter_bufs(ca, cb):
        return [
            pltpu.VMEM(shape, bf16)
            for shape in (
                rows + (2 * ca,),
                (2, SIDE, 2, SUB, 2 * ca),
                (2, SIDE, SIDE, SUB, cb),
                (2, 2, SUB, 2 * ca),
                (2, SIDE, SUB, cb),
                (2, SIDE, SUB, ca),
                (2, SIDE, SUB, cb),
            )
        ]

    results = pl.pallas_call(
        kernel,
        out_shape=[
            pltpu.VMEM(w.shape, f32)
            for w in (query_weight, key_weight, value_weight, out_weight)
        ],
        in_specs=[any_space, any_space, pl.BlockSpec(memory_space=pltpu.VMEM)]
        + [pl.BlockSpec(memory_space=pltpu.SMEM)] * 3
        + [any_space] * 4,
        out_specs=[pl.BlockSpec(memory_space=pltpu.VMEM)] * 4,
        scratch_shapes=[
            pltpu.VMEM((2,) + rows + (width,), bf16),
            pltpu.VMEM((2,) + rows + (2 * q_wide,), bf16),
            pltpu.VMEM((2,) + rows + (width,), bf16),
            pltpu.VMEM(rows + (2 * cols,), bf16),
            pltpu.VMEM(rows + (2 * wide,), bf16),
            pltpu.VMEM(rows + (width,), bf16),
            pltpu.VMEM(rows + (2 * q_wide,), bf16),
            pltpu.VMEM(rows + (width,), bf16),
            pltpu.VMEM(rows + (2 * cols,), bf16),
            pltpu.VMEM((2, 2, width, cols), bf16),
            pltpu.VMEM((2, 2 * q_wide, width), bf16),
            pltpu.VMEM(rows + (width,), bf16),
            pltpu.VMEM(rows + (width,), bf16),
            pltpu.VMEM(rows + (width,), bf16),
            pltpu.VMEM(rows + (width,), bf16),
            pltpu.VMEM((2, 2, SLOT, cols), bf16),
            pltpu.VMEM((2, 2, SLOT, LANES), f32),
            pltpu.VMEM((2, 2, group * SLOT, SLOT), f32),
            pltpu.VMEM((2, SLOT, q_wide), bf16),
            pltpu.VMEM((2, 2, 2, SUB, width), bf16),
        ]
        + scatter_bufs(wide, cols) * 2
        + scatter_bufs(q_wide, q_wide) * 2
        + [
            pltpu.SemaphoreType.DMA((9, 2, 4)),
            pltpu.SemaphoreType.DMA((9, 2, 4)),
            pltpu.SemaphoreType.DMA((6, 2, 2)),
            pltpu.SemaphoreType.DMA((6, 2, 2)),
            pltpu.SemaphoreType.DMA((12,)),
            pltpu.SemaphoreType.DMA((12,)),
            pltpu.SemaphoreType.DMA((9,)),
        ],
        compiler_params=pltpu.CompilerParams(
            collective_id=0, has_side_effects=True, vmem_limit_bytes=56 * 1024 * 1024
        ),
    )(
        inputs.reshape(2, 2, 2, 2, SUB, width),
        head_grad.reshape(2, 2, 2, 2, SUB, width),
        noise_mask,
        *(jnp.swapaxes(v, 1, 2) for v in (lengths, rewards, groups)),
        query_weight,
        key_weight,
        value_weight,
        out_weight,
    )
    return pl.pallas_call(
        write_out,
        out_shape=[jax.ShapeDtypeStruct(r.shape, r.dtype) for r in results],
        in_specs=[any_space] * 4,
        out_specs=[any_space] * 4,
        scratch_shapes=[pltpu.SemaphoreType.DMA((4,))],
        compiler_params=pltpu.CompilerParams(vmem_limit_bytes=1024 * 1024),
    )(*results)


def solution(mesh):
    return jax.shard_map(
        local,
        mesh=mesh,
        in_specs=(
            P(None, "tp", "fsdp"),
            P(None, "tp", "fsdp"),
            P(None, "tp"),
            P(),
            P(),
            P(),
            P("pp", "fsdp", "tp"),
            P("pp", "fsdp", "tp"),
            P("pp", "fsdp", "tp"),
            P("pp", "tp", "fsdp"),
        ),
        out_specs=(
            P("pp", "fsdp", "tp"),
            P("pp", "fsdp", "tp"),
            P("pp", "fsdp", "tp"),
            P("pp", "tp", "fsdp"),
        ),
        check_vma=False,
    )
```
